32 devices in a mesh: rows: 8 (over z, x), heads: 4 (over y, core).
Axes of the slice: x: 2, y: 2, z: 4, core: 2. Of those that a mesh axis runs over, the one named last changes fastest.
Arguments:
- tokens: bfloat16 [32768, 512], P('rows', 'heads'), may hold values from -12 to 12
- ln1_gain: float32 [512], P('heads'), may hold values from 0.25 to 1.75
- ln1_bias: float32 [512], P('heads'), may hold values from -1.75 to 1.75
- qkv_weight: bfloat16 [3, 512, 512], P(None, 'heads', 'rows'), may hold values from -0.25 to 0.25
- out_weight: bfloat16 [512, 512], P('heads', 'rows'), may hold values from -0.375 to 0.375
- ln2_gain: float32 [512], P('heads'), may hold values from 0.25 to 1.75
- ln2_bias: float32 [512], P('heads'), may hold values from -1.75 to 1.75
- ffn_in: bfloat16 [2048, 512], P('heads', 'rows'), may hold values from -0.25 to 0.25
- ffn_out: bfloat16 [2048, 512], P('heads', 'rows'), may hold values from -0.125 to 0.125
- feature_proj: bfloat16 [64, 256], replicated, may hold values from -4 to 4
- masked_pos: int32 [4, 2048], replicated, may hold values from 0 to 8191, as said below
- masked_count: int32 [4], replicated, may hold values from 409 to 2048
- out_grad: bfloat16 [32768, 512], P('rows', 'heads'), may hold values from -12 to 12
Outputs:
- mixed: bfloat16 [32768, 512], P('rows', 'heads')
- input_grad: float32 [32768, 512], P('rows', 'heads')
- qkv_weight_grad: float32 [3, 512, 512], P(None, 'heads', 'rows')
- out_weight_grad: float32 [512, 512], P('heads', 'rows')
- ffn_in_grad: float32 [2048, 512], P('heads', 'rows')
- ffn_out_grad: float32 [2048, 512], P('heads', 'rows')
- ln1_gain_grad: float32 [512], P('heads')
- ln1_bias_grad: float32 [512], P('heads')
- ln2_gain_grad: float32 [512], P('heads')
- ln2_bias_grad: float32 [512], P('heads')
The draws below stay inside these ranges and needn't reach their ends.
Inputs may be any that keep to these rules, and one draw needn't show every extreme that they name: `masked_pos`: row s lists 2048 distinct positions of sequence s; its first masked_count[s] entries are the masked ones.
All inputs are finite; a program needn't handle non-finite values.
Results may differ from the reference program's by a relative error of at most 0.022.
Values may be sent and summed in bfloat16 or wider, within the bound.
No kernel may reach another device: no remote copies, remote signals or barrier semaphores. Data moves between devices by JAX's collectives and lax.ppermute only.
A program may use at most 192 MiB of HBM per device.

```python
import math
from functools import partial
import jax
import jax.numpy as jnp
from jax import lax

D = 512
HEADS = 8
HEAD_DIM = 64
FEATS = 256
FF = 2048
LENGTH = 8192
SEQS = 4
TOKENS = 32768
MASK_MAX = 2048


def one_order(sub_key):
    return jax.random.permutation(sub_key, LENGTH)


def draw_masked_pos(key, part):
    key = jax.random.fold_in(key, 11)
    split_keys = jax.random.split(key, SEQS + 2)
    orders = jax.vmap(one_order)(split_keys[:SEQS])[:, :MASK_MAX].astype(jnp.int32)
    high_seq = jax.random.randint(split_keys[SEQS], (), 0, SEQS)
    low_seq = (high_seq + 1 + jax.random.randint(split_keys[SEQS + 1], (), 0, SEQS - 1)) % SEQS
    seq_ids = jnp.arange(SEQS, dtype=jnp.int32)
    shifts = jnp.where(seq_ids == high_seq, LENGTH - 1 - orders[:, 0], jnp.where(seq_ids == low_seq, LENGTH - orders[:, 0], 0))
    return ((orders + shifts[:, None]) % LENGTH).astype(jnp.int32)


def draw_masked_count(key, part):
    key = jax.random.fold_in(key, 12)
    first_key, second_key, third_key = jax.random.split(key, 3)
    least = max(1, LENGTH // 20)
    counts = jax.random.randint(first_key, (SEQS,), least, MASK_MAX + 1)
    top_seq = jax.random.randint(second_key, (), 0, SEQS)
    bottom_seq = (top_seq + 1 + jax.random.randint(third_key, (), 0, SEQS - 1)) % SEQS
    seq_ids = jnp.arange(SEQS, dtype=jnp.int32)
    counts = jnp.where(seq_ids == top_seq, MASK_MAX, jnp.where(seq_ids == bottom_seq, least, counts))
    return counts.astype(jnp.int32)


def draw_tokens(key, part):
    key = jax.random.fold_in(key, 5)
    first_key, second_key = jax.random.split(key, 2)
    columns = 0.5 + jnp.arange(D, dtype=jnp.float32) / (D - 1)
    base = jnp.clip(jax.random.normal(first_key, (TOKENS, D), jnp.float32), -5.0, 5.0)
    scales = jnp.exp(jax.random.uniform(second_key, (TOKENS, 1), jnp.float32, -0.5, 0.47))
    return (base * scales * columns[None, :]).astype(jnp.bfloat16)


def draw_out_grad(key, part):
    key = jax.random.fold_in(key, 7)
    first_key = jax.random.fold_in(key, 0)
    rising = 1.0 + 2.0 * jnp.arange(TOKENS, dtype=jnp.float32) / (TOKENS - 1)
    base = jnp.clip(jax.random.normal(first_key, (TOKENS, D), jnp.float32), -4.0, 4.0)
    return (base * rising[:, None]).astype(jnp.bfloat16)


def shard_levels(stream_key, extent, cuts, smallest, largest):
    gain = 1.0
    for position, blocks in cuts:
        heights = jax.random.uniform(jax.random.fold_in(jax.random.fold_in(stream_key, 6), position), (blocks,), jnp.float32, smallest / len(cuts), largest / len(cuts))
        gain = gain * jnp.repeat(jnp.exp(heights), extent[position] // blocks).reshape((-1,) + (1,) * (len(extent) - 1 - position))
    return gain


def noise(key, shape, deviation, bound, pieces=(), kind=jnp.bfloat16):
    entries = deviation * jax.random.normal(key, shape, jnp.float32)
    if pieces:
        entries = entries * shard_levels(key, shape, pieces, -0.22, 0.18)
    return jnp.clip(entries, -bound, bound).astype(kind)


def setup_inputs(seed: int = 0) -> dict:
    splits = jax.random.split(jax.random.key(seed), 14)
    tokens = draw_tokens(jax.random.fold_in(splits[13], 71), 0)
    ln1_gain = jnp.clip(1.0 + 0.15 * jax.random.normal(splits[1], (D,), jnp.float32), 0.25, 1.75)
    ln1_bias = noise(splits[2], (D,), 0.3, 1.75, ((0, 4),), jnp.float32)
    qkv_weight = noise(splits[3], (3, D, D), D ** -0.5, 0.25, ((1, 4), (2, 8)))
    out_weight = noise(splits[4], (D, D), (1.5 * D ** -0.5), 0.375, ((0, 4), (1, 8)))
    ln2_gain = jnp.clip(1.0 + 0.15 * jax.random.normal(splits[5], (D,), jnp.float32), 0.25, 1.75)
    ln2_bias = noise(splits[6], (D,), 0.3, 1.75, ((0, 4),), jnp.float32)
    ffn_in = noise(splits[7], (FF, D), D ** -0.5, 0.25, ((0, 4), (1, 8)))
    ffn_out = noise(splits[8], (FF, D), FF ** -0.5, 0.125, ((0, 4), (1, 8)))
    feature_proj = noise(splits[9], (HEAD_DIM, FEATS), 1.0, 4.0)
    masked_pos = draw_masked_pos(jax.random.fold_in(splits[13], 71), 0)
    masked_count = draw_masked_count(jax.random.fold_in(splits[13], 71), 0)
    out_grad = draw_out_grad(jax.random.fold_in(splits[13], 71), 0)
    return {"tokens": tokens, "ln1_gain": ln1_gain, "ln1_bias": ln1_bias, "qkv_weight": qkv_weight, "out_weight": out_weight, "ln2_gain": ln2_gain, "ln2_bias": ln2_bias, "ffn_in": ffn_in, "ffn_out": ffn_out, "feature_proj": feature_proj, "masked_pos": masked_pos, "masked_count": masked_count, "out_grad": out_grad}


@jax.custom_vjp
def low(v):
    return lax.optimization_barrier(v.astype(jnp.bfloat16)).astype(jnp.float32)

@jax.custom_vjp
def low_back(v):
    return v

def low_keep(v):
    return (low(v), None)

def low_pass(kept, grad):
    return (grad,)

def back_keep(v):
    return (v, None)

def back_low(kept, grad):
    return (low(grad),)
low.defvjp(low_keep, low_pass)
low_back.defvjp(back_keep, back_low)
epsilon = 1e-05
highest = lax.Precision.HIGHEST

def layer_norm(values, norm_gain, norm_bias):
    row_mean = lax.optimization_barrier(jnp.mean(values, axis=-1, keepdims=True))
    spread = lax.optimization_barrier(jnp.mean(jnp.square(values - row_mean), axis=-1, keepdims=True))
    return (values - row_mean) * lax.rsqrt(spread + epsilon) * norm_gain + norm_bias

def feature_map(projection, directions):
    feat_scale = HEAD_DIM ** (-0.25)
    projected = low_back(jnp.einsum('lhe,ef->lhf', projection, directions, precision=highest))
    square = lax.optimization_barrier(jnp.sum(projection * projection, axis=-1, keepdims=True))
    return low(jnp.exp(feat_scale * projected - 0.5 * feat_scale * feat_scale * square) / math.sqrt(FEATS))

def forward(directions, tokens, ln1_gain, ln1_bias, qkv_weight, out_weight, ln2_gain, ln2_bias, ffn_in, ffn_out):

    def one_sequence(seq_rows):
        length = seq_rows.shape[0]
        normed_a = low(layer_norm(seq_rows, ln1_gain, ln1_bias))
        projected = jnp.einsum('li,pji->plj', normed_a, qkv_weight, precision=highest)
        projections = [low(low_back(projected[which_part])).reshape(length, HEADS, HEAD_DIM) for which_part in range(3)]
        phi_q = feature_map(projections[0], directions)
        phi_k = feature_map(projections[1], directions)
        summary = low(low_back(jnp.einsum('lhf,lhe->hfe', phi_k, projections[2], precision=highest)))
        totals = low(low_back(lax.optimization_barrier(jnp.sum(phi_k, axis=0))))
        numerator = low_back(jnp.einsum('lhf,hfe->lhe', phi_q, summary, precision=highest))
        denominator = low_back(jnp.einsum('lhf,hf->lh', phi_q, totals, precision=highest))
        mixed_heads = low(numerator / denominator[:, :, None]).reshape(length, D)
        hidden_one = seq_rows + low_back(jnp.dot(mixed_heads, out_weight, precision=highest))
        normed_c = low(layer_norm(hidden_one, ln2_gain, ln2_bias))
        ffn_upper = low_back(jnp.dot(normed_c, ffn_in.T, precision=highest))
        ffn_activ = low(jax.nn.gelu(ffn_upper, approximate=False))
        return hidden_one + low_back(jnp.dot(ffn_activ, ffn_out, precision=highest))
    stacked = tokens.reshape(SEQS, LENGTH, D)
    return lax.map(jax.checkpoint(one_sequence), stacked).reshape(TOKENS, D)

def sequence_mask(positions, mask_limit):
    slot_ids = jnp.arange(MASK_MAX, dtype=jnp.int32)
    targets = jnp.where(slot_ids < mask_limit, positions, LENGTH)
    return jnp.zeros((LENGTH,), jnp.float32).at[targets].add(1.0, mode='drop')

def reference(tokens, ln1_gain, ln1_bias, qkv_weight, out_weight, ln2_gain, ln2_bias, ffn_in, ffn_out, feature_proj, masked_pos, masked_count, out_grad):
    output, pull = jax.vjp(partial(forward, feature_proj.astype(jnp.float32)), tokens.astype(jnp.float32), ln1_gain, ln1_bias, qkv_weight.astype(jnp.float32), out_weight.astype(jnp.float32), ln2_gain, ln2_bias, ffn_in.astype(jnp.float32), ffn_out.astype(jnp.float32))
    row_mask = jax.vmap(sequence_mask)(masked_pos, masked_count).reshape(TOKENS)
    grads = pull(out_grad.astype(jnp.float32) * row_mask[:, None])
    return (output.astype(jnp.bfloat16), grads[0], grads[3], grads[4], grads[7], grads[8], grads[1], grads[2], grads[5], grads[6])
```

```python
import math

import jax
import jax.numpy as jnp
from jax import lax
from jax.experimental import pallas as pl
from jax.experimental.pallas import tpu as pltpu
from jax.sharding import PartitionSpec as P

D = 512
HEAD_DIM = 64
FEATS = 256
PAIR = 2 * HEAD_DIM
SPAN = 2
PACK = 80
SCALE = HEAD_DIM ** (-0.25)
HALF_SQ = 0.5 * SCALE * SCALE
epsilon = 1e-05
f32 = jnp.float32
b16 = jnp.bfloat16
VMEM_LIMIT = 48 * 1024 * 1024
TILE = 256
MASK_TILE = 320


def mm(left, right):
    return lax.dot_general(left, right, (((1,), (0,)), ((), ())), preferred_element_type=f32)


def mm_nt(left, right):
    return lax.dot_general(left, right, (((1,), (1,)), ((), ())), preferred_element_type=f32)


def mm_tn(left, right):
    return lax.dot_general(left, right, (((0,), (0,)), ((), ())), preferred_element_type=f32)


def layer_stats(values):
    mean = jnp.sum(values, axis=1, keepdims=True) * (1.0 / D)
    centred = values - mean
    var = jnp.sum(centred * centred, axis=1, keepdims=True) * (1.0 / D)
    scale = lax.rsqrt(var + epsilon)
    return centred * scale, scale


def layer_back(grad, normed, scale, gain):
    scaled = grad * gain
    first = jnp.sum(scaled, axis=1, keepdims=True) * (1.0 / D)
    second = jnp.sum(scaled * normed, axis=1, keepdims=True) * (1.0 / D)
    return scale * (scaled - first - normed * second)


def features(rows, directions):
    projected = mm(rows, directions)
    wide = rows.astype(f32)
    square = wide * wide
    first = lax.broadcasted_iota(jnp.int32, square.shape, 1) < HEAD_DIM
    left = jnp.sum(jnp.where(first, square, 0.0), axis=1, keepdims=True)
    right = jnp.sum(jnp.where(first, 0.0, square), axis=1, keepdims=True)
    return jnp.concatenate(
        [
            jnp.exp(SCALE * projected[:, :FEATS] - HALF_SQ * left) * (1.0 / math.sqrt(FEATS)),
            jnp.exp(SCALE * projected[:, FEATS:] - HALF_SQ * right) * (1.0 / math.sqrt(FEATS)),
        ],
        axis=1,
    )


def normal_parts(u):
    bell = jnp.exp(-0.5 * u * u)
    t = 1.0 / (1.0 + (0.3275911 / math.sqrt(2.0)) * jnp.abs(u))
    poly = t * (
        0.5 * 0.254829592
        + t
        * (
            0.5 * -0.284496736
            + t * (0.5 * 1.421413741 + t * (0.5 * -1.453152027 + t * (0.5 * 1.061405429)))
        )
    )
    tail = poly * bell
    return jnp.where(u < 0, tail, 1.0 - tail), bell


def summary_matrix(packed, blk):
    half = packed[blk]
    zero = jnp.zeros((HEAD_DIM, FEATS), b16)
    top = jnp.concatenate([half[:HEAD_DIM, :FEATS], zero], axis=1)
    low = jnp.concatenate([zero, half[:HEAD_DIM, FEATS:]], axis=1)
    sums = half[HEAD_DIM : HEAD_DIM + 1].astype(f32)
    rows = jnp.broadcast_to(sums, (HEAD_DIM, 2 * FEATS))
    left = lax.broadcasted_iota(jnp.int32, rows.shape, 1) < FEATS
    return jnp.concatenate(
        [
            top,
            low,
            jnp.where(left, rows, 0.0).astype(b16),
            jnp.where(left, 0.0, rows).astype(b16),
        ],
        axis=0,
    )


def pack_summary(matrix, sums):
    kept = jnp.concatenate([matrix[:HEAD_DIM, :FEATS], matrix[HEAD_DIM:PAIR, FEATS:]], axis=1)
    return jnp.concatenate(
        [kept.astype(b16), jnp.broadcast_to(sums, (PACK - HEAD_DIM, 2 * FEATS)).astype(b16)], axis=0
    )


def block_of(own, sib, blk):
    return own[blk] if blk < 2 else sib[blk - 2]


def gather_columns(pieces, target, me):
    for j in range(4):
        at = pl.multiple_of((me ^ j) * PAIR, PAIR)
        target[:, pl.ds(at, PAIR)] = pieces[j][...]


def spread_columns(source, pieces, me):
    for j in range(4):
        at = pl.multiple_of((me ^ j) * PAIR, PAIR)
        pieces[j][...] = source[:, pl.ds(at, PAIR)]


def keys_kernel(me_ref, x0, x1, x2, x3, norm_ref, own, sib, dirs, x_ref, a_ref, k_ref, v_ref, phi_ref,
                pack_own, pack_sib, acc, sums):
    gather_columns((x0, x1, x2, x3), x_ref, me_ref[0])
    acc[...] = jnp.zeros_like(acc)
    sums[...] = jnp.zeros_like(sums)

    def step(i, carry):
        rows = pl.ds(pl.multiple_of(i * TILE, TILE), TILE)
        normed, _ = layer_stats(x_ref[rows, :].astype(f32))
        a = (normed * norm_ref[0:1, :] + norm_ref[1:2, :]).astype(b16)
        a_ref[rows, :] = a
        for blk in range(4):
            kv = mm(a, block_of(own, sib, blk)[:, PAIR : 3 * PAIR]).astype(b16)
            k, v = kv[:, :PAIR], kv[:, PAIR:]
            k_ref[rows, blk * PAIR : (blk + 1) * PAIR] = k
            v_ref[rows, blk * PAIR : (blk + 1) * PAIR] = v
            phi = features(k, dirs[...]).astype(b16)
            phi_ref[rows, blk * 2 * FEATS : (blk + 1) * 2 * FEATS] = phi
            acc[blk] += mm_tn(v, phi)
            sums[blk] += jnp.sum(phi.astype(f32).reshape(TILE // 8, 8, 2 * FEATS), axis=0)
        return carry

    lax.fori_loop(0, x_ref.shape[0] // TILE, step, 0)
    for blk in range(4):
        packed = pack_summary(acc[blk], jnp.sum(sums[blk], axis=0, keepdims=True))
        (pack_own if blk < 2 else pack_sib)[blk % 2] = packed


def queries_kernel(a_ref, own, sib, dirs, q_ref, phi_ref):
    def step(i, carry):
        rows = pl.ds(pl.multiple_of(i * TILE, TILE), TILE)
        a = a_ref[rows, :]
        for blk in range(4):
            q = mm(a, block_of(own, sib, blk)[:, :PAIR]).astype(b16)
            q_ref[rows, blk * PAIR : (blk + 1) * PAIR] = q
            phi_ref[rows, blk * 2 * FEATS : (blk + 1) * 2 * FEATS] = features(q, dirs[...]).astype(b16)
        return carry

    lax.fori_loop(0, a_ref.shape[0] // TILE, step, 0)


def attention_kernel(x_ref, phi_ref, pack_own, pack_sib, out_own, out_sib, hi_ref, lo_ref, summ, wout):
    for blk in range(4):
        summ[blk] = summary_matrix(pack_own if blk < 2 else pack_sib, blk % 2)
        wout[:, blk * PAIR : (blk + 1) * PAIR] = block_of(out_own, out_sib, blk)

    def step(i, carry):
        rows = pl.ds(pl.multiple_of(i * TILE, TILE), TILE)
        heads = []
        for blk in range(4):
            both = mm_nt(phi_ref[rows, blk * 2 * FEATS : (blk + 1) * 2 * FEATS], summ[blk])
            heads.append((both[:, :PAIR] / both[:, PAIR:]).astype(b16))
        hidden = x_ref[rows, :].astype(f32) + mm_nt(jnp.concatenate(heads, axis=1), wout[...])
        high = hidden.astype(b16)
        hi_ref[rows, :] = high
        lo_ref[rows, :] = (hidden - high.astype(f32)).astype(b16)
        return carry

    lax.fori_loop(0, x_ref.shape[0] // TILE, step, 0)


def forward_kernel(me_ref, hi_ref, lo_ref, norm_ref, in_own, in_sib, out_own, out_sib,
                   m0, m1, m2, m3, mixed):
    def step(i, carry):
        rows = pl.ds(pl.multiple_of(i * TILE, TILE), TILE)
        hidden = hi_ref[rows, :].astype(f32) + lo_ref[rows, :].astype(f32)
        normed, _ = layer_stats(hidden)
        c = (normed * norm_ref[2:3, :] + norm_ref[3:4, :]).astype(b16)
        for blk in range(4):
            u = mm(c, block_of(in_own, in_sib, blk))
            g = (u * normal_parts(u)[0]).astype(b16)
            hidden = hidden + mm_nt(g, block_of(out_own, out_sib, blk))
        mixed[rows, :] = hidden.astype(b16)
        return carry

    lax.fori_loop(0, hi_ref.shape[0] // TILE, step, 0)
    spread_columns(mixed, (m0, m1, m2, m3), me_ref[0])


def masked_kernel(me_ref, count_ref, rank_row, rank_col, hi_ref, lo_ref, q_ref, d0, d1, d2, d3, norm_ref,
                  in_own, in_sib, fo_own, fo_sib, out_own, out_sib, pack_own, pack_sib, dirs,
                  gin_keep, gin_send, gfo_keep, gfo_send, gout_keep, gout_send, dpack_own, dpack_sib,
                  dh_ref, dq_ref, norm_grad,
                  dy_ref, summ, wout, acc_in, acc_fo, acc_out, acc_kv, g_s, du_s, cat):
    gather_columns((d0, d1, d2, d3), dy_ref, me_ref[0])
    for blk in range(4):
        summ[blk] = summary_matrix(pack_own if blk < 2 else pack_sib, blk % 2)
        wout[:, blk * PAIR : (blk + 1) * PAIR] = block_of(out_own, out_sib, blk)
    cat[:, :D] = hi_ref[...]
    cat[:, D : 2 * D] = lo_ref[...]
    cat[:, 2 * D : 3 * D] = q_ref[...]
    cat[:, 3 * D :] = dy_ref[...]
    acc_in[...] = jnp.zeros_like(acc_in)
    acc_fo[...] = jnp.zeros_like(acc_fo)
    acc_out[...] = jnp.zeros_like(acc_out)
    acc_kv[...] = jnp.zeros_like(acc_kv)
    dh_ref[...] = jnp.zeros_like(dh_ref)
    dq_ref[...] = jnp.zeros_like(dq_ref)
    norm_grad[...] = jnp.zeros_like(norm_grad)
    total = rank_row.shape[1]
    gain = norm_ref[2:3, :]

    def step(tile, carry):
        base = tile * MASK_TILE
        slots = base + lax.broadcasted_iota(jnp.int32, (MASK_TILE, total), 0)
        pick = jnp.where(rank_row[...] == slots, 1.0, 0.0).astype(b16)
        h_m = mm(pick, cat[:, :D]) + mm(pick, cat[:, D : 2 * D])
        q_m = mm(pick, cat[:, 2 * D : 3 * D]).astype(b16)
        dy = mm(pick, cat[:, 3 * D :])
        dy_low = dy.astype(b16)
        normed, scale = layer_stats(h_m)
        c = (normed * gain + norm_ref[3:4, :]).astype(b16)
        dc = jnp.zeros((MASK_TILE, D), f32)
        for blk in range(4):
            w_in = block_of(in_own, in_sib, blk)
            w_fo = block_of(fo_own, fo_sib, blk)
            u = mm(c, w_in)
            phi, bell = normal_parts(u)
            g = (u * phi).astype(b16)
            slope = phi + u * bell * (1.0 / math.sqrt(2.0 * math.pi))
            du = (mm(dy_low, w_fo) * slope).astype(b16)
            dc = dc + mm_nt(du, w_in)
            acc_fo[blk] += mm_tn(dy_low, g)
            acc_in[blk] += mm_tn(c, du)
        norm_grad[0:8, :] += jnp.sum((dc * normed).reshape(MASK_TILE // 8, 8, D), axis=0)
        norm_grad[8:16, :] += jnp.sum(dc.reshape(MASK_TILE // 8, 8, D), axis=0)
        dh = dy + layer_back(dc, normed, scale, gain)
        dattn = dh.astype(b16)
        dmix = mm(dattn, wout[...])
        dq_blocks = []
        for blk in range(4):
            cols = slice(blk * PAIR, (blk + 1) * PAIR)
            q = q_m[:, cols]
            eq = features(q, dirs[...])
            phi_q = eq.astype(b16)
            both = mm_nt(phi_q, summ[blk])
            num, den = both[:, :PAIR], both[:, PAIR:]
            live = base + lax.broadcasted_iota(jnp.int32, num.shape, 0) < count_ref[0]
            den = jnp.where(live, den, 1.0)
            o = (num / den).astype(b16)
            acc_out[blk] += mm_tn(dattn, o)
            do = dmix[:, cols]
            dnum = (do / den).astype(b16)
            prod = do * num
            first = lax.broadcasted_iota(jnp.int32, prod.shape, 1) < HEAD_DIM
            left = jnp.sum(jnp.where(first, prod, 0.0), axis=1, keepdims=True)
            right = jnp.sum(jnp.where(first, 0.0, prod), axis=1, keepdims=True)
            dden = (-jnp.where(first, left, right) / (den * den)).astype(b16)
            ext = jnp.concatenate([dnum, (dden.astype(f32) * (1.0 / HEAD_DIM)).astype(b16)], axis=1)
            acc_kv[blk] += mm_tn(ext, phi_q)
            d_exp = mm(ext, summ[blk]) * eq
            dp = (SCALE * d_exp).astype(b16)
            lin = mm_nt(dp, dirs[...])
            left = jnp.sum(d_exp[:, :FEATS], axis=1, keepdims=True)
            right = jnp.sum(d_exp[:, FEATS:], axis=1, keepdims=True)
            dq = lin - (SCALE * SCALE) * q.astype(f32) * jnp.where(first, left, right)
            dq_blocks.append(dq.astype(b16))
        slots = base + lax.broadcasted_iota(jnp.int32, (total, MASK_TILE), 1)
        place = jnp.where(rank_col[...] == slots, 1.0, 0.0).astype(b16)
        dh_ref[...] += mm(place, dattn).astype(b16)
        dq_ref[...] += mm(place, jnp.concatenate(dq_blocks, axis=1)).astype(b16)
        return carry

    lax.fori_loop(0, (count_ref[0] + MASK_TILE - 1) // MASK_TILE, step, 0)
    for blk in range(4):
        sums = jnp.concatenate(
            [acc_kv[blk, PAIR : PAIR + 1, :FEATS], acc_kv[blk, PAIR + HEAD_DIM : PAIR + HEAD_DIM + 1, FEATS:]],
            axis=1,
        ) * float(HEAD_DIM)
        (dpack_own if blk < 2 else dpack_sib)[blk % 2] = pack_summary(acc_kv[blk, :PAIR], sums)
    for blk in range(2):
        gin_keep[blk] = acc_in[blk]
        gin_send[blk] = acc_in[blk + 2].astype(b16)
        gfo_keep[blk] = acc_fo[blk]
        gfo_send[blk] = acc_fo[blk + 2].astype(b16)
        gout_keep[blk] = acc_out[blk]
        gout_send[blk] = acc_out[blk + 2].astype(b16)


def inputs_kernel(me_ref, x_ref, a_ref, k_ref, v_ref, phi_ref, dh_ref, dq_ref, pack_own, pack_sib,
                  norm_ref, own, sib, dirs,
                  i0, i1, i2, i3, keep, send, norm_grad, summ, rows_grad, mixed):
    for blk in range(4):
        summ[blk] = summary_matrix(pack_own if blk < 2 else pack_sib, blk % 2)
    norm_grad[...] = jnp.zeros_like(norm_grad)
    wide = 3 * PAIR
    gain = norm_ref[0:1, :]

    def step(i, carry):
        rows = pl.ds(pl.multiple_of(i * TILE, TILE), TILE)
        da = jnp.zeros((TILE, D), f32)
        for blk in range(4):
            cols = slice(blk * PAIR, (blk + 1) * PAIR)
            v = v_ref[rows, cols]
            ext = jnp.concatenate([v, jnp.full(v.shape, 1.0 / HEAD_DIM, b16)], axis=1)
            phi = phi_ref[rows, blk * 2 * FEATS : (blk + 1) * 2 * FEATS]
            d_exp = mm(ext, summ[blk]) * phi.astype(f32)
            dp = (SCALE * d_exp).astype(b16)
            lin = mm_nt(dp, dirs[...])
            left = jnp.sum(d_exp[:, :FEATS], axis=1, keepdims=True)
            right = jnp.sum(d_exp[:, FEATS:], axis=1, keepdims=True)
            first = lax.broadcasted_iota(jnp.int32, lin.shape, 1) < HEAD_DIM
            k = k_ref[rows, cols].astype(f32)
            dk = (lin - (SCALE * SCALE) * k * jnp.where(first, left, right)).astype(b16)
            dv = mm_nt(phi, summ[blk, :PAIR, :]).astype(b16)
            grads = jnp.concatenate([dq_ref[rows, cols], dk, dv], axis=1)
            rows_grad[rows, blk * wide : (blk + 1) * wide] = grads
            da = da + mm_nt(grads, block_of(own, sib, blk))
        normed, scale = layer_stats(x_ref[rows, :].astype(f32))
        norm_grad[0:8, :] += jnp.sum((da * normed).reshape(TILE // 8, 8, D), axis=0)
        norm_grad[8:16, :] += jnp.sum(da.reshape(TILE // 8, 8, D), axis=0)
        grad = dh_ref[rows, :].astype(f32) + layer_back(da, normed, scale, gain)
        mixed[rows, :] = grad.astype(b16)
        return carry

    lax.fori_loop(0, x_ref.shape[0] // TILE, step, 0)
    spread_columns(mixed, (i0, i1, i2, i3), me_ref[0])
    for blk in range(4):
        grad = mm_tn(a_ref[...], rows_grad[:, blk * wide : (blk + 1) * wide])
        if blk < 2:
            keep[blk] = grad
        else:
            send[blk - 2] = grad.astype(b16)


def call(kernel, name, outs, scratch, flops, args, smem=()):
    specs = [
        pl.BlockSpec(memory_space=pltpu.SMEM if i in smem else pltpu.VMEM) for i in range(len(args))
    ]
    moved = sum(math.prod(a.shape) * a.dtype.itemsize for a in list(args) + list(outs))
    return pl.pallas_call(
        kernel,
        name=name,
        out_shape=outs,
        in_specs=specs,
        out_specs=[pl.BlockSpec(memory_space=pltpu.VMEM)] * len(outs),
        scratch_shapes=scratch,
        compiler_params=pltpu.CompilerParams(vmem_limit_bytes=VMEM_LIMIT),
        cost_estimate=pl.CostEstimate(flops=flops, bytes_accessed=moved, transcendentals=0),
    )(*args)


def shape(dims, dtype=b16):
    return jax.ShapeDtypeStruct(dims, dtype)


def swap(block, axis, distance):
    count = lax.axis_size(axis)
    return lax.ppermute(block, axis, [(i, i ^ distance) for i in range(count)])


def bit_of(axis, bit):
    return (lax.axis_index(axis) >> bit) & 1


def widen(block, axis, bit, at):
    other = swap(block, axis, 1 << bit)
    low = bit_of(axis, bit) == 0
    return jnp.stack([jnp.where(low, block, other), jnp.where(low, other, block)], axis=at)


def halve(total, axis, bit, at):
    mine = bit_of(axis, bit)
    away = lax.dynamic_index_in_dim(total, 1 - mine, at, keepdims=False).astype(b16)
    here = lax.dynamic_index_in_dim(total, mine, at, keepdims=False)
    return here + swap(away, axis, 1 << bit).astype(f32)


def tie(value, *others):
    return lax.optimization_barrier((value,) + others)[0]


def row_bits():
    return lax.axis_size("rows").bit_length() - 1


def gather_y_first(shard):
    bits = row_bits()
    block = widen(shard, "heads", 1, 0)
    for step in range(bits):
        block = widen(block, "rows", bits - 1 - step, 1 + step)
    own = block.reshape(2, D, shard.shape[1])
    return own, swap(own, "heads", 1)


def gather_y_last(shard):
    bits = row_bits()
    block = shard
    for step in range(bits):
        block = widen(block, "rows", bits - 1 - step, step)
    own = widen(block, "heads", 1, 0).reshape(2, D, shard.shape[1])
    return own, swap(own, "heads", 1)


def scatter_sum(keep, send, y_first):
    bits = row_bits()
    total = keep + swap(send, "heads", 1).astype(f32)
    total = total.reshape((2,) * (1 + bits) + (D >> bits, keep.shape[2]))
    if y_first:
        total = halve(total, "heads", 1, 0)
    for bit in range(bits):
        total = halve(total, "rows", bit, total.ndim - 3)
    if not y_first:
        total = halve(total, "heads", 1, 0)
    return total


def sequence_sum(own, sib):
    total = own.astype(f32) + swap(sib, "heads", 1).astype(f32)
    total = total + swap(total.astype(b16), "rows", 1).astype(f32)
    total = (total + swap(total.astype(b16), "heads", 2).astype(f32)).astype(b16)
    return total, swap(total, "heads", 1)


def split_rows(block):
    me = lax.axis_index("heads")
    parts = block.reshape(4, block.shape[0] // 4, block.shape[1])
    got = [lax.dynamic_index_in_dim(parts, me, 0, keepdims=False)]
    for j in (1, 2, 3):
        got.append(swap(lax.dynamic_index_in_dim(parts, me ^ j, 0, keepdims=False), "heads", j))
    return got


def join_rows(pieces, dtype):
    got = [pieces[0]] + [swap(pieces[j], "heads", j) for j in (1, 2, 3)]
    low = bit_of("heads", 0) == 0
    high = bit_of("heads", 1) == 0
    a = jnp.where(low, got[0], got[1]), jnp.where(low, got[1], got[0])
    b = jnp.where(low, got[2], got[3]), jnp.where(low, got[3], got[2])
    rows = [jnp.where(high, a[0], b[0]), jnp.where(high, a[1], b[1]),
            jnp.where(high, b[0], a[0]), jnp.where(high, b[1], a[1])]
    return jnp.concatenate(rows, axis=0).astype(dtype)


def all_norms(gains):
    block = widen(widen(gains, "heads", 1, 1), "heads", 0, 2)
    return block.reshape(gains.shape[0], 4 * gains.shape[1])


def mask_ranks(masked_pos, masked_count, rows_dev, n):
    group = lax.axis_index("rows")
    offset = group % SPAN * rows_dev + lax.axis_index("heads") * n
    place = lax.dynamic_index_in_dim(masked_pos, group // SPAN, 0, keepdims=False) - offset
    limit = lax.dynamic_index_in_dim(masked_count, group // SPAN, 0, keepdims=False)
    inside = (jnp.arange(place.shape[0], dtype=jnp.int32) < limit) & (place >= 0) & (place < n)
    side = 32
    grid = jnp.arange(side, dtype=jnp.int32)[None, :]
    high = ((place // side)[:, None] == grid) & inside[:, None]
    low = (place % side)[:, None] == grid
    hits = mm_tn(high.astype(b16), low.astype(b16))
    marks = jnp.minimum(hits, 1.0)
    lower = grid < grid.T
    within = mm_nt(marks.astype(b16), lower.astype(b16))
    rows = jnp.sum(marks, axis=1)
    before = jnp.sum(jnp.where(lower, rows[None, :], 0.0), axis=1)
    rank = jnp.where(marks > 0, within + before[:, None], -1.0).astype(jnp.int32)
    count = jnp.sum(rows).astype(jnp.int32)
    return rank.reshape(1, n), rank.reshape(n, 1), count.reshape(1)


def body(
    tokens,
    ln1_gain,
    ln1_bias,
    qkv_weight,
    out_weight,
    ln2_gain,
    ln2_bias,
    ffn_in,
    ffn_out,
    feature_proj,
    masked_pos,
    masked_count,
    out_grad,
):
    rows_dev = tokens.shape[0]
    n = rows_dev // 4
    me = lax.axis_index("heads").astype(jnp.int32).reshape(1)
    zero = jnp.zeros_like(feature_proj)
    dirs = jnp.concatenate(
        [jnp.concatenate([feature_proj, zero], 1), jnp.concatenate([zero, feature_proj], 1)], 0
    )

    qkv_shard = qkv_weight.transpose(2, 0, 1).reshape(qkv_weight.shape[2], -1)
    in_shard = ffn_in.T
    rest_shard = jnp.concatenate([ffn_out.T, out_weight.T], axis=1)

    x_parts = split_rows(tokens)
    norms = all_norms(jnp.stack([ln1_gain, ln1_bias, ln2_gain, ln2_bias]))
    qkv_own, qkv_sib = gather_y_first(qkv_shard)
    in_own, in_sib = gather_y_first(in_shard)
    rest_own, rest_sib = gather_y_last(rest_shard)
    hidden = ffn_out.shape[0]
    fo_own, fo_sib = rest_own[:, :, :hidden], rest_sib[:, :, :hidden]
    out_own, out_sib = rest_own[:, :, hidden:], rest_sib[:, :, hidden:]
    dy_parts = split_rows(out_grad)
    rank_row, rank_col, count = mask_ranks(masked_pos, masked_count, rows_dev, n)

    x, a, k, v, phi_k, kv_own, kv_sib = call(
        keys_kernel, "keys",
        [shape((n, D)), shape((n, D)), shape((n, D)), shape((n, D)), shape((n, 4 * D)),
         shape((2, PACK, D)), shape((2, PACK, D))],
        [pltpu.VMEM((4, PAIR, D), f32), pltpu.VMEM((4, 8, D), f32)],
        2 * n * 2_000_000, [me, *x_parts, norms, qkv_own, qkv_sib, dirs], smem=(0,),
    )
    q, phi_q = call(
        queries_kernel, "queries", [shape((n, D)), shape((n, 4 * D))], [],
        2 * n * 1_000_000, [a, qkv_own, qkv_sib, dirs],
    )
    kv_own, kv_sib = sequence_sum(kv_own, kv_sib)
    high, low = call(
        attention_kernel, "attention", [shape((n, D)), shape((n, D))],
        [pltpu.VMEM((4, 256, D), b16), pltpu.VMEM((D, D), b16)],
        2 * n * 800_000, [x, phi_q, kv_own, kv_sib, out_own, out_sib],
    )
    (gin_keep, gin_send, gfo_keep, gfo_send, gout_keep, gout_send, dkv_own, dkv_sib, dh, dq,
     norm_two) = call(
        masked_kernel, "masked",
        [shape((2, D, hidden), f32), shape((2, D, hidden)), shape((2, D, hidden), f32),
         shape((2, D, hidden)), shape((2, D, PAIR), f32), shape((2, D, PAIR)),
         shape((2, PACK, D)), shape((2, PACK, D)), shape((n, D)), shape((n, D)), shape((16, D), f32)],
        [pltpu.VMEM((n, D), b16), pltpu.VMEM((4, 256, D), b16), pltpu.VMEM((D, D), b16),
         pltpu.VMEM((4, D, hidden), f32), pltpu.VMEM((4, D, hidden), f32),
         pltpu.VMEM((4, D, PAIR), f32), pltpu.VMEM((4, 256, D), f32),
         pltpu.VMEM((8, 128), b16), pltpu.VMEM((8, 128), b16), pltpu.VMEM((n, 4 * D), b16)],
        2 * MASK_TILE * 10_000_000,
        [me, count, rank_row, rank_col, high, low, q, *dy_parts, norms, in_own, in_sib, fo_own, fo_sib,
         out_own, out_sib, kv_own, kv_sib, dirs],
        smem=(0, 1),
    )
    dkv_own, dkv_sib = sequence_sum(dkv_own, dkv_sib)
    mixed_parts = call(
        forward_kernel, "forward", [shape((n, PAIR))] * 4, [pltpu.VMEM((n, D), b16)],
        2 * n * 4_000_000, [me, high, low, norms, in_own, in_sib, fo_own, fo_sib], smem=(0,),
    )
    i0, i1, i2, i3, gqkv_keep, gqkv_send, norm_one = call(
        inputs_kernel, "inputs",
        [shape((n, PAIR))] * 4 + [shape((2, D, 3 * PAIR), f32), shape((2, D, 3 * PAIR)), shape((16, D), f32)],
        [pltpu.VMEM((4, 256, D), b16), pltpu.VMEM((n, 3 * D), b16), pltpu.VMEM((n, D), b16)],
        2 * n * 3_000_000,
        [me, x, a, k, v, phi_k, dh, dq, dkv_own, dkv_sib, norms, qkv_own, qkv_sib, dirs], smem=(0,),
    )
    mixed_out = join_rows(mixed_parts, b16)
    input_grad = join_rows([i0, i1, i2, i3], f32)
    gin = scatter_sum(gin_keep, gin_send, False)
    grest = scatter_sum(
        jnp.concatenate([gfo_keep, gout_keep], 2), jnp.concatenate([gfo_send, gout_send], 2), True
    )
    gqkv = scatter_sum(gqkv_keep, gqkv_send, False)

    sums = jnp.concatenate([norm_one, norm_two], 0).reshape(4, 8, D).sum(1)
    sums = sums + swap(sums, "heads", 1)
    for bit in range(row_bits()):
        sums = sums + swap(sums, "rows", 1 << bit)
    sums = sums + swap(sums, "heads", 2)
    mine = lax.dynamic_slice_in_dim(sums, lax.axis_index("heads") * PAIR, PAIR, 1)

    return (
        mixed_out,
        input_grad,
        gqkv.reshape(gqkv.shape[0], 3, PAIR).transpose(1, 2, 0),
        grest[:, hidden:].T,
        gin.T,
        grest[:, :hidden].T,
        mine[0],
        mine[1],
        mine[2],
        mine[3],
    )


def solution(mesh):
    in_specs = (
        P("rows", "heads"),
        P("heads"),
        P("heads"),
        P(None, "heads", "rows"),
        P("heads", "rows"),
        P("heads"),
        P("heads"),
        P("heads", "rows"),
        P("heads", "rows"),
        P(),
        P(),
        P(),
        P("rows", "heads"),
    )
    out_specs = (
        P("rows", "heads"),
        P("rows", "heads"),
        P(None, "heads", "rows"),
        P("heads", "rows"),
        P("heads", "rows"),
        P("heads", "rows"),
        P("heads"),
        P("heads"),
        P("heads"),
        P("heads"),
    )
    return jax.shard_map(body, mesh=mesh, in_specs=in_specs, out_specs=out_specs, check_vma=False)
```

```python
import math

import jax
import jax.numpy as jnp
from jax import lax
from jax.experimental import pallas as pl
from jax.experimental.pallas import tpu as pltpu
from jax.sharding import PartitionSpec as P

D = 512
HEAD_DIM = 64
FEATS = 256
PAIR = 2 * HEAD_DIM
SPAN = 2
PACK = 80
SCALE = HEAD_DIM ** (-0.25)
HALF_SQ = 0.5 * SCALE * SCALE
LOG2E = math.log2(math.e)
LOG2_ROOT = 0.5 * math.log2(FEATS)
epsilon = 1e-05
f32 = jnp.float32
b16 = jnp.bfloat16
MIB = 1024 * 1024
TILE = 1024
FORWARD_TILE = 512
MASK_TILE = 304
US = 1.15e9


def mm(left, right):
    return lax.dot_general(left, right, (((1,), (0,)), ((), ())), preferred_element_type=f32)


def mm_nt(left, right):
    return lax.dot_general(left, right, (((1,), (1,)), ((), ())), preferred_element_type=f32)


def mm_tn(left, right):
    return lax.dot_general(left, right, (((0,), (0,)), ((), ())), preferred_element_type=f32)


def layer_stats(values):
    mean = jnp.sum(values, axis=1, keepdims=True) * (1.0 / D)
    centred = values - mean
    var = jnp.sum(centred * centred, axis=1, keepdims=True) * (1.0 / D)
    scale = lax.rsqrt(var + epsilon)
    return centred * scale, scale


def layer_back(grad, normed, scale, gain):
    scaled = grad * gain
    first = jnp.sum(scaled, axis=1, keepdims=True) * (1.0 / D)
    second = jnp.sum(scaled * normed, axis=1, keepdims=True) * (1.0 / D)
    return scale * (scaled - first - normed * second)


def features(rows, directions):
    projected = mm(rows, directions)
    wide = rows.astype(f32)
    square = wide * wide
    first = lax.broadcasted_iota(jnp.int32, square.shape, 1) < HEAD_DIM
    left = jnp.sum(jnp.where(first, square, 0.0), axis=1, keepdims=True)
    right = jnp.sum(jnp.where(first, 0.0, square), axis=1, keepdims=True)
    return jnp.concatenate(
        [
            jnp.exp2((SCALE * LOG2E) * projected[:, :FEATS] - (HALF_SQ * LOG2E * left + LOG2_ROOT)),
            jnp.exp2((SCALE * LOG2E) * projected[:, FEATS:] - (HALF_SQ * LOG2E * right + LOG2_ROOT)),
        ],
        axis=1,
    )


def normal_cdf(u):
    return 0.5 + 0.5 * lax.erf(u * math.sqrt(0.5))


def summary_matrix(packed, blk):
    half = packed[blk]
    zero = jnp.zeros((HEAD_DIM, FEATS), b16)
    top = jnp.concatenate([half[:HEAD_DIM, :FEATS], zero], axis=1)
    low = jnp.concatenate([zero, half[:HEAD_DIM, FEATS:]], axis=1)
    sums = half[HEAD_DIM : HEAD_DIM + 1].astype(f32)
    rows = jnp.broadcast_to(sums, (HEAD_DIM, 2 * FEATS))
    left = lax.broadcasted_iota(jnp.int32, rows.shape, 1) < FEATS
    return jnp.concatenate(
        [
            top,
            low,
            jnp.where(left, rows, 0.0).astype(b16),
            jnp.where(left, 0.0, rows).astype(b16),
        ],
        axis=0,
    )


def pack_summary(matrix, sums):
    kept = jnp.concatenate([matrix[:HEAD_DIM, :FEATS], matrix[HEAD_DIM:PAIR, FEATS:]], axis=1)
    return jnp.concatenate(
        [kept.astype(b16), jnp.broadcast_to(sums, (PACK - HEAD_DIM, 2 * FEATS)).astype(b16)], axis=0
    )


def block_of(own, sib, blk):
    return own[blk] if blk < 2 else sib[blk - 2]


def gather_columns(block, side, near, target, me):
    n = target.shape[0]
    parts = (
        block[pl.ds(pl.multiple_of(me * n, n), n), :],
        near[0, :n, :],
        side[pl.ds(pl.multiple_of((me & 1) * n, n), n), :],
        near[1, :n, :],
    )
    for j in range(4):
        target[:, pl.ds(pl.multiple_of((me ^ j) * PAIR, PAIR), PAIR)] = parts[j]


def spread_columns(source, own, near, far, me):
    def columns(j):
        return source[:, pl.ds(pl.multiple_of((me ^ j) * PAIR, PAIR), PAIR)]

    own[...] = columns(0)
    near[0] = columns(1)
    near[1] = columns(3)
    far[...] = columns(2)


def norm_kernel(me_ref, block, side, near, gains_own, x_ref, a_ref, norm_ref):
    n = x_ref.shape[0]
    gather_columns(block, side, near, x_ref, me_ref[0])
    for blk in range(4):
        core = (me_ref[0] & 1) ^ (blk // 2)
        at = pl.multiple_of((blk % 2 * 2 + core) * PAIR, PAIR)
        if blk < 2:
            part = gains_own[blk].astype(f32)
        else:
            part = near[(me_ref[0] >> 1) ^ (blk - 2), n:, :].astype(f32)
        norm_ref[:, pl.ds(at, PAIR)] = part[0:4] + (part[4:8] + part[8:12])

    def step(i, carry):
        rows = pl.ds(pl.multiple_of(i * TILE, TILE), TILE)
        normed, _ = layer_stats(x_ref[rows, :].astype(f32))
        a_ref[rows, :] = (normed * norm_ref[0:1, :] + norm_ref[1:2, :]).astype(b16)
        return carry

    lax.fori_loop(0, x_ref.shape[0] // TILE, step, 0)


def keys_kernel(a_ref, own, sib, dirs, k_ref, v_ref, phi_ref, pack_own, pack_sib, acc, sums):
    acc[...] = jnp.zeros_like(acc)
    sums[...] = jnp.zeros_like(sums)

    def step(i, carry):
        rows = pl.ds(pl.multiple_of(i * TILE, TILE), TILE)
        a = a_ref[rows, :]
        for blk in range(4):
            kv = mm(a, block_of(own, sib, blk)[:, PAIR : 3 * PAIR]).astype(b16)
            k, v = kv[:, :PAIR], kv[:, PAIR:]
            k_ref[rows, blk * PAIR : (blk + 1) * PAIR] = k
            v_ref[rows, blk * PAIR : (blk + 1) * PAIR] = v
            phi = features(k, dirs[...]).astype(b16)
            phi_ref[rows, blk * 2 * FEATS : (blk + 1) * 2 * FEATS] = phi
            acc[blk] += mm_tn(v, phi)
            sums[blk] += jnp.sum(phi.astype(f32).reshape(TILE // 8, 8, 2 * FEATS), axis=0)
        return carry

    lax.fori_loop(0, a_ref.shape[0] // TILE, step, 0)
    for blk in range(4):
        packed = pack_summary(acc[blk], jnp.sum(sums[blk], axis=0, keepdims=True))
        (pack_own if blk < 2 else pack_sib)[blk % 2] = packed


def queries_kernel(a_ref, own, sib, dirs, phi_ref):
    def step(i, carry):
        rows = pl.ds(pl.multiple_of(i * TILE, TILE), TILE)
        a = a_ref[rows, :]
        for blk in range(4):
            q = mm(a, block_of(own, sib, blk)[:, :PAIR]).astype(b16)
            phi_ref[rows, blk * 2 * FEATS : (blk + 1) * 2 * FEATS] = features(q, dirs[...]).astype(b16)
        return carry

    lax.fori_loop(0, a_ref.shape[0] // TILE, step, 0)


def attention_kernel(x_ref, phi_ref, pack_own, pack_sib, qkvo_own, qkvo_sib, hi_ref, lo_ref, summ, wout):
    for blk in range(4):
        summ[blk] = summary_matrix(pack_own if blk < 2 else pack_sib, blk % 2)
        wout[:, blk * PAIR : (blk + 1) * PAIR] = block_of(qkvo_own, qkvo_sib, blk)[:, 3 * PAIR :]

    def step(i, carry):
        rows = pl.ds(pl.multiple_of(i * TILE, TILE), TILE)
        heads = []
        for blk in range(4):
            both = mm_nt(phi_ref[rows, blk * 2 * FEATS : (blk + 1) * 2 * FEATS], summ[blk])
            heads.append((both[:, :PAIR] / both[:, PAIR:]).astype(b16))
        hidden = x_ref[rows, :].astype(f32) + mm_nt(jnp.concatenate(heads, axis=1), wout[...])
        high = hidden.astype(b16)
        hi_ref[rows, :] = high
        lo_ref[rows, :] = (hidden - high.astype(f32)).astype(b16)
        return carry

    lax.fori_loop(0, x_ref.shape[0] // TILE, step, 0)


def forward_kernel(me_ref, hi_ref, lo_ref, norm_ref, in_own, in_sib, out_own, out_sib, m_own, m_near, m_far, mixed,
                   low_ref, sum_ref):
    def step(i, carry):
        rows = pl.ds(pl.multiple_of(i * FORWARD_TILE, FORWARD_TILE), FORWARD_TILE)
        hidden = hi_ref[rows, :].astype(f32) + lo_ref[rows, :].astype(f32)
        normed, _ = layer_stats(hidden)
        low_ref[...] = (normed * norm_ref[2:3, :] + norm_ref[3:4, :]).astype(b16)
        sum_ref[...] = hidden
        for w_in, w_out in ((in_own, out_own), (in_sib, out_sib)):

            def block(blk, carry, w_in=w_in, w_out=w_out):
                u = mm(low_ref[...], w_in[blk])
                g = (u * normal_cdf(u)).astype(b16)
                sum_ref[...] += mm_nt(g, w_out[blk])
                return carry

            lax.fori_loop(0, 2, block, 0)
        mixed[rows, :] = sum_ref[...].astype(b16)
        return carry

    lax.fori_loop(0, hi_ref.shape[0] // FORWARD_TILE, step, 0)
    spread_columns(mixed, m_own, m_near, m_far, me_ref[0])


def masked_kernel(me_ref, count_ref, rank_row, hi_ref, lo_ref, a_ref, dy_block, dy_side, dy_near, norm_ref,
                  in_own, in_sib, fo_own, fo_sib, qkvo_own, qkvo_sib, pack_own, pack_sib, dirs,
                  ino_keep, ino_send, foq_keep, foq_send, dpack_own, dpack_sib, dh_ref, da_ref, norm_grad,
                  dy_ref, summ, wout, w_in, w_fo, w_q, ino, foq, acc_kv, dc_ref, dmix_ref):
    hidden = fo_own.shape[2]
    total = rank_row.shape[1]
    gather_columns(dy_block, dy_side, dy_near, dy_ref, me_ref[0])
    for blk in range(4):
        summ[blk] = summary_matrix(pack_own if blk < 2 else pack_sib, blk % 2)
        wout[:, blk * PAIR : (blk + 1) * PAIR] = block_of(qkvo_own, qkvo_sib, blk)[:, 3 * PAIR :]
        w_in[blk] = block_of(in_own, in_sib, blk)
        w_fo[blk] = block_of(fo_own, fo_sib, blk)
        w_q[blk] = block_of(qkvo_own, qkvo_sib, blk)[:, :PAIR]
    gain = norm_ref[2:3, :]

    def step(tile, carry):
        def put(ref, at, value):
            before = jnp.where(tile > 0, ref[at].astype(f32), 0.0)
            ref[at] = (before + value).astype(ref.dtype)

        base = tile * MASK_TILE
        slots = base + lax.broadcasted_iota(jnp.int32, (MASK_TILE, total), 0)
        pick = jnp.where(rank_row[...] == slots, 1.0, 0.0).astype(b16)
        h_m = mm(pick, hi_ref[...]) + mm(pick, lo_ref[...])
        a_m = mm(pick, a_ref[...]).astype(b16)
        dy = mm(pick, dy_ref[...])
        dy_low = dy.astype(b16)
        normed, scale = layer_stats(h_m)
        c = (normed * gain + norm_ref[3:4, :]).astype(b16)
        dc_ref[...] = jnp.zeros_like(dc_ref)

        def hidden_block(blk, carry):
            u = mm(c, w_in[blk])
            phi = normal_cdf(u)
            g = (u * phi).astype(b16)
            slope = phi + u * (jnp.exp(-0.5 * u * u) * (1.0 / math.sqrt(2.0 * math.pi)))
            du = (mm(dy_low, w_fo[blk]) * slope).astype(b16)
            dc_ref[...] += mm_nt(du, w_in[blk])
            put(foq, (blk, slice(None), slice(0, hidden)), mm_tn(dy_low, g))
            put(ino, (blk, slice(None), slice(0, hidden)), mm_tn(c, du))
            return carry

        lax.fori_loop(0, 4, hidden_block, 0)
        dc = dc_ref[...]
        put(norm_grad, slice(0, 8), jnp.sum((dc * normed).reshape(MASK_TILE // 8, 8, D), axis=0))
        put(norm_grad, slice(8, 16), jnp.sum(dc.reshape(MASK_TILE // 8, 8, D), axis=0))
        dh = dy + layer_back(dc, normed, scale, gain)
        dattn = dh.astype(b16)
        dmix = mm(dattn, wout[...])
        for blk in range(4):
            dmix_ref[blk] = dmix[:, blk * PAIR : (blk + 1) * PAIR]
        dc_ref[...] = jnp.zeros_like(dc_ref)

        def head_block(blk, carry):
            q = mm(a_m, w_q[blk]).astype(b16)
            eq = features(q, dirs[...])
            phi_q = eq.astype(b16)
            both = mm_nt(phi_q, summ[blk])
            num, den = both[:, :PAIR], both[:, PAIR:]
            inverse = 1.0 / den
            o = (num * inverse).astype(b16)
            put(ino, (blk, slice(None), slice(hidden, hidden + PAIR)), mm_tn(dattn, o))
            do = dmix_ref[blk]
            dnum = (do * inverse).astype(b16)
            prod = do * num
            first = lax.broadcasted_iota(jnp.int32, prod.shape, 1) < HEAD_DIM
            left = jnp.sum(jnp.where(first, prod, 0.0), axis=1, keepdims=True)
            right = jnp.sum(jnp.where(first, 0.0, prod), axis=1, keepdims=True)
            dden = (-jnp.where(first, left, right) * inverse * inverse).astype(b16)
            ext = jnp.concatenate([dnum, (dden.astype(f32) * (1.0 / HEAD_DIM)).astype(b16)], axis=1)
            put(acc_kv, blk, mm_tn(ext, phi_q))
            d_exp = mm(ext, summ[blk]) * eq
            dp = (SCALE * d_exp).astype(b16)
            lin = mm_nt(dp, dirs[...])
            left = jnp.sum(d_exp[:, :FEATS], axis=1, keepdims=True)
            right = jnp.sum(d_exp[:, FEATS:], axis=1, keepdims=True)
            dq = (lin - (SCALE * SCALE) * q.astype(f32) * jnp.where(first, left, right)).astype(b16)
            put(foq, (blk, slice(None), slice(hidden, hidden + PAIR)), mm_tn(a_m, dq))
            dc_ref[...] += mm_nt(dq, w_q[blk])
            return carry

        lax.fori_loop(0, 4, head_block, 0)
        put(dh_ref, slice(None), mm_tn(pick, dattn))
        put(da_ref, slice(None), mm_tn(pick, dc_ref[...].astype(b16)))
        return carry

    lax.fori_loop(0, jnp.maximum((count_ref[0] + MASK_TILE - 1) // MASK_TILE, 1), step, 0)
    for blk in range(4):
        sums = jnp.concatenate(
            [acc_kv[blk, PAIR : PAIR + 1, :FEATS], acc_kv[blk, PAIR + HEAD_DIM : PAIR + HEAD_DIM + 1, FEATS:]],
            axis=1,
        ) * float(HEAD_DIM)
        (dpack_own if blk < 2 else dpack_sib)[blk % 2] = pack_summary(acc_kv[blk, :PAIR], sums)
        (ino_keep if blk < 2 else ino_send)[blk % 2] = ino[blk]
        (foq_keep if blk < 2 else foq_send)[blk % 2] = foq[blk]


def inputs_kernel(me_ref, x_ref, k_ref, v_ref, phi_ref, dh_ref, da_ref, pack_own, pack_sib,
                  norm_ref, own, sib, dirs, norm_two,
                  i_own, i_near, i_far, rows_grad, norm_sums, summ, mixed, norm_grad):
    for blk in range(4):
        summ[blk] = summary_matrix(pack_own if blk < 2 else pack_sib, blk % 2)
    norm_grad[...] = jnp.zeros_like(norm_grad)
    wide = 2 * PAIR
    gain = norm_ref[0:1, :]

    def step(i, carry):
        rows = pl.ds(pl.multiple_of(i * TILE, TILE), TILE)
        da = da_ref[rows, :].astype(f32)
        for blk in range(4):
            cols = slice(blk * PAIR, (blk + 1) * PAIR)
            v = v_ref[rows, cols]
            ext = jnp.concatenate([v, jnp.full(v.shape, 1.0 / HEAD_DIM, b16)], axis=1)
            phi = phi_ref[rows, blk * 2 * FEATS : (blk + 1) * 2 * FEATS]
            d_exp = mm(ext, summ[blk]) * phi.astype(f32)
            dp = (SCALE * d_exp).astype(b16)
            lin = mm_nt(dp, dirs[...])
            left = jnp.sum(d_exp[:, :FEATS], axis=1, keepdims=True)
            right = jnp.sum(d_exp[:, FEATS:], axis=1, keepdims=True)
            first = lax.broadcasted_iota(jnp.int32, lin.shape, 1) < HEAD_DIM
            k = k_ref[rows, cols].astype(f32)
            dk = (lin - (SCALE * SCALE) * k * jnp.where(first, left, right)).astype(b16)
            dv = mm_nt(phi, summ[blk, :PAIR, :]).astype(b16)
            grads = jnp.concatenate([dk, dv], axis=1)
            rows_grad[rows, blk * wide : (blk + 1) * wide] = grads
            da = da + mm_nt(grads, block_of(own, sib, blk)[:, PAIR : 3 * PAIR])
        normed, scale = layer_stats(x_ref[rows, :].astype(f32))
        norm_grad[0:8, :] += jnp.sum((da * normed).reshape(TILE // 8, 8, D), axis=0)
        norm_grad[8:16, :] += jnp.sum(da.reshape(TILE // 8, 8, D), axis=0)
        grad = dh_ref[rows, :].astype(f32) + layer_back(da, normed, scale, gain)
        mixed[rows, :] = grad.astype(b16)
        return carry

    lax.fori_loop(0, x_ref.shape[0] // TILE, step, 0)
    spread_columns(mixed, i_own, i_near, i_far, me_ref[0])
    for i in range(4):
        source = norm_grad if i < 2 else norm_two
        row = jnp.sum(source[i % 2 * 8 : i % 2 * 8 + 8, :], axis=0, keepdims=True)
        norm_sums[i : i + 1, :] = row[:, : D // 2]
        norm_sums[4 + i : 5 + i, :] = row[:, D // 2 :]


def weights_kernel(a_ref, rows_grad, norm_sums, keep, send):
    wide = 2 * PAIR
    for blk in (2, 3, 0, 1):
        grad = mm_tn(a_ref[...], rows_grad[:, blk * wide : (blk + 1) * wide])
        if blk < 2:
            keep[blk * D : (blk + 1) * D] = grad
        else:
            send[(blk - 2) * D : (blk - 1) * D] = grad.astype(b16)
    send[2 * D :] = two_parts(norm_sums[...])


def two_parts(values):
    high = values.astype(b16)
    return jnp.concatenate([high, (values - high.astype(f32)).astype(b16)], axis=0)


def call(kernel, name, outs, scratch, micros, args, smem=(), vmem=20):
    specs = [
        pl.BlockSpec(memory_space=pltpu.SMEM if i in smem else pltpu.VMEM) for i in range(len(args))
    ]
    return pl.pallas_call(
        kernel,
        name=name,
        out_shape=outs,
        in_specs=specs,
        out_specs=[pl.BlockSpec(memory_space=pltpu.VMEM)] * len(outs),
        scratch_shapes=scratch,
        compiler_params=pltpu.CompilerParams(vmem_limit_bytes=vmem * MIB),
        cost_estimate=pl.CostEstimate(flops=int(micros * US), bytes_accessed=1_000, transcendentals=0),
    )(*args)


def shape(dims, dtype=b16):
    return jax.ShapeDtypeStruct(dims, dtype)


def swap(block, rows=0, heads=0):
    count = lax.axis_size("heads")
    if rows == 0:
        return lax.ppermute(block, "heads", [(i, i ^ heads) for i in range(count)])
    total = lax.axis_size("rows")
    if heads == 0:
        return lax.ppermute(block, "rows", [(i, i ^ rows) for i in range(total)])
    pairs = [
        (r * count + h, (r ^ rows) * count + (h ^ heads)) for r in range(total) for h in range(count)
    ]
    return lax.ppermute(block, ("rows", "heads"), pairs)


def bit_of(axis, bit):
    return (lax.axis_index(axis) >> bit) & 1


def sort_blocks(blocks, low_bits):
    blocks = list(blocks)
    for i, low in enumerate(low_bits):
        for d in range(len(blocks)):
            if d >> i & 1 == 0:
                one, two = blocks[d], blocks[d | 1 << i]
                blocks[d] = jnp.where(low, one, two)
                blocks[d | 1 << i] = jnp.where(low, two, one)
    return blocks


def tie(value, *others):
    return lax.optimization_barrier((value,) + others)[0]


def row_bits():
    return lax.axis_size("rows").bit_length() - 1


def chunks_of_bits():
    high = row_bits()
    groups = []
    while high > 1:
        width = min(2, high - 1)
        high -= width
        groups.append((high, width))
    return groups


def widen_bit(block, axis, bit, at, after=()):
    other = swap(block, rows=1 << bit) if axis == "rows" else swap(block, heads=1 << bit)
    other = tie(other, *after)
    return jnp.stack(sort_blocks([block, other], [bit_of(axis, bit) == 0]), axis=at)


def widen_high(block, at, after=()):
    for low, width in chunks_of_bits():
        got = [block] + [tie(swap(block, rows=d << low), *after) for d in range(1, 1 << width)]
        lows = [bit_of("rows", low + i) == 0 for i in range(width)]
        block = jnp.stack(sort_blocks(got, lows), axis=at)
        at += 1
    return block


def widen_square(block, before):
    late = tie(block, *before)
    got = [block, swap(block, rows=1), swap(late, heads=2), swap(late, rows=1, heads=2)]
    got = sort_blocks(got, [bit_of("rows", 0) == 0, bit_of("heads", 1) == 0])
    at = block.ndim - 2
    sides = [jnp.stack(got[:2], axis=at), jnp.stack(got[2:], axis=at)]
    return jnp.stack(sides).reshape(2, D, block.shape[-1])


def halve(total, axis, bit, at, after=()):
    mine = bit_of(axis, bit)
    away = lax.dynamic_index_in_dim(total, 1 - mine, at, keepdims=False)
    here = lax.dynamic_index_in_dim(total, mine, at, keepdims=False)
    other = swap(away, rows=1 << bit) if axis == "rows" else swap(away, heads=1 << bit)
    return (here.astype(f32) + tie(other, *after).astype(f32)).astype(b16)


def add_low(one, two):
    return (one.astype(f32) + two.astype(f32)).astype(b16)


def spread_sum(total, beside):
    sent = total.astype(b16)
    got = [tie(swap(sent, rows=rows, heads=heads), *beside) for rows, heads in ((1, 0), (0, 2), (1, 2))]
    for block in got:
        total = total + block.astype(f32)
    total = total.astype(b16)
    return total, swap(total, heads=1)


def add_parts(sums, got):
    tail = sums.shape[0]
    return sums + (got[-2 * tail : -tail].astype(f32) + got[-tail:].astype(f32))


def add_sibling(keep, send, sums):
    got = swap(send, heads=1)
    total = keep + got[: -2 * sums.shape[0]].astype(f32)
    return total.reshape((2,) * (1 + row_bits()) + (D >> row_bits(), keep.shape[1])), add_parts(sums, got)


def sum_stage(total, sums, axis, bit, at, after=()):
    wide = total.shape[-1]
    mine = bit_of(axis, bit)
    away = lax.dynamic_index_in_dim(total, 1 - mine, at, keepdims=False).astype(b16).reshape(-1, wide)
    total = lax.dynamic_index_in_dim(total, mine, at, keepdims=False)
    away = jnp.concatenate([away, two_parts(sums)], axis=0)
    got = tie(swap(away, rows=1 << bit) if axis == "rows" else swap(away, heads=1 << bit), *after)
    total = total + got[: -2 * sums.shape[0]].reshape(total.shape).astype(f32)
    return total, add_parts(sums, got)


def side_rows(block):
    parts = block.reshape(2, block.shape[0] // 2, block.shape[1])
    return lax.dynamic_index_in_dim(parts, 1 - bit_of("heads", 1), 0, keepdims=False)


def near_rows(block, side):
    core = bit_of("heads", 0)
    n = block.shape[0] // 4
    own = lax.dynamic_slice_in_dim(block, (2 * bit_of("heads", 1) + 1 - core) * n, n, 0)
    return jnp.stack([own, lax.dynamic_slice_in_dim(side, (1 - core) * n, n, 0)])


def join_rows(own, near, side, dtype):
    got = sort_blocks([own, near[0], side[0], side[1]], [bit_of("heads", 0) == 0, bit_of("heads", 1) == 0])
    return jnp.concatenate(got, axis=0).astype(dtype)


def mask_ranks(masked_pos, masked_count, rows_dev, n):
    group = lax.axis_index("rows")
    offset = group % SPAN * rows_dev + lax.axis_index("heads") * n
    place = lax.dynamic_index_in_dim(masked_pos, group // SPAN, 0, keepdims=False) - offset
    limit = lax.dynamic_index_in_dim(masked_count, group // SPAN, 0, keepdims=False)
    inside = (jnp.arange(place.shape[0], dtype=jnp.int32) < limit) & (place >= 0) & (place < n)
    side = 32
    grid = jnp.arange(side, dtype=jnp.int32)[None, :]
    high = ((place // side)[:, None] == grid) & inside[:, None]
    low = (place % side)[:, None] == grid
    hits = mm_tn(high.astype(b16), low.astype(b16))
    marks = jnp.minimum(hits, 1.0)
    lower = grid < grid.T
    within = mm_nt(marks.astype(b16), lower.astype(b16))
    rows = jnp.sum(marks, axis=1)
    before = jnp.sum(jnp.where(lower, rows[None, :], 0.0), axis=1)
    rank = jnp.where(marks > 0, within + before[:, None], -1.0).astype(jnp.int32)
    count = jnp.sum(rows).astype(jnp.int32)
    return rank.reshape(1, n), count.reshape(1)


def body(
    tokens,
    ln1_gain,
    ln1_bias,
    qkv_weight,
    out_weight,
    ln2_gain,
    ln2_bias,
    ffn_in,
    ffn_out,
    feature_proj,
    masked_pos,
    masked_count,
    out_grad,
):
    rows_dev = tokens.shape[0]
    n = rows_dev // 4
    hidden = ffn_out.shape[0]
    narrow = ffn_out.shape[1]
    bits = row_bits()
    groups = len(chunks_of_bits())
    me = lax.axis_index("heads").astype(jnp.int32).reshape(1)

    x_cut = side_rows(tokens)
    x_side = swap(x_cut, heads=2)
    shard = jnp.concatenate([tie(qkv_weight, x_cut).transpose(2, 0, 1).reshape(narrow, -1), out_weight.T], axis=1)
    shard = widen_high(shard, 0)
    gains = tie(jnp.stack([ln1_gain, ln1_bias, ln2_gain, ln2_bias]), x_cut)
    first = gains.astype(b16)
    left = gains - first.astype(f32)
    second = left.astype(b16)
    third = (left - second.astype(f32)).astype(b16)
    gains = jnp.concatenate([first, second, third, jnp.zeros((4, PAIR), b16)], axis=0)
    both = jnp.concatenate([tie(ffn_in, x_cut).T, ffn_out.T], axis=1)
    both = jnp.concatenate([both, jnp.pad(gains, ((0, 0), (0, both.shape[1] - PAIR)))], axis=0)
    both = widen_bit(tie(both, x_side), "heads", 1, 0)
    fin, fo, gains_own = both[:, :narrow, :hidden], both[:, :narrow, hidden:], both[:, narrow:, :PAIR]
    gains_other = lax.dynamic_index_in_dim(gains_own, 1 - bit_of("heads", 1), 0, keepdims=False)
    near = jnp.concatenate([near_rows(tokens, x_side), jnp.stack([gains, tie(gains_other, x_side)])], axis=1)
    x_near = swap(near, heads=1)
    attn_own = widen_square(shard, (x_side,))
    fo = widen_bit(fo, "rows", 0, 1, (x_near,))
    for step in range(bits - 1):
        fin = widen_bit(fin, "rows", bits - 1 - step, 1 + step, ((x_near,), (attn_own,))[step > 0])
    attn_sib = swap(attn_own, heads=1)
    x, a, norms = call(
        norm_kernel, "norm", [shape((n, D)), shape((n, D)), shape((4, D), f32)], [], 1,
        [me, tokens, x_side, x_near, gains_own], smem=(0,),
    )
    dy_cut = side_rows(tie(out_grad, shard))
    rank_row, count = mask_ranks(tie(masked_pos, shard), masked_count, rows_dev, n)
    zero = jnp.zeros_like(feature_proj)
    dirs = tie(feature_proj, shard)
    dirs = jnp.concatenate([jnp.concatenate([dirs, zero], 1), jnp.concatenate([zero, dirs], 1)], 0)
    dirs = tie(dirs, rank_row, count, dy_cut)

    k, v, phi_k, kv_own, kv_sib = call(
        keys_kernel, "keys",
        [shape((n, D)), shape((n, D)), shape((n, 4 * D)), shape((2, PACK, D)), shape((2, PACK, D))],
        [pltpu.VMEM((4, PAIR, D), f32), pltpu.VMEM((4, 8, D), f32)],
        4, [a, attn_own, attn_sib, dirs],
    )
    (phi_q,) = call(
        queries_kernel, "queries", [shape((n, 4 * D))], [], 3, [tie(a, kv_own), attn_own, attn_sib, dirs],
    )
    fin_own = widen_bit(fin, "rows", 0, bits, (kv_own,)).reshape(2, D, hidden)
    kv_total = kv_own.astype(f32) + swap(kv_sib, heads=1).astype(f32)
    kv_first = kv_own
    kv_own, kv_sib = spread_sum(kv_total, (phi_q,))
    for step in range(bits - 1):
        fo = widen_bit(fo, "rows", bits - 1 - step, 1 + step, ((kv_first,), (kv_own,))[step > 0])
    fo_own = fo.reshape(2, D, hidden)
    fin_sib = swap(fin_own, heads=1)
    fo_sib = swap(fo_own, heads=1)
    high, low = call(
        attention_kernel, "attention", [shape((n, D)), shape((n, D))],
        [pltpu.VMEM((4, 256, D), b16), pltpu.VMEM((D, D), b16)],
        2, [x, phi_q, kv_own, kv_sib, attn_own, attn_sib],
    )
    dy_side = tie(swap(tie(dy_cut, attn_own), heads=2), phi_q)
    dy_near = swap(near_rows(out_grad, dy_side), heads=1)
    ino_keep, ino_send, foq_keep, foq_send, dkv_own, dkv_sib, dh, da, norm_two = call(
        masked_kernel, "masked",
        [shape((2, D, hidden + PAIR))] * 4 + [
         shape((2, PACK, D)), shape((2, PACK, D)), shape((n, D)), shape((n, D)), shape((16, D), f32)],
        [pltpu.VMEM((n, D), b16), pltpu.VMEM((4, 256, D), b16), pltpu.VMEM((D, D), b16),
         pltpu.VMEM((4, D, hidden), b16), pltpu.VMEM((4, D, hidden), b16), pltpu.VMEM((4, D, PAIR), b16),
         pltpu.VMEM((4, D, hidden + PAIR), b16), pltpu.VMEM((4, D, hidden + PAIR), b16),
         pltpu.VMEM((4, 256, D), f32), pltpu.VMEM((MASK_TILE, D), f32), pltpu.VMEM((4, MASK_TILE, PAIR), f32)],
        18,
        [me, count, rank_row, high, low, a, out_grad, dy_side, dy_near, norms, fin_own, fin_sib, fo_own, fo_sib,
         attn_own, attn_sib, kv_own, kv_sib, dirs],
        smem=(0, 1), vmem=26,
    )

    dkv_total = dkv_own.astype(f32) + swap(dkv_sib, heads=1).astype(f32)
    blocks = (2,) * (1 + bits) + (narrow, hidden + PAIR)
    gino = add_low(ino_keep, swap(tie(ino_send, dkv_total), heads=1)).reshape(blocks)
    gfoq = add_low(foq_keep, swap(tie(foq_send, dkv_total), heads=1)).reshape(blocks)
    dkv_own, dkv_sib = spread_sum(dkv_total, (gino, gfoq))
    i_own, i_near, i_far, rows_grad, norm_sums = call(
        inputs_kernel, "inputs",
        [shape((n, PAIR)), shape((2, n, PAIR)), shape((n, PAIR)), shape((n, 2 * D)), shape((8, D // 2), f32)],
        [pltpu.VMEM((4, 256, D), b16), pltpu.VMEM((n, D), b16), pltpu.VMEM((16, D), f32)],
        6,
        [me, tie(x, gino, gfoq), k, v, phi_k, dh, da, dkv_own, dkv_sib, norms, attn_own, attn_sib, dirs, norm_two],
        smem=(0,),
    )
    keep, send = call(
        weights_kernel, "weights",
        [shape((2 * D, 2 * PAIR), f32), shape((2 * D + 16, 2 * PAIR))], [],
        1.3, [a, rows_grad, norm_sums],
    )
    i_near = swap(i_near, heads=1)
    total, norm_sums = add_sibling(keep, send, norm_sums)
    gino = halve(gino, "rows", 0, bits, (send,))
    gfoq = halve(gfoq, "heads", 1, 0, (send,))
    i_side = swap(tie(jnp.stack([i_far, i_near[1]]), total), heads=2)
    m_own, m_near, m_far = call(
        forward_kernel, "forward", [shape((n, PAIR)), shape((2, n, PAIR)), shape((n, PAIR))],
        [pltpu.VMEM((n, D), b16), pltpu.VMEM((FORWARD_TILE, D), b16), pltpu.VMEM((FORWARD_TILE, D), f32)], 6,
        [me, tie(high, total, gino, gfoq), low, norms, fin_own, fin_sib, fo_own, fo_sib], smem=(0,),
    )

    total, norm_sums = sum_stage(total, norm_sums, "rows", 0, bits, (m_own,))
    gino = halve(gino, "rows", 1, bits - 1, (m_own,))
    gfoq = halve(gfoq, "rows", 0, bits - 1, (m_own,))
    total, norm_sums, gino, gfoq, m_near = lax.optimization_barrier((total, norm_sums, gino, gfoq, m_near))
    m_near = swap(m_near, heads=1)
    total, norm_sums = sum_stage(total, norm_sums, "heads", 1, 0)
    for step in range(2, bits):
        gino = halve(gino, "rows", step, bits - step)
    gfoq = halve(gfoq, "rows", 1, bits - 2)
    total, norm_sums, gino, gfoq, m_near, i_side = lax.optimization_barrier(
        (total, norm_sums, gino, gfoq, m_near, i_side)
    )
    m_side = swap(jnp.stack([m_far, m_near[1]]), heads=2)
    gino = halve(gino, "heads", 1, 0)
    for step in range(2, bits):
        gfoq = halve(gfoq, "rows", step, bits - 1 - step)
    for step in range(1, bits):
        total, norm_sums = sum_stage(total, norm_sums, "rows", step, bits - 1 - step)
    gkv = total
    mixed_out = join_rows(m_own, m_near, m_side, b16)
    input_grad = join_rows(i_own, i_near, i_side, f32)
    head = lax.axis_index("heads")
    mine = lax.dynamic_slice(norm_sums, (4 * (head // 2), PAIR * (head % 2)), (4, PAIR))
    gqkv = jnp.stack([gfoq[:, hidden:].T.astype(f32), gkv[:, :PAIR].T, gkv[:, PAIR:].T])

    return (
        mixed_out,
        input_grad,
        gqkv,
        gino[:, hidden:].T.astype(f32),
        gino[:, :hidden].T.astype(f32),
        gfoq[:, :hidden].T.astype(f32),
        mine[0],
        mine[1],
        mine[2],
        mine[3],
    )


def solution(mesh):
    in_specs = (
        P("rows", "heads"),
        P("heads"),
        P("heads"),
        P(None, "heads", "rows"),
        P("heads", "rows"),
        P("heads"),
        P("heads"),
        P("heads", "rows"),
        P("heads", "rows"),
        P(),
        P(),
        P(),
        P("rows", "heads"),
    )
    out_specs = (
        P("rows", "heads"),
        P("rows", "heads"),
        P(None, "heads", "rows"),
        P("heads", "rows"),
        P("heads", "rows"),
        P("heads", "rows"),
        P("heads"),
        P("heads"),
        P("heads"),
        P("heads"),
    )
    return jax.shard_map(body, mesh=mesh, in_specs=in_specs, out_specs=out_specs, check_vma=False)
```

```python
import math

import jax
import jax.numpy as jnp
from jax import lax
from jax.experimental import pallas as pl
from jax.experimental.pallas import tpu as pltpu
from jax.sharding import PartitionSpec as P

D = 512
HEAD_DIM = 64
FEATS = 256
PAIR = 2 * HEAD_DIM
SPAN = 2
PACK = 80
SCALE = HEAD_DIM ** (-0.25)
HALF_SQ = 0.5 * SCALE * SCALE
LOG2E = math.log2(math.e)
LOG2_ROOT = 0.5 * math.log2(FEATS)
epsilon = 1e-05
f32 = jnp.float32
b16 = jnp.bfloat16
MIB = 1024 * 1024
TILE = 1024
FORWARD_TILE = 512
MASK_TILE = 304
US = 1.15e9


def mm(left, right):
    return lax.dot_general(left, right, (((1,), (0,)), ((), ())), preferred_element_type=f32)


def mm_nt(left, right):
    return lax.dot_general(left, right, (((1,), (1,)), ((), ())), preferred_element_type=f32)


def mm_tn(left, right):
    return lax.dot_general(left, right, (((0,), (0,)), ((), ())), preferred_element_type=f32)


def layer_stats(values):
    mean = jnp.sum(values, axis=1, keepdims=True) * (1.0 / D)
    centred = values - mean
    var = jnp.sum(centred * centred, axis=1, keepdims=True) * (1.0 / D)
    scale = lax.rsqrt(var + epsilon)
    return centred * scale, scale


def layer_back(grad, normed, scale, gain):
    scaled = grad * gain
    first = jnp.sum(scaled, axis=1, keepdims=True) * (1.0 / D)
    second = jnp.sum(scaled * normed, axis=1, keepdims=True) * (1.0 / D)
    return scale * (scaled - first - normed * second)


def features(rows, directions):
    projected = mm(rows, directions)
    wide = rows.astype(f32)
    square = wide * wide
    first = lax.broadcasted_iota(jnp.int32, square.shape, 1) < HEAD_DIM
    left = jnp.sum(jnp.where(first, square, 0.0), axis=1, keepdims=True)
    right = jnp.sum(jnp.where(first, 0.0, square), axis=1, keepdims=True)
    return jnp.concatenate(
        [
            jnp.exp2((SCALE * LOG2E) * projected[:, :FEATS] - (HALF_SQ * LOG2E * left + LOG2_ROOT)),
            jnp.exp2((SCALE * LOG2E) * projected[:, FEATS:] - (HALF_SQ * LOG2E * right + LOG2_ROOT)),
        ],
        axis=1,
    )


def normal_cdf(u):
    return 0.5 + 0.5 * lax.erf(u * math.sqrt(0.5))


def summary_matrix(packed, blk):
    half = packed[blk]
    zero = jnp.zeros((HEAD_DIM, FEATS), b16)
    top = jnp.concatenate([half[:HEAD_DIM, :FEATS], zero], axis=1)
    low = jnp.concatenate([zero, half[:HEAD_DIM, FEATS:]], axis=1)
    sums = half[HEAD_DIM : HEAD_DIM + 1].astype(f32)
    rows = jnp.broadcast_to(sums, (HEAD_DIM, 2 * FEATS))
    left = lax.broadcasted_iota(jnp.int32, rows.shape, 1) < FEATS
    return jnp.concatenate(
        [
            top,
            low,
            jnp.where(left, rows, 0.0).astype(b16),
            jnp.where(left, 0.0, rows).astype(b16),
        ],
        axis=0,
    )


def pack_summary(matrix, sums):
    kept = jnp.concatenate([matrix[:HEAD_DIM, :FEATS], matrix[HEAD_DIM:PAIR, FEATS:]], axis=1)
    return jnp.concatenate(
        [kept.astype(b16), jnp.broadcast_to(sums, (PACK - HEAD_DIM, 2 * FEATS)).astype(b16)], axis=0
    )


def block_of(own, sib, blk):
    return own[blk] if blk < 2 else sib[blk - 2]


def gather_columns(block, side, near, target, me):
    n = target.shape[0]
    parts = (
        block[pl.ds(pl.multiple_of(me * n, n), n), :],
        near[0, :n, :],
        side[pl.ds(pl.multiple_of((me & 1) * n, n), n), :],
        near[1, :n, :],
    )
    for j in range(4):
        target[:, pl.ds(pl.multiple_of((me ^ j) * PAIR, PAIR), PAIR)] = parts[j]


def spread_columns(source, own, near, far, me):
    def columns(j):
        return source[:, pl.ds(pl.multiple_of((me ^ j) * PAIR, PAIR), PAIR)]

    own[...] = columns(0)
    near[0] = columns(1)
    near[1] = columns(3)
    far[...] = columns(2)


def norm_kernel(me_ref, block, side, near, gains, gains_side, gains_near, x_ref, a_ref, norm_ref):
    gather_columns(block, side, near, x_ref, me_ref[0])
    for j, part in enumerate((gains[...], gains_near[0], gains_side[...], gains_near[1])):
        norm_ref[:, pl.ds(pl.multiple_of((me_ref[0] ^ j) * PAIR, PAIR), PAIR)] = part

    def step(i, carry):
        rows = pl.ds(pl.multiple_of(i * TILE, TILE), TILE)
        normed, _ = layer_stats(x_ref[rows, :].astype(f32))
        a_ref[rows, :] = (normed * norm_ref[0:1, :] + norm_ref[1:2, :]).astype(b16)
        return carry

    lax.fori_loop(0, x_ref.shape[0] // TILE, step, 0)


def keys_kernel(a_ref, own, sib, dirs, k_ref, v_ref, phi_ref, pack_own, pack_sib, w_ref, acc, sums):
    for blk in range(4):
        w_ref[blk] = block_of(own, sib, blk)
    acc[...] = jnp.zeros_like(acc)
    sums[...] = jnp.zeros_like(sums)

    def step(i, carry):
        rows = pl.ds(pl.multiple_of(i * TILE, TILE), TILE)
        a = a_ref[rows, :]
        for blk in range(4):
            kv = mm(a, w_ref[blk, :, PAIR : 3 * PAIR]).astype(b16)
            k, v = kv[:, :PAIR], kv[:, PAIR:]
            k_ref[rows, blk * PAIR : (blk + 1) * PAIR] = k
            v_ref[rows, blk * PAIR : (blk + 1) * PAIR] = v
            phi = features(k, dirs[...]).astype(b16)
            phi_ref[rows, blk * 2 * FEATS : (blk + 1) * 2 * FEATS] = phi
            acc[blk] += mm_tn(v, phi)
            sums[blk] += jnp.sum(phi.astype(f32).reshape(TILE // 8, 8, 2 * FEATS), axis=0)
        return carry

    lax.fori_loop(0, a_ref.shape[0] // TILE, step, 0)
    for blk in range(4):
        packed = pack_summary(acc[blk], jnp.sum(sums[blk], axis=0, keepdims=True))
        (pack_own if blk < 2 else pack_sib)[blk % 2] = packed


def queries_kernel(a_ref, w_ref, dirs, phi_ref):
    def step(i, carry):
        rows = pl.ds(pl.multiple_of(i * TILE, TILE), TILE)
        a = a_ref[rows, :]
        for blk in range(4):
            q = mm(a, w_ref[blk, :, :PAIR]).astype(b16)
            phi_ref[rows, blk * 2 * FEATS : (blk + 1) * 2 * FEATS] = features(q, dirs[...]).astype(b16)
        return carry

    lax.fori_loop(0, a_ref.shape[0] // TILE, step, 0)


def attention_kernel(x_ref, phi_ref, pack_own, pack_sib, w_ref, hi_ref, lo_ref, summ, wout):
    for blk in range(4):
        summ[blk] = summary_matrix(pack_own if blk < 2 else pack_sib, blk % 2)
        wout[:, blk * PAIR : (blk + 1) * PAIR] = w_ref[blk, :, 3 * PAIR :]

    def step(i, carry):
        rows = pl.ds(pl.multiple_of(i * TILE, TILE), TILE)
        heads = []
        for blk in range(4):
            both = mm_nt(phi_ref[rows, blk * 2 * FEATS : (blk + 1) * 2 * FEATS], summ[blk])
            heads.append((both[:, :PAIR] / both[:, PAIR:]).astype(b16))
        hidden = x_ref[rows, :].astype(f32) + mm_nt(jnp.concatenate(heads, axis=1), wout[...])
        high = hidden.astype(b16)
        hi_ref[rows, :] = high
        lo_ref[rows, :] = (hidden - high.astype(f32)).astype(b16)
        return carry

    lax.fori_loop(0, x_ref.shape[0] // TILE, step, 0)


def forward_kernel(me_ref, hi_ref, lo_ref, norm_ref, in_own, in_sib, out_own, out_sib, m_own, m_near, m_far, mixed,
                   low_ref, sum_ref):
    def step(i, carry):
        rows = pl.ds(pl.multiple_of(i * FORWARD_TILE, FORWARD_TILE), FORWARD_TILE)
        hidden = hi_ref[rows, :].astype(f32) + lo_ref[rows, :].astype(f32)
        normed, _ = layer_stats(hidden)
        low_ref[...] = (normed * norm_ref[2:3, :] + norm_ref[3:4, :]).astype(b16)
        sum_ref[...] = hidden
        for w_in, w_out in ((in_own, out_own), (in_sib, out_sib)):

            def block(blk, carry, w_in=w_in, w_out=w_out):
                u = mm(low_ref[...], w_in[blk])
                g = (u * normal_cdf(u)).astype(b16)
                sum_ref[...] += mm_nt(g, w_out[blk])
                return carry

            lax.fori_loop(0, 2, block, 0)
        mixed[rows, :] = sum_ref[...].astype(b16)
        return carry

    lax.fori_loop(0, hi_ref.shape[0] // FORWARD_TILE, step, 0)
    spread_columns(mixed, m_own, m_near, m_far, me_ref[0])


def masked_kernel(me_ref, count_ref, rank_row, hi_ref, lo_ref, a_ref, dy_block, dy_side, dy_near, norm_ref,
                  in_own, in_sib, fo_own, fo_sib, w_ref, pack_own, pack_sib, dirs,
                  ino_keep, ino_send, foq_keep, foq_send, dpack_own, dpack_sib, dh_ref, da_ref, norm_grad,
                  dy_ref, summ, wout, w_in, w_fo, ino, foq, acc_kv, dc_ref, dmix_ref):
    hidden = fo_own.shape[2]
    total = rank_row.shape[1]
    gather_columns(dy_block, dy_side, dy_near, dy_ref, me_ref[0])
    for blk in range(4):
        summ[blk] = summary_matrix(pack_own if blk < 2 else pack_sib, blk % 2)
        wout[:, blk * PAIR : (blk + 1) * PAIR] = w_ref[blk, :, 3 * PAIR :]
        w_in[blk] = block_of(in_own, in_sib, blk)
        w_fo[blk] = block_of(fo_own, fo_sib, blk)
    gain = norm_ref[2:3, :]

    def step(tile, carry):
        def put(ref, at, value):
            before = jnp.where(tile > 0, ref[at].astype(f32), 0.0)
            ref[at] = (before + value).astype(ref.dtype)

        base = tile * MASK_TILE
        slots = base + lax.broadcasted_iota(jnp.int32, (MASK_TILE, total), 0)
        pick = jnp.where(rank_row[...] == slots, 1.0, 0.0).astype(b16)
        h_m = mm(pick, hi_ref[...]) + mm(pick, lo_ref[...])
        a_m = mm(pick, a_ref[...]).astype(b16)
        dy = mm(pick, dy_ref[...])
        dy_low = dy.astype(b16)
        normed, scale = layer_stats(h_m)
        c = (normed * gain + norm_ref[3:4, :]).astype(b16)
        dc_ref[...] = jnp.zeros_like(dc_ref)

        def hidden_block(blk, carry):
            u = mm(c, w_in[blk])
            phi = normal_cdf(u)
            g = (u * phi).astype(b16)
            slope = phi + u * (jnp.exp(-0.5 * u * u) * (1.0 / math.sqrt(2.0 * math.pi)))
            du = (mm(dy_low, w_fo[blk]) * slope).astype(b16)
            dc_ref[...] += mm_nt(du, w_in[blk])
            put(foq, (blk, slice(None), slice(0, hidden)), mm_tn(dy_low, g))
            put(ino, (blk, slice(None), slice(0, hidden)), mm_tn(c, du))
            return carry

        lax.fori_loop(0, 4, hidden_block, 0)
        dc = dc_ref[...]
        put(norm_grad, slice(0, 8), jnp.sum((dc * normed).reshape(MASK_TILE // 8, 8, D), axis=0))
        put(norm_grad, slice(8, 16), jnp.sum(dc.reshape(MASK_TILE // 8, 8, D), axis=0))
        dh = dy + layer_back(dc, normed, scale, gain)
        dattn = dh.astype(b16)
        dmix = mm(dattn, wout[...])
        for blk in range(4):
            dmix_ref[blk] = dmix[:, blk * PAIR : (blk + 1) * PAIR]
        dc_ref[...] = jnp.zeros_like(dc_ref)

        def head_block(blk, carry):
            q = mm(a_m, w_ref[blk, :, :PAIR]).astype(b16)
            eq = features(q, dirs[...])
            phi_q = eq.astype(b16)
            both = mm_nt(phi_q, summ[blk])
            num, den = both[:, :PAIR], both[:, PAIR:]
            inverse = 1.0 / den
            o = (num * inverse).astype(b16)
            put(ino, (blk, slice(None), slice(hidden, hidden + PAIR)), mm_tn(dattn, o))
            do = dmix_ref[blk]
            dnum = (do * inverse).astype(b16)
            prod = do * num
            first = lax.broadcasted_iota(jnp.int32, prod.shape, 1) < HEAD_DIM
            left = jnp.sum(jnp.where(first, prod, 0.0), axis=1, keepdims=True)
            right = jnp.sum(jnp.where(first, 0.0, prod), axis=1, keepdims=True)
            dden = (-jnp.where(first, left, right) * inverse * inverse).astype(b16)
            ext = jnp.concatenate([dnum, (dden.astype(f32) * (1.0 / HEAD_DIM)).astype(b16)], axis=1)
            put(acc_kv, blk, mm_tn(ext, phi_q))
            d_exp = mm(ext, summ[blk]) * eq
            dp = (SCALE * d_exp).astype(b16)
            lin = mm_nt(dp, dirs[...])
            left = jnp.sum(d_exp[:, :FEATS], axis=1, keepdims=True)
            right = jnp.sum(d_exp[:, FEATS:], axis=1, keepdims=True)
            dq = (lin - (SCALE * SCALE) * q.astype(f32) * jnp.where(first, left, right)).astype(b16)
            put(foq, (blk, slice(None), slice(hidden, hidden + PAIR)), mm_tn(a_m, dq))
            dc_ref[...] += mm_nt(dq, w_ref[blk, :, :PAIR])
            return carry

        lax.fori_loop(0, 4, head_block, 0)
        put(dh_ref, slice(None), mm_tn(pick, dattn))
        put(da_ref, slice(None), mm_tn(pick, dc_ref[...].astype(b16)))
        return carry

    lax.fori_loop(0, jnp.maximum((count_ref[0] + MASK_TILE - 1) // MASK_TILE, 1), step, 0)
    for blk in range(4):
        sums = jnp.concatenate(
            [acc_kv[blk, PAIR : PAIR + 1, :FEATS], acc_kv[blk, PAIR + HEAD_DIM : PAIR + HEAD_DIM + 1, FEATS:]],
            axis=1,
        ) * float(HEAD_DIM)
        (dpack_own if blk < 2 else dpack_sib)[blk % 2] = pack_summary(acc_kv[blk, :PAIR], sums)
        (ino_keep if blk < 2 else ino_send)[blk % 2] = ino[blk]
        (foq_keep if blk < 2 else foq_send)[blk % 2] = foq[blk]


def inputs_kernel(me_ref, x_ref, k_ref, v_ref, phi_ref, dh_ref, da_ref, pack_own, pack_sib,
                  norm_ref, w_ref, dirs, norm_two,
                  i_own, i_near, i_far, rows_grad, norm_sums, summ, mixed, norm_grad):
    for blk in range(4):
        summ[blk] = summary_matrix(pack_own if blk < 2 else pack_sib, blk % 2)
    norm_grad[...] = jnp.zeros_like(norm_grad)
    wide = 2 * PAIR
    gain = norm_ref[0:1, :]

    def step(i, carry):
        rows = pl.ds(pl.multiple_of(i * TILE, TILE), TILE)
        da = da_ref[rows, :].astype(f32)
        for blk in range(4):
            cols = slice(blk * PAIR, (blk + 1) * PAIR)
            v = v_ref[rows, cols]
            ext = jnp.concatenate([v, jnp.full(v.shape, 1.0 / HEAD_DIM, b16)], axis=1)
            phi = phi_ref[rows, blk * 2 * FEATS : (blk + 1) * 2 * FEATS]
            d_exp = mm(ext, summ[blk]) * phi.astype(f32)
            dp = (SCALE * d_exp).astype(b16)
            lin = mm_nt(dp, dirs[...])
            left = jnp.sum(d_exp[:, :FEATS], axis=1, keepdims=True)
            right = jnp.sum(d_exp[:, FEATS:], axis=1, keepdims=True)
            first = lax.broadcasted_iota(jnp.int32, lin.shape, 1) < HEAD_DIM
            k = k_ref[rows, cols].astype(f32)
            dk = (lin - (SCALE * SCALE) * k * jnp.where(first, left, right)).astype(b16)
            dv = mm_nt(phi, summ[blk, :PAIR, :]).astype(b16)
            grads = jnp.concatenate([dk, dv], axis=1)
            rows_grad[rows, blk * wide : (blk + 1) * wide] = grads
            da = da + mm_nt(grads, w_ref[blk, :, PAIR : 3 * PAIR])
        normed, scale = layer_stats(x_ref[rows, :].astype(f32))
        norm_grad[0:8, :] += jnp.sum((da * normed).reshape(TILE // 8, 8, D), axis=0)
        norm_grad[8:16, :] += jnp.sum(da.reshape(TILE // 8, 8, D), axis=0)
        grad = dh_ref[rows, :].astype(f32) + layer_back(da, normed, scale, gain)
        mixed[rows, :] = grad.astype(b16)
        return carry

    lax.fori_loop(0, x_ref.shape[0] // TILE, step, 0)
    spread_columns(mixed, i_own, i_near, i_far, me_ref[0])
    for i in range(4):
        source = norm_grad if i < 2 else norm_two
        row = jnp.sum(source[i % 2 * 8 : i % 2 * 8 + 8, :], axis=0, keepdims=True)
        norm_sums[i : i + 1, :] = row[:, : D // 2]
        norm_sums[4 + i : 5 + i, :] = row[:, D // 2 :]


def weights_kernel(a_ref, rows_grad, norm_sums, keep, send):
    wide = 2 * PAIR
    for blk in (2, 3, 0, 1):
        grad = mm_tn(a_ref[...], rows_grad[:, blk * wide : (blk + 1) * wide])
        if blk < 2:
            keep[blk * D : (blk + 1) * D] = grad
        else:
            send[(blk - 2) * D : (blk - 1) * D] = grad.astype(b16)
    send[2 * D :] = two_parts(norm_sums[...])


def coarse(values):
    return lax.reduce_precision(values, exponent_bits=8, mantissa_bits=7)


def two_parts(values):
    high = values.astype(b16)
    return jnp.concatenate([high, (values - high.astype(f32)).astype(b16)], axis=0)


def call(kernel, name, outs, scratch, micros, args, smem=(), vmem=20):
    specs = [
        pl.BlockSpec(memory_space=pltpu.SMEM if i in smem else pltpu.VMEM) for i in range(len(args))
    ]
    return pl.pallas_call(
        kernel,
        name=name,
        out_shape=outs,
        in_specs=specs,
        out_specs=[pl.BlockSpec(memory_space=pltpu.VMEM)] * len(outs),
        scratch_shapes=scratch,
        compiler_params=pltpu.CompilerParams(vmem_limit_bytes=vmem * MIB),
        cost_estimate=pl.CostEstimate(flops=int(micros * US), bytes_accessed=1_000, transcendentals=0),
    )(*args)


def shape(dims, dtype=b16):
    return jax.ShapeDtypeStruct(dims, dtype)


def swap(block, rows=0, heads=0):
    count = lax.axis_size("heads")
    if rows == 0:
        return lax.ppermute(block, "heads", [(i, i ^ heads) for i in range(count)])
    total = lax.axis_size("rows")
    if heads == 0:
        return lax.ppermute(block, "rows", [(i, i ^ rows) for i in range(total)])
    pairs = [
        (r * count + h, (r ^ rows) * count + (h ^ heads)) for r in range(total) for h in range(count)
    ]
    return lax.ppermute(block, ("rows", "heads"), pairs)


def bit_of(axis, bit):
    return (lax.axis_index(axis) >> bit) & 1


def sort_blocks(blocks, low_bits):
    blocks = list(blocks)
    for i, low in enumerate(low_bits):
        for d in range(len(blocks)):
            if d >> i & 1 == 0:
                one, two = blocks[d], blocks[d | 1 << i]
                blocks[d] = jnp.where(low, one, two)
                blocks[d | 1 << i] = jnp.where(low, two, one)
    return blocks


def tie(value, *others):
    return lax.optimization_barrier((value,) + others)[0]


def row_bits():
    return lax.axis_size("rows").bit_length() - 1


def chunks_of_bits():
    high = row_bits()
    groups = []
    while high > 1:
        width = min(2, high - 1)
        high -= width
        groups.append((high, width))
    return groups


def widen_bit(block, axis, bit, at, after=()):
    other = swap(block, rows=1 << bit) if axis == "rows" else swap(block, heads=1 << bit)
    other = tie(other, *after)
    return jnp.stack(sort_blocks([block, other], [bit_of(axis, bit) == 0]), axis=at)


def widen_high(block, at, after=()):
    for low, width in chunks_of_bits():
        got = [block] + [tie(swap(block, rows=d << low), *after) for d in range(1, 1 << width)]
        lows = [bit_of("rows", low + i) == 0 for i in range(width)]
        block = jnp.stack(sort_blocks(got, lows), axis=at)
        at += 1
    return block


def widen_square(block):
    got = [block, swap(block, rows=1), swap(block, heads=2), swap(block, rows=1, heads=2)]
    got = sort_blocks(got, [bit_of("rows", 0) == 0, bit_of("heads", 1) == 0])
    at = block.ndim - 2
    sides = [jnp.stack(got[:2], axis=at), jnp.stack(got[2:], axis=at)]
    return jnp.stack(sides).reshape(2, D, block.shape[-1])


def split_half(total, axis, bit, at):
    mine = bit_of(axis, bit)
    return (lax.dynamic_index_in_dim(total, mine, at, keepdims=False),
            lax.dynamic_index_in_dim(total, 1 - mine, at, keepdims=False))


def halve(total, axis, bit, at, after=()):
    here, away = split_half(total, axis, bit, at)
    other = swap(away, rows=1 << bit) if axis == "rows" else swap(away, heads=1 << bit)
    return add_low(here, tie(other, *after))


def add_low(one, two):
    return (one.astype(f32) + two.astype(f32)).astype(b16)


def spread_sum(total, beside):
    sent = total.astype(b16)
    got = [tie(swap(sent, rows=rows, heads=heads), *beside) for rows, heads in ((1, 0), (0, 2), (1, 2))]
    for block in got:
        total = total + block.astype(f32)
    total = total.astype(b16)
    return total, swap(total, heads=1)


def add_parts(sums, got):
    tail = sums.shape[0]
    return sums + (got[-2 * tail : -tail].astype(f32) + got[-tail:].astype(f32))


def add_sibling(keep, send, sums):
    got = swap(send, heads=1)
    total = keep + got[: -2 * sums.shape[0]].astype(f32)
    return total.reshape((2,) * (1 + row_bits()) + (D >> row_bits(), keep.shape[1])), add_parts(sums, got)


def sum_stage(total, sums, axis, bit, at, after=()):
    wide = total.shape[-1]
    mine = bit_of(axis, bit)
    away = lax.dynamic_index_in_dim(total, 1 - mine, at, keepdims=False).astype(b16).reshape(-1, wide)
    total = lax.dynamic_index_in_dim(total, mine, at, keepdims=False)
    high = coarse(sums)
    away = jnp.concatenate([away, high.astype(b16), (sums - high).astype(b16)], axis=0)
    got = tie(swap(away, rows=1 << bit) if axis == "rows" else swap(away, heads=1 << bit), *after)
    total = total + got[: -2 * sums.shape[0]].reshape(total.shape).astype(f32)
    return total, add_parts(sums, got)


def side_rows(block):
    parts = block.reshape(2, block.shape[0] // 2, block.shape[1])
    return lax.dynamic_index_in_dim(parts, 1 - bit_of("heads", 1), 0, keepdims=False)


def near_rows(block, side):
    core = bit_of("heads", 0)
    n = block.shape[0] // 4
    own = lax.dynamic_slice_in_dim(block, (2 * bit_of("heads", 1) + 1 - core) * n, n, 0)
    return jnp.stack([own, lax.dynamic_slice_in_dim(side, (1 - core) * n, n, 0)])


def join_rows(own, near, side, dtype):
    got = sort_blocks([own, near[0], side[0], side[1]], [bit_of("heads", 0) == 0, bit_of("heads", 1) == 0])
    return jnp.concatenate(got, axis=0).astype(dtype)


def mask_ranks(masked_pos, masked_count, rows_dev, n):
    group = lax.axis_index("rows")
    offset = group % SPAN * rows_dev + lax.axis_index("heads") * n
    place = lax.dynamic_index_in_dim(masked_pos, group // SPAN, 0, keepdims=False) - offset
    limit = lax.dynamic_index_in_dim(masked_count, group // SPAN, 0, keepdims=False)
    inside = (jnp.arange(place.shape[0], dtype=jnp.int32) < limit) & (place >= 0) & (place < n)
    side = 32
    grid = jnp.arange(side, dtype=jnp.int32)[None, :]
    high = ((place // side)[:, None] == grid) & inside[:, None]
    low = (place % side)[:, None] == grid
    hits = mm_tn(high.astype(b16), low.astype(b16))
    marks = jnp.minimum(hits, 1.0)
    lower = grid < grid.T
    within = mm_nt(marks.astype(b16), lower.astype(b16))
    rows = jnp.sum(marks, axis=1)
    before = jnp.sum(jnp.where(lower, rows[None, :], 0.0), axis=1)
    rank = jnp.where(marks > 0, within + before[:, None], -1.0).astype(jnp.int32)
    count = jnp.sum(rows).astype(jnp.int32)
    return rank.reshape(1, n), count.reshape(1)


def body(
    tokens,
    ln1_gain,
    ln1_bias,
    qkv_weight,
    out_weight,
    ln2_gain,
    ln2_bias,
    ffn_in,
    ffn_out,
    feature_proj,
    masked_pos,
    masked_count,
    out_grad,
):
    rows_dev = tokens.shape[0]
    n = rows_dev // 4
    hidden = ffn_out.shape[0]
    narrow = ffn_out.shape[1]
    bits = row_bits()
    groups = len(chunks_of_bits())
    me = lax.axis_index("heads").astype(jnp.int32).reshape(1)

    x_cut = side_rows(tokens)
    x_side = swap(x_cut, heads=2)
    shard = jnp.concatenate([tie(qkv_weight, x_cut).transpose(2, 0, 1).reshape(narrow, -1), out_weight.T], axis=1)
    shard = widen_bit(widen_high(shard, 0), "rows", 0, groups)
    both = jnp.concatenate([tie(ffn_in, x_cut).T, ffn_out.T], axis=1)
    both = widen_bit(both, "heads", 1, 0)
    gains = tie(jnp.stack([ln1_gain, ln1_bias, ln2_gain, ln2_bias]), x_cut)
    gains_side = swap(gains, heads=2)
    x_side, shard, both, gains_side = lax.optimization_barrier((x_side, shard, both, gains_side))

    attn_own = widen_bit(shard, "heads", 1, 0).reshape(2, D, 4 * PAIR)
    fin = widen_high(both[:, :, :hidden], 1)
    fo = widen_bit(both[:, :, hidden:], "rows", 0, 1)
    dy_cut = side_rows(tie(out_grad, x_side))
    rank_row, count = mask_ranks(tie(masked_pos, x_side), masked_count, rows_dev, n)
    zero = jnp.zeros_like(feature_proj)
    dirs = tie(feature_proj, x_side)
    dirs = jnp.concatenate([jnp.concatenate([dirs, zero], 1), jnp.concatenate([zero, dirs], 1)], 0)
    near = near_rows(tokens, x_side)
    attn_own, fin, fo, dirs, dy_cut, rank_row, count, near = lax.optimization_barrier(
        (attn_own, fin, fo, dirs, dy_cut, rank_row, count, near)
    )

    attn_sib = swap(attn_own, heads=1)
    x_near = swap(near, heads=1)
    gains_near = swap(jnp.stack([gains, gains_side]), heads=1)
    x, a, norms = call(
        norm_kernel, "norm", [shape((n, D)), shape((n, D)), shape((4, D), f32)], [], 1,
        [me, tokens, x_side, x_near, gains, gains_side, gains_near], smem=(0,),
    )
    k, v, phi_k, kv_own, kv_sib, w_attn = call(
        keys_kernel, "keys",
        [shape((n, D)), shape((n, D)), shape((n, 4 * D)), shape((2, PACK, D)), shape((2, PACK, D)),
         shape((4, D, 4 * PAIR))],
        [pltpu.VMEM((4, PAIR, D), f32), pltpu.VMEM((4, 8, D), f32)],
        4, [a, attn_own, attn_sib, dirs],
    )
    fin_own = widen_bit(fin, "rows", 0, 1 + groups, (k,)).reshape(2, D, hidden)
    fo = widen_bit(fo, "rows", bits - 1, 1, (k,))
    dy_side = tie(swap(dy_cut, heads=2), k)
    kv_total = kv_own.astype(f32) + swap(kv_sib, heads=1).astype(f32)
    kv_total, fin_own, fo, dy_side = lax.optimization_barrier((kv_total, fin_own, fo, dy_side))

    (phi_q,) = call(
        queries_kernel, "queries", [shape((n, 4 * D))], [], 3, [tie(a, kv_total), w_attn, dirs],
    )
    for step in range(1, bits - 1):
        fo = widen_bit(fo, "rows", bits - 1 - step, 1 + step, (phi_q,))
    fo_own = fo.reshape(2, D, hidden)
    fin_sib = swap(fin_own, heads=1)
    kv_own, kv_sib = spread_sum(kv_total, (phi_q,))
    high, low = call(
        attention_kernel, "attention", [shape((n, D)), shape((n, D))],
        [pltpu.VMEM((4, 256, D), b16), pltpu.VMEM((D, D), b16)],
        2, [tie(x, fo_own), phi_q, kv_own, kv_sib, w_attn],
    )
    fo_sib = swap(fo_own, heads=1)
    dy_near = swap(near_rows(out_grad, tie(dy_side, kv_own)), heads=1)
    ino_keep, ino_send, foq_keep, foq_send, dkv_own, dkv_sib, dh, da, norm_two = call(
        masked_kernel, "masked",
        [shape((2, D, hidden + PAIR))] * 4 + [
         shape((2, PACK, D)), shape((2, PACK, D)), shape((n, D)), shape((n, D)), shape((16, D), f32)],
        [pltpu.VMEM((n, D), b16), pltpu.VMEM((4, 256, D), b16), pltpu.VMEM((D, D), b16),
         pltpu.VMEM((4, D, hidden), b16), pltpu.VMEM((4, D, hidden), b16),
         pltpu.VMEM((4, D, hidden + PAIR), b16), pltpu.VMEM((4, D, hidden + PAIR), b16),
         pltpu.VMEM((4, 256, D), f32), pltpu.VMEM((MASK_TILE, D), f32), pltpu.VMEM((4, MASK_TILE, PAIR), f32)],
        18,
        [me, count, rank_row, high, low, a, out_grad, dy_side, dy_near, norms, fin_own, fin_sib, fo_own, fo_sib,
         w_attn, kv_own, kv_sib, dirs],
        smem=(0, 1), vmem=26,
    )

    dkv_total = dkv_own.astype(f32) + swap(dkv_sib, heads=1).astype(f32)
    blocks = (2,) * (1 + bits) + (narrow, hidden + PAIR)
    gino = add_low(ino_keep, swap(tie(ino_send, dkv_total), heads=1)).reshape(blocks)
    gfoq = add_low(foq_keep, swap(tie(foq_send, dkv_total), heads=1)).reshape(blocks)
    dkv_own, dkv_sib = spread_sum(dkv_total, (gino, gfoq))
    gino, ino_away = split_half(gino, "rows", 0, bits)
    gfoq, foq_away = split_half(gfoq, "heads", 1, 0)
    i_own, i_near, i_far, rows_grad, norm_sums = call(
        inputs_kernel, "inputs",
        [shape((n, PAIR)), shape((2, n, PAIR)), shape((n, PAIR)), shape((n, 2 * D)), shape((8, D // 2), f32)],
        [pltpu.VMEM((4, 256, D), b16), pltpu.VMEM((n, D), b16), pltpu.VMEM((16, D), f32)],
        6,
        [me, tie(x, gino, gfoq, ino_away, foq_away), k, v, phi_k, dh, da, dkv_own, dkv_sib, norms, w_attn, dirs, norm_two],
        smem=(0,),
    )
    keep, send = call(
        weights_kernel, "weights",
        [shape((2 * D, 2 * PAIR), f32), shape((2 * D + 16, 2 * PAIR))], [],
        1.3, [a, rows_grad, norm_sums],
    )
    i_near = swap(i_near, heads=1)
    total, norm_sums = add_sibling(keep, send, norm_sums)
    gino = add_low(gino, tie(swap(ino_away, rows=1), send))
    gfoq = add_low(gfoq, tie(swap(foq_away, heads=2), send))
    i_side = swap(tie(jnp.stack([i_far, i_near[1]]), total), heads=2)
    m_own, m_near, m_far = call(
        forward_kernel, "forward", [shape((n, PAIR)), shape((2, n, PAIR)), shape((n, PAIR))],
        [pltpu.VMEM((n, D), b16), pltpu.VMEM((FORWARD_TILE, D), b16), pltpu.VMEM((FORWARD_TILE, D), f32)], 6,
        [me, tie(high, total, gino, gfoq), low, norms, fin_own, fin_sib, fo_own, fo_sib], smem=(0,),
    )

    m_near = swap(m_near, heads=1)
    total, norm_sums = sum_stage(total, norm_sums, "heads", 1, 0, (m_own,))
    gino = halve(gino, "rows", 1, bits - 1, (m_own,))
    gfoq = halve(gfoq, "rows", 0, bits - 1, (m_own,))
    total, norm_sums, gino, gfoq, m_near = lax.optimization_barrier((total, norm_sums, gino, gfoq, m_near))
    m_side = swap(jnp.stack([m_far, m_near[1]]), heads=2)
    total, norm_sums = sum_stage(total, norm_sums, "rows", 0, bits - 1)
    for step in range(2, bits):
        gino = halve(gino, "rows", step, bits - step)
    gfoq = halve(gfoq, "rows", 1, bits - 2)
    total, norm_sums, gino, gfoq, i_side = lax.optimization_barrier((total, norm_sums, gino, gfoq, i_side))
    gino = halve(gino, "heads", 1, 0)
    for step in range(2, bits):
        gfoq = halve(gfoq, "rows", step, bits - 1 - step)
    for step in range(1, bits):
        total, norm_sums = sum_stage(total, norm_sums, "rows", step, bits - 1 - step)
    gkv = total
    mixed_out = join_rows(m_own, m_near, m_side, b16)
    input_grad = join_rows(i_own, i_near, i_side, f32)
    head = lax.axis_index("heads")
    mine = lax.dynamic_slice(norm_sums, (4 * (head // 2), PAIR * (head % 2)), (4, PAIR))
    gqkv = jnp.stack([gfoq[:, hidden:].T.astype(f32), gkv[:, :PAIR].T, gkv[:, PAIR:].T])

    return (
        mixed_out,
        input_grad,
        gqkv,
        gino[:, hidden:].T.astype(f32),
        gino[:, :hidden].T.astype(f32),
        gfoq[:, :hidden].T.astype(f32),
        mine[0],
        mine[1],
        mine[2],
        mine[3],
    )


def solution(mesh):
    in_specs = (
        P("rows", "heads"),
        P("heads"),
        P("heads"),
        P(None, "heads", "rows"),
        P("heads", "rows"),
        P("heads"),
        P("heads"),
        P("heads", "rows"),
        P("heads", "rows"),
        P(),
        P(),
        P(),
        P("rows", "heads"),
    )
    out_specs = (
        P("rows", "heads"),
        P("rows", "heads"),
        P(None, "heads", "rows"),
        P("heads", "rows"),
        P("heads", "rows"),
        P("heads", "rows"),
        P("heads"),
        P("heads"),
        P("heads"),
        P("heads"),
    )
    return jax.shard_map(body, mesh=mesh, in_specs=in_specs, out_specs=out_specs, check_vma=False)
```

```python
import functools
import math

import jax
import jax.numpy as jnp
from jax import lax
from jax.experimental import pallas as pl
from jax.experimental.pallas import tpu as pltpu
from jax.sharding import PartitionSpec as P

D = 512
HEAD_DIM = 64
FEATS = 256
PAIR = 2 * HEAD_DIM
SPAN = 2
PACK = 80
SCALE = HEAD_DIM ** (-0.25)
HALF_SQ = 0.5 * SCALE * SCALE
LOG2E = math.log2(math.e)
LOG2_ROOT = 0.5 * math.log2(FEATS)
epsilon = 1e-05
f32 = jnp.float32
b16 = jnp.bfloat16
MIB = 1024 * 1024
TILE = 1024
FORWARD_TILE = 512
MASK_TILE = 304
US = 1.15e9


def mm(left, right):
    return lax.dot_general(left, right, (((1,), (0,)), ((), ())), preferred_element_type=f32)


def mm_nt(left, right):
    return lax.dot_general(left, right, (((1,), (1,)), ((), ())), preferred_element_type=f32)


def mm_tn(left, right):
    return lax.dot_general(left, right, (((0,), (0,)), ((), ())), preferred_element_type=f32)


def layer_stats(values):
    mean = jnp.sum(values, axis=1, keepdims=True) * (1.0 / D)
    centred = values - mean
    var = jnp.sum(centred * centred, axis=1, keepdims=True) * (1.0 / D)
    scale = lax.rsqrt(var + epsilon)
    return centred * scale, scale


def layer_back(grad, normed, scale, gain):
    scaled = grad * gain
    first = jnp.sum(scaled, axis=1, keepdims=True) * (1.0 / D)
    second = jnp.sum(scaled * normed, axis=1, keepdims=True) * (1.0 / D)
    return scale * (scaled - first - normed * second)


def features(rows, directions):
    projected = mm(rows, directions)
    wide = rows.astype(f32)
    square = wide * wide
    first = lax.broadcasted_iota(jnp.int32, square.shape, 1) < HEAD_DIM
    left = jnp.sum(jnp.where(first, square, 0.0), axis=1, keepdims=True)
    right = jnp.sum(jnp.where(first, 0.0, square), axis=1, keepdims=True)
    return jnp.concatenate(
        [
            jnp.exp2((SCALE * LOG2E) * projected[:, :FEATS] - (HALF_SQ * LOG2E * left + LOG2_ROOT)),
            jnp.exp2((SCALE * LOG2E) * projected[:, FEATS:] - (HALF_SQ * LOG2E * right + LOG2_ROOT)),
        ],
        axis=1,
    )


def normal_cdf(u):
    return 0.5 + 0.5 * lax.erf(u * math.sqrt(0.5))


def summary_matrix(packed, blk):
    half = packed[blk]
    zero = jnp.zeros((HEAD_DIM, FEATS), b16)
    top = jnp.concatenate([half[:HEAD_DIM, :FEATS], zero], axis=1)
    low = jnp.concatenate([zero, half[:HEAD_DIM, FEATS:]], axis=1)
    sums = half[HEAD_DIM : HEAD_DIM + 1].astype(f32)
    rows = jnp.broadcast_to(sums, (HEAD_DIM, 2 * FEATS))
    left = lax.broadcasted_iota(jnp.int32, rows.shape, 1) < FEATS
    return jnp.concatenate(
        [
            top,
            low,
            jnp.where(left, rows, 0.0).astype(b16),
            jnp.where(left, 0.0, rows).astype(b16),
        ],
        axis=0,
    )


def pack_summary(matrix, sums):
    kept = jnp.concatenate([matrix[:HEAD_DIM, :FEATS], matrix[HEAD_DIM:PAIR, FEATS:]], axis=1)
    return jnp.concatenate(
        [kept.astype(b16), jnp.broadcast_to(sums, (PACK - HEAD_DIM, 2 * FEATS)).astype(b16)], axis=0
    )


def block_of(own, sib, blk):
    return own[blk] if blk < 2 else sib[blk - 2]


def gather_columns(block, side, near, target, me):
    n = target.shape[0]
    parts = (
        block[pl.ds(pl.multiple_of(me * n, n), n), :],
        near[0, :n, :],
        side[pl.ds(pl.multiple_of((me & 1) * n, n), n), :],
        near[1, :n, :],
    )
    for j in range(4):
        target[:, pl.ds(pl.multiple_of((me ^ j) * PAIR, PAIR), PAIR)] = parts[j]


def spread_columns(source, own, near, far, me):
    def columns(j):
        return source[:, pl.ds(pl.multiple_of((me ^ j) * PAIR, PAIR), PAIR)]

    own[...] = columns(0)
    near[0] = columns(1)
    near[1] = columns(3)
    far[...] = columns(2)


def norm_kernel(me_ref, block, side, near, gains, gains_side, gains_near, x_ref, a_ref, norm_ref):
    gather_columns(block, side, near, x_ref, me_ref[0])
    for j, part in enumerate((gains[...], gains_near[0], gains_side[...], gains_near[1])):
        norm_ref[:, pl.ds(pl.multiple_of((me_ref[0] ^ j) * PAIR, PAIR), PAIR)] = part

    def step(i, carry):
        rows = pl.ds(pl.multiple_of(i * TILE, TILE), TILE)
        normed, _ = layer_stats(x_ref[rows, :].astype(f32))
        a_ref[rows, :] = (normed * norm_ref[0:1, :] + norm_ref[1:2, :]).astype(b16)
        return carry

    lax.fori_loop(0, x_ref.shape[0] // TILE, step, 0)


def keys_kernel(a_ref, own, sib, dirs, k_ref, v_ref, phi_ref, pack_own, pack_sib, w_ref, acc, sums):
    for blk in range(4):
        w_ref[blk] = block_of(own, sib, blk)
    acc[...] = jnp.zeros_like(acc)
    sums[...] = jnp.zeros_like(sums)

    def step(i, carry):
        rows = pl.ds(pl.multiple_of(i * TILE, TILE), TILE)
        a = a_ref[rows, :]
        for blk in range(4):
            kv = mm(a, w_ref[blk, :, PAIR : 3 * PAIR]).astype(b16)
            k, v = kv[:, :PAIR], kv[:, PAIR:]
            k_ref[rows, blk * PAIR : (blk + 1) * PAIR] = k
            v_ref[rows, blk * PAIR : (blk + 1) * PAIR] = v
            phi = features(k, dirs[...]).astype(b16)
            phi_ref[rows, blk * 2 * FEATS : (blk + 1) * 2 * FEATS] = phi
            acc[blk] += mm_tn(v, phi)
            sums[blk] += jnp.sum(phi.astype(f32).reshape(TILE // 8, 8, 2 * FEATS), axis=0)
        return carry

    lax.fori_loop(0, a_ref.shape[0] // TILE, step, 0)
    for blk in range(4):
        packed = pack_summary(acc[blk], jnp.sum(sums[blk], axis=0, keepdims=True))
        (pack_own if blk < 2 else pack_sib)[blk % 2] = packed


def queries_kernel(a_ref, w_ref, dirs, phi_ref):
    def step(i, carry):
        rows = pl.ds(pl.multiple_of(i * TILE, TILE), TILE)
        a = a_ref[rows, :]
        for blk in range(4):
            q = mm(a, w_ref[blk, :, :PAIR]).astype(b16)
            phi_ref[rows, blk * 2 * FEATS : (blk + 1) * 2 * FEATS] = features(q, dirs[...]).astype(b16)
        return carry

    lax.fori_loop(0, a_ref.shape[0] // TILE, step, 0)


def attention_kernel(x_ref, phi_ref, pack_own, pack_sib, w_ref, hi_ref, lo_ref, summ, wout):
    for blk in range(4):
        summ[blk] = summary_matrix(pack_own if blk < 2 else pack_sib, blk % 2)
        wout[:, blk * PAIR : (blk + 1) * PAIR] = w_ref[blk, :, 3 * PAIR :]

    def step(i, carry):
        rows = pl.ds(pl.multiple_of(i * TILE, TILE), TILE)
        heads = []
        for blk in range(4):
            both = mm_nt(phi_ref[rows, blk * 2 * FEATS : (blk + 1) * 2 * FEATS], summ[blk])
            heads.append((both[:, :PAIR] / both[:, PAIR:]).astype(b16))
        hidden = x_ref[rows, :].astype(f32) + mm_nt(jnp.concatenate(heads, axis=1), wout[...])
        high = hidden.astype(b16)
        hi_ref[rows, :] = high
        lo_ref[rows, :] = (hidden - high.astype(f32)).astype(b16)
        return carry

    lax.fori_loop(0, x_ref.shape[0] // TILE, step, 0)


def forward_kernel(me_ref, hi_ref, lo_ref, norm_ref, in_own, in_sib, out_own, out_sib, m_own, m_near, m_far, mixed,
                   low_ref, sum_ref):
    def step(i, carry):
        rows = pl.ds(pl.multiple_of(i * FORWARD_TILE, FORWARD_TILE), FORWARD_TILE)
        hidden = hi_ref[rows, :].astype(f32) + lo_ref[rows, :].astype(f32)
        normed, _ = layer_stats(hidden)
        low_ref[...] = (normed * norm_ref[2:3, :] + norm_ref[3:4, :]).astype(b16)
        sum_ref[...] = hidden
        for w_in, w_out in ((in_own, out_own), (in_sib, out_sib)):

            def block(blk, carry, w_in=w_in, w_out=w_out):
                u = mm(low_ref[...], w_in[blk])
                g = (u * normal_cdf(u)).astype(b16)
                sum_ref[...] += mm_nt(g, w_out[blk])
                return carry

            lax.fori_loop(0, 2, block, 0)
        mixed[rows, :] = sum_ref[...].astype(b16)
        return carry

    lax.fori_loop(0, hi_ref.shape[0] // FORWARD_TILE, step, 0)
    spread_columns(mixed, m_own, m_near, m_far, me_ref[0])


def masked_kernel(me_ref, count_ref, rank_row, hi_ref, lo_ref, x_ref, dy_block, dy_side, dy_near, norm_ref,
                  in_own, in_sib, fo_own, fo_sib, w_ref, pack_own, pack_sib, dirs,
                  ino_keep, ino_send, foq_keep, foq_send, dpack_own, dpack_sib, grad_ref, norm_grad,
                  dy_ref, summ, wout, w_in, w_fo, acc_kv, dc_ref, dmix_ref):
    hidden = fo_own.shape[2]
    total = rank_row.shape[1]
    gather_columns(dy_block, dy_side, dy_near, dy_ref, me_ref[0])
    for blk in range(4):
        summ[blk] = summary_matrix(pack_own if blk < 2 else pack_sib, blk % 2)
        wout[:, blk * PAIR : (blk + 1) * PAIR] = w_ref[blk, :, 3 * PAIR :]
        w_in[blk] = block_of(in_own, in_sib, blk)
        w_fo[blk] = block_of(fo_own, fo_sib, blk)
    gain = norm_ref[2:3, :]

    def step(tile, carry):
        def put(ref, at, value):
            before = jnp.where(tile > 0, ref[at].astype(f32), 0.0)
            ref[at] = (before + value).astype(ref.dtype)

        base = tile * MASK_TILE
        slots = base + lax.broadcasted_iota(jnp.int32, (MASK_TILE, total), 0)
        pick = jnp.where(rank_row[...] == slots, 1.0, 0.0).astype(b16)
        h_m = mm(pick, hi_ref[...]) + mm(pick, lo_ref[...])
        first_normed, first_scale = layer_stats(mm(pick, x_ref[...]))
        a_m = (first_normed * norm_ref[0:1, :] + norm_ref[1:2, :]).astype(b16)
        dy = mm(pick, dy_ref[...])
        dy_low = dy.astype(b16)
        normed, scale = layer_stats(h_m)
        c = (normed * gain + norm_ref[3:4, :]).astype(b16)
        dc_ref[...] = jnp.zeros_like(dc_ref)

        def hidden_block(ino, foq, half, i, carry):
            blk = 2 * half + i
            u = mm(c, w_in[blk])
            phi = normal_cdf(u)
            g = (u * phi).astype(b16)
            slope = phi + u * (jnp.exp(-0.5 * u * u) * (1.0 / math.sqrt(2.0 * math.pi)))
            du = (mm(dy_low, w_fo[blk]) * slope).astype(b16)
            dc_ref[...] += mm_nt(du, w_in[blk])
            put(foq, (i, slice(None), slice(0, hidden)), mm_tn(dy_low, g))
            put(ino, (i, slice(None), slice(0, hidden)), mm_tn(c, du))
            return carry

        lax.fori_loop(0, 2, functools.partial(hidden_block, ino_keep, foq_keep, 0), 0, unroll=True)
        lax.fori_loop(0, 2, functools.partial(hidden_block, ino_send, foq_send, 1), 0, unroll=True)
        dc = dc_ref[...]
        put(norm_grad, slice(2, 3), jnp.sum(dc * normed, axis=0, keepdims=True))
        put(norm_grad, slice(3, 4), jnp.sum(dc, axis=0, keepdims=True))
        dh = dy + layer_back(dc, normed, scale, gain)
        dattn = dh.astype(b16)
        dmix = mm(dattn, wout[...])
        for blk in range(4):
            dmix_ref[blk] = dmix[:, blk * PAIR : (blk + 1) * PAIR]
        dc_ref[...] = jnp.zeros_like(dc_ref)

        def head_block(ino, foq, half, i, carry):
            blk = 2 * half + i
            q = mm(a_m, w_ref[blk, :, :PAIR]).astype(b16)
            eq = features(q, dirs[...])
            phi_q = eq.astype(b16)
            both = mm_nt(phi_q, summ[blk])
            num, den = both[:, :PAIR], both[:, PAIR:]
            inverse = 1.0 / den
            o = (num * inverse).astype(b16)
            put(ino, (i, slice(None), slice(hidden, hidden + PAIR)), mm_tn(dattn, o))
            do = dmix_ref[blk]
            dnum = (do * inverse).astype(b16)
            prod = do * num
            first = lax.broadcasted_iota(jnp.int32, prod.shape, 1) < HEAD_DIM
            left = jnp.sum(jnp.where(first, prod, 0.0), axis=1, keepdims=True)
            right = jnp.sum(jnp.where(first, 0.0, prod), axis=1, keepdims=True)
            dden = (-jnp.where(first, left, right) * inverse * inverse).astype(b16)
            ext = jnp.concatenate([dnum, (dden.astype(f32) * (1.0 / HEAD_DIM)).astype(b16)], axis=1)
            put(acc_kv, blk, mm_tn(ext, phi_q))
            d_exp = mm(ext, summ[blk]) * eq
            dp = (SCALE * d_exp).astype(b16)
            lin = mm_nt(dp, dirs[...])
            left = jnp.sum(d_exp[:, :FEATS], axis=1, keepdims=True)
            right = jnp.sum(d_exp[:, FEATS:], axis=1, keepdims=True)
            dq = (lin - (SCALE * SCALE) * q.astype(f32) * jnp.where(first, left, right)).astype(b16)
            put(foq, (i, slice(None), slice(hidden, hidden + PAIR)), mm_tn(a_m, dq))
            dc_ref[...] += mm_nt(dq, w_ref[blk, :, :PAIR])
            return carry

        lax.fori_loop(0, 2, functools.partial(head_block, ino_keep, foq_keep, 0), 0, unroll=True)
        lax.fori_loop(0, 2, functools.partial(head_block, ino_send, foq_send, 1), 0, unroll=True)
        da = dc_ref[...]
        put(norm_grad, slice(0, 1), jnp.sum(da * first_normed, axis=0, keepdims=True))
        put(norm_grad, slice(1, 2), jnp.sum(da, axis=0, keepdims=True))
        grad = dh + layer_back(da, first_normed, first_scale, norm_ref[0:1, :])
        put(grad_ref, slice(None), mm_tn(pick, grad.astype(b16)))
        return carry

    lax.fori_loop(0, jnp.maximum((count_ref[0] + MASK_TILE - 1) // MASK_TILE, 1), step, 0)
    for blk in range(4):
        sums = jnp.concatenate(
            [acc_kv[blk, PAIR : PAIR + 1, :FEATS], acc_kv[blk, PAIR + HEAD_DIM : PAIR + HEAD_DIM + 1, FEATS:]],
            axis=1,
        ) * float(HEAD_DIM)
        (dpack_own if blk < 2 else dpack_sib)[blk % 2] = pack_summary(acc_kv[blk, :PAIR], sums)


def inputs_kernel(me_ref, x_ref, k_ref, v_ref, phi_ref, grad_ref, pack_own, pack_sib,
                  norm_ref, w_ref, dirs, norm_masked,
                  i_own, i_near, i_far, rows_grad, norm_sums, summ, mixed, norm_grad):
    for blk in range(4):
        summ[blk] = summary_matrix(pack_own if blk < 2 else pack_sib, blk % 2)
    norm_grad[...] = jnp.zeros_like(norm_grad)
    wide = 2 * PAIR
    gain = norm_ref[0:1, :]

    def step(i, carry):
        rows = pl.ds(pl.multiple_of(i * TILE, TILE), TILE)
        da = jnp.zeros((TILE, D), f32)
        for blk in range(4):
            cols = slice(blk * PAIR, (blk + 1) * PAIR)
            v = v_ref[rows, cols]
            ext = jnp.concatenate([v, jnp.full(v.shape, 1.0 / HEAD_DIM, b16)], axis=1)
            phi = phi_ref[rows, blk * 2 * FEATS : (blk + 1) * 2 * FEATS]
            d_exp = mm(ext, summ[blk]) * phi.astype(f32)
            dp = (SCALE * d_exp).astype(b16)
            lin = mm_nt(dp, dirs[...])
            left = jnp.sum(d_exp[:, :FEATS], axis=1, keepdims=True)
            right = jnp.sum(d_exp[:, FEATS:], axis=1, keepdims=True)
            first = lax.broadcasted_iota(jnp.int32, lin.shape, 1) < HEAD_DIM
            k = k_ref[rows, cols].astype(f32)
            dk = (lin - (SCALE * SCALE) * k * jnp.where(first, left, right)).astype(b16)
            dv = mm_nt(phi, summ[blk, :PAIR, :]).astype(b16)
            grads = jnp.concatenate([dk, dv], axis=1)
            rows_grad[rows, blk * wide : (blk + 1) * wide] = grads
            da = da + mm_nt(grads, w_ref[blk, :, PAIR : 3 * PAIR])
        normed, scale = layer_stats(x_ref[rows, :].astype(f32))
        norm_grad[0:8, :] += jnp.sum((da * normed).reshape(TILE // 8, 8, D), axis=0)
        norm_grad[8:16, :] += jnp.sum(da.reshape(TILE // 8, 8, D), axis=0)
        grad = grad_ref[rows, :].astype(f32) + layer_back(da, normed, scale, gain)
        mixed[rows, :] = grad.astype(b16)
        return carry

    lax.fori_loop(0, x_ref.shape[0] // TILE, step, 0)
    spread_columns(mixed, i_own, i_near, i_far, me_ref[0])
    for i in range(4):
        row = norm_masked[i : i + 1, :]
        if i < 2:
            row = row + jnp.sum(norm_grad[i * 8 : i * 8 + 8, :], axis=0, keepdims=True)
        norm_sums[i : i + 1, :] = row[:, : D // 2]
        norm_sums[4 + i : 5 + i, :] = row[:, D // 2 :]


def weights_kernel(a_ref, rows_grad, norm_sums, keep, send):
    wide = 2 * PAIR
    for blk in (2, 3, 0, 1):
        grad = mm_tn(a_ref[...], rows_grad[:, blk * wide : (blk + 1) * wide])
        if blk < 2:
            keep[blk * D : (blk + 1) * D] = grad
        else:
            send[(blk - 2) * D : (blk - 1) * D] = grad.astype(b16)
    send[2 * D :] = two_parts(norm_sums[...])


def coarse(values):
    return lax.reduce_precision(values, exponent_bits=8, mantissa_bits=7)


def two_parts(values):
    high = values.astype(b16)
    return jnp.concatenate([high, (values - high.astype(f32)).astype(b16)], axis=0)


def call(kernel, name, outs, scratch, micros, args, smem=(), vmem=20):
    specs = [
        pl.BlockSpec(memory_space=pltpu.SMEM if i in smem else pltpu.VMEM) for i in range(len(args))
    ]
    return pl.pallas_call(
        kernel,
        name=name,
        out_shape=outs,
        in_specs=specs,
        out_specs=[pl.BlockSpec(memory_space=pltpu.VMEM)] * len(outs),
        scratch_shapes=scratch,
        compiler_params=pltpu.CompilerParams(vmem_limit_bytes=vmem * MIB),
        cost_estimate=pl.CostEstimate(flops=int(micros * US), bytes_accessed=1_000, transcendentals=0),
    )(*args)


def shape(dims, dtype=b16):
    return jax.ShapeDtypeStruct(dims, dtype)


def swap(block, rows=0, heads=0):
    count = lax.axis_size("heads")
    if rows == 0:
        return lax.ppermute(block, "heads", [(i, i ^ heads) for i in range(count)])
    total = lax.axis_size("rows")
    if heads == 0:
        return lax.ppermute(block, "rows", [(i, i ^ rows) for i in range(total)])
    pairs = [
        (r * count + h, (r ^ rows) * count + (h ^ heads)) for r in range(total) for h in range(count)
    ]
    return lax.ppermute(block, ("rows", "heads"), pairs)


def bit_of(axis, bit):
    return (lax.axis_index(axis) >> bit) & 1


def sort_blocks(blocks, low_bits):
    blocks = list(blocks)
    for i, low in enumerate(low_bits):
        for d in range(len(blocks)):
            if d >> i & 1 == 0:
                one, two = blocks[d], blocks[d | 1 << i]
                blocks[d] = jnp.where(low, one, two)
                blocks[d | 1 << i] = jnp.where(low, two, one)
    return blocks


def tie(value, *others):
    return lax.optimization_barrier((value,) + others)[0]


def row_bits():
    return lax.axis_size("rows").bit_length() - 1


def chunks_of_bits():
    high = row_bits()
    groups = []
    while high > 1:
        width = min(2, high - 1)
        high -= width
        groups.append((high, width))
    return groups


def widen_bit(block, axis, bit, at, after=()):
    other = swap(block, rows=1 << bit) if axis == "rows" else swap(block, heads=1 << bit)
    other = tie(other, *after)
    return jnp.stack(sort_blocks([block, other], [bit_of(axis, bit) == 0]), axis=at)


def widen_high(block, at, after=()):
    for low, width in chunks_of_bits():
        got = [block] + [tie(swap(block, rows=d << low), *after) for d in range(1, 1 << width)]
        lows = [bit_of("rows", low + i) == 0 for i in range(width)]
        block = jnp.stack(sort_blocks(got, lows), axis=at)
        at += 1
    return block


def widen_square(block):
    got = [block, swap(block, rows=1), swap(block, heads=2), swap(block, rows=1, heads=2)]
    got = sort_blocks(got, [bit_of("rows", 0) == 0, bit_of("heads", 1) == 0])
    at = block.ndim - 2
    sides = [jnp.stack(got[:2], axis=at), jnp.stack(got[2:], axis=at)]
    return jnp.stack(sides).reshape(2, D, block.shape[-1])


def split_half(total, axis, bit, at):
    mine = bit_of(axis, bit)
    return (lax.dynamic_index_in_dim(total, mine, at, keepdims=False),
            lax.dynamic_index_in_dim(total, 1 - mine, at, keepdims=False))


def halve(total, axis, bit, at, after=()):
    here, away = split_half(total, axis, bit, at)
    other = swap(away, rows=1 << bit) if axis == "rows" else swap(away, heads=1 << bit)
    return add_low(here, tie(other, *after))


def add_low(one, two):
    return (one.astype(f32) + two.astype(f32)).astype(b16)


def spread_sum(total, beside):
    sent = total.astype(b16)
    got = [tie(swap(sent, rows=rows, heads=heads), *beside) for rows, heads in ((1, 0), (0, 2), (1, 2))]
    for block in got:
        total = total + block.astype(f32)
    total = total.astype(b16)
    return total, swap(total, heads=1)


def add_parts(sums, got):
    tail = sums.shape[0]
    return sums + (got[-2 * tail : -tail].astype(f32) + got[-tail:].astype(f32))


def add_sibling(keep, send, sums, beside):
    got = tie(swap(send, heads=1), beside)
    total = keep + got[: -2 * sums.shape[0]].astype(f32)
    return total.reshape((2,) * (1 + row_bits()) + (D >> row_bits(), keep.shape[1])), add_parts(sums, got)


def sum_stage(total, sums, axis, bit, at, after=()):
    wide = total.shape[-1]
    mine = bit_of(axis, bit)
    away = lax.dynamic_index_in_dim(total, 1 - mine, at, keepdims=False).astype(b16).reshape(-1, wide)
    total = lax.dynamic_index_in_dim(total, mine, at, keepdims=False)
    high = coarse(sums)
    away = jnp.concatenate([away, high.astype(b16), (sums - high).astype(b16)], axis=0)
    got = tie(swap(away, rows=1 << bit) if axis == "rows" else swap(away, heads=1 << bit), *after)
    total = total + got[: -2 * sums.shape[0]].reshape(total.shape).astype(f32)
    return total, add_parts(sums, got)


def side_rows(block):
    parts = block.reshape(2, block.shape[0] // 2, block.shape[1])
    return lax.dynamic_index_in_dim(parts, 1 - bit_of("heads", 1), 0, keepdims=False)


def near_rows(block, side):
    core = bit_of("heads", 0)
    n = block.shape[0] // 4
    own = lax.dynamic_slice_in_dim(block, (2 * bit_of("heads", 1) + 1 - core) * n, n, 0)
    return jnp.stack([own, lax.dynamic_slice_in_dim(side, (1 - core) * n, n, 0)])


def join_rows(own, near, side, dtype):
    got = sort_blocks([own, near[0], side[0], side[1]], [bit_of("heads", 0) == 0, bit_of("heads", 1) == 0])
    return jnp.concatenate(got, axis=0).astype(dtype)


def mask_ranks(masked_pos, masked_count, rows_dev, n):
    group = lax.axis_index("rows")
    offset = group % SPAN * rows_dev + lax.axis_index("heads") * n
    place = lax.dynamic_index_in_dim(masked_pos, group // SPAN, 0, keepdims=False) - offset
    limit = lax.dynamic_index_in_dim(masked_count, group // SPAN, 0, keepdims=False)
    inside = (jnp.arange(place.shape[0], dtype=jnp.int32) < limit) & (place >= 0) & (place < n)
    side = 32
    grid = jnp.arange(side, dtype=jnp.int32)[None, :]
    high = ((place // side)[:, None] == grid) & inside[:, None]
    low = (place % side)[:, None] == grid
    hits = mm_tn(high.astype(b16), low.astype(b16))
    marks = jnp.minimum(hits, 1.0)
    lower = grid < grid.T
    within = mm_nt(marks.astype(b16), lower.astype(b16))
    rows = jnp.sum(marks, axis=1)
    before = jnp.sum(jnp.where(lower, rows[None, :], 0.0), axis=1)
    rank = jnp.where(marks > 0, within + before[:, None], -1.0).astype(jnp.int32)
    count = jnp.sum(rows).astype(jnp.int32)
    return rank.reshape(1, n), count.reshape(1)


def body(
    tokens,
    ln1_gain,
    ln1_bias,
    qkv_weight,
    out_weight,
    ln2_gain,
    ln2_bias,
    ffn_in,
    ffn_out,
    feature_proj,
    masked_pos,
    masked_count,
    out_grad,
):
    rows_dev = tokens.shape[0]
    n = rows_dev // 4
    hidden = ffn_out.shape[0]
    narrow = ffn_out.shape[1]
    bits = row_bits()
    groups = len(chunks_of_bits())
    me = lax.axis_index("heads").astype(jnp.int32).reshape(1)

    x_cut = side_rows(tokens)
    x_side = swap(x_cut, heads=2)
    shard = jnp.concatenate([tie(qkv_weight, x_cut).transpose(2, 0, 1).reshape(narrow, -1), out_weight.T], axis=1)
    shard = widen_bit(widen_high(shard, 0), "rows", 0, groups)
    both = jnp.concatenate([tie(ffn_in, x_cut).T, ffn_out.T], axis=1)
    both = widen_bit(both, "heads", 1, 0)
    gains = tie(jnp.stack([ln1_gain, ln1_bias, ln2_gain, ln2_bias]), x_cut)
    gains_side = swap(gains, heads=2)
    x_side, shard, both, gains_side = lax.optimization_barrier((x_side, shard, both, gains_side))

    attn_own = widen_bit(shard, "heads", 1, 0).reshape(2, D, 4 * PAIR)
    fin = widen_high(both[:, :, :hidden], 1)
    fo = widen_bit(both[:, :, hidden:], "rows", 0, 1)
    dy_cut = side_rows(tie(out_grad, x_side))
    rank_row, count = mask_ranks(tie(masked_pos, x_side), masked_count, rows_dev, n)
    zero = jnp.zeros_like(feature_proj)
    dirs = tie(feature_proj, x_side)
    dirs = jnp.concatenate([jnp.concatenate([dirs, zero], 1), jnp.concatenate([zero, dirs], 1)], 0)
    near = near_rows(tokens, x_side)
    attn_own, fin, fo, dirs, dy_cut, rank_row, count, near = lax.optimization_barrier(
        (attn_own, fin, fo, dirs, dy_cut, rank_row, count, near)
    )

    attn_sib = swap(attn_own, heads=1)
    x_near = swap(near, heads=1)
    gains_near = swap(jnp.stack([gains, gains_side]), heads=1)
    x, a, norms = call(
        norm_kernel, "norm", [shape((n, D)), shape((n, D)), shape((4, D), f32)], [], 1,
        [me, tokens, x_side, x_near, gains, gains_side, gains_near], smem=(0,),
    )
    k, v, phi_k, kv_own, kv_sib, w_attn = call(
        keys_kernel, "keys",
        [shape((n, D)), shape((n, D)), shape((n, 4 * D)), shape((2, PACK, D)), shape((2, PACK, D)),
         shape((4, D, 4 * PAIR))],
        [pltpu.VMEM((4, PAIR, D), f32), pltpu.VMEM((4, 8, D), f32)],
        4, [a, attn_own, attn_sib, dirs],
    )
    fin_own = widen_bit(fin, "rows", 0, 1 + groups, (k,)).reshape(2, D, hidden)
    fo = widen_bit(fo, "rows", bits - 1, 1, (k,))
    dy_side = tie(swap(dy_cut, heads=2), k)
    kv_total = kv_own.astype(f32) + swap(kv_sib, heads=1).astype(f32)
    kv_total, fin_own, fo, dy_side = lax.optimization_barrier((kv_total, fin_own, fo, dy_side))

    (phi_q,) = call(
        queries_kernel, "queries", [shape((n, 4 * D))], [], 3, [tie(a, kv_total), w_attn, dirs],
    )
    fin_sib = swap(fin_own, heads=1)
    kv_own, kv_sib = spread_sum(kv_total, (phi_q,))
    high, low = call(
        attention_kernel, "attention", [shape((n, D)), shape((n, D))],
        [pltpu.VMEM((4, 256, D), b16), pltpu.VMEM((D, D), b16)],
        2, [x, phi_q, kv_own, kv_sib, w_attn],
    )
    for step in range(1, bits - 1):
        fo = widen_bit(fo, "rows", bits - 1 - step, 1 + step, (high,))
    fo_own = fo.reshape(2, D, hidden)
    fo_sib = swap(fo_own, heads=1)
    dy_near = swap(near_rows(out_grad, tie(dy_side, kv_own)), heads=1)
    ino_keep, ino_send, foq_keep, foq_send, dkv_own, dkv_sib, masked_grad, norm_grad = call(
        masked_kernel, "masked",
        [shape((2, D, hidden + PAIR))] * 4 + [
         shape((2, PACK, D)), shape((2, PACK, D)), shape((n, D)), shape((4, D), f32)],
        [pltpu.VMEM((n, D), b16), pltpu.VMEM((4, 256, D), b16), pltpu.VMEM((D, D), b16),
         pltpu.VMEM((4, D, hidden), b16), pltpu.VMEM((4, D, hidden), b16),
         pltpu.VMEM((4, 256, D), f32), pltpu.VMEM((MASK_TILE, D), f32), pltpu.VMEM((4, MASK_TILE, PAIR), f32)],
        18,
        [me, count, rank_row, high, low, x, out_grad, dy_side, dy_near, norms, fin_own, fin_sib, fo_own, fo_sib,
         w_attn, kv_own, kv_sib, dirs],
        smem=(0, 1), vmem=26,
    )

    dkv_total = dkv_own.astype(f32) + swap(dkv_sib, heads=1).astype(f32)
    blocks = (2,) * (1 + bits) + (narrow, hidden + PAIR)
    gino = add_low(ino_keep, swap(tie(ino_send, dkv_total), heads=1)).reshape(blocks)
    gfoq = add_low(foq_keep, swap(tie(foq_send, dkv_total), heads=1)).reshape(blocks)
    dkv_own, dkv_sib = spread_sum(dkv_total, (gino, gfoq))
    gino, ino_away = split_half(gino, "rows", 0, bits)
    gfoq, foq_away = split_half(gfoq, "heads", 1, 0)
    i_own, i_near, i_far, rows_grad, norm_sums = call(
        inputs_kernel, "inputs",
        [shape((n, PAIR)), shape((2, n, PAIR)), shape((n, PAIR)), shape((n, 2 * D)), shape((8, D // 2), f32)],
        [pltpu.VMEM((4, 256, D), b16), pltpu.VMEM((n, D), b16), pltpu.VMEM((16, D), f32)],
        6,
        [me, tie(x, gino, gfoq, ino_away, foq_away), k, v, phi_k, masked_grad, dkv_own, dkv_sib, norms, w_attn, dirs, norm_grad],
        smem=(0,),
    )
    keep, send = call(
        weights_kernel, "weights",
        [shape((2 * D, 2 * PAIR), f32), shape((2 * D + 16, 2 * PAIR))], [],
        1.3, [a, rows_grad, norm_sums],
    )
    i_near = swap(i_near, heads=1)
    m_own, m_near, m_far = call(
        forward_kernel, "forward", [shape((n, PAIR)), shape((2, n, PAIR)), shape((n, PAIR))],
        [pltpu.VMEM((n, D), b16), pltpu.VMEM((FORWARD_TILE, D), b16), pltpu.VMEM((FORWARD_TILE, D), f32)], 6,
        [me, tie(high, send), low, norms, fin_own, fin_sib, fo_own, fo_sib], smem=(0,),
    )
    total, norm_sums = add_sibling(keep, send, norm_sums, m_own)
    gino = add_low(gino, tie(swap(ino_away, rows=1), m_own))
    gfoq = add_low(gfoq, tie(swap(foq_away, heads=2), m_own))
    total, norm_sums, gino, gfoq, i_near, m_near = lax.optimization_barrier(
        (total, norm_sums, gino, gfoq, i_near, m_near)
    )
    i_side = swap(jnp.stack([i_far, i_near[1]]), heads=2)

    m_near = swap(m_near, heads=1)
    total, norm_sums = sum_stage(total, norm_sums, "heads", 1, 0)
    gino = halve(gino, "rows", 1, bits - 1)
    gfoq = halve(gfoq, "rows", 0, bits - 1)
    total, norm_sums, gino, gfoq, m_near = lax.optimization_barrier((total, norm_sums, gino, gfoq, m_near))
    m_side = swap(jnp.stack([m_far, m_near[1]]), heads=2)
    total, norm_sums = sum_stage(total, norm_sums, "rows", 0, bits - 1)
    for step in range(2, bits):
        gino = halve(gino, "rows", step, bits - step)
    gfoq = halve(gfoq, "rows", 1, bits - 2)
    total, norm_sums, gino, gfoq, i_side = lax.optimization_barrier((total, norm_sums, gino, gfoq, i_side))
    gino = halve(gino, "heads", 1, 0)
    for step in range(2, bits):
        gfoq = halve(gfoq, "rows", step, bits - 1 - step)
    for step in range(1, bits):
        total, norm_sums = sum_stage(total, norm_sums, "rows", step, bits - 1 - step)
    gkv = total
    mixed_out = join_rows(m_own, m_near, m_side, b16)
    input_grad = join_rows(i_own, i_near, i_side, f32)
    head = lax.axis_index("heads")
    mine = lax.dynamic_slice(norm_sums, (4 * (head // 2), PAIR * (head % 2)), (4, PAIR))
    gqkv = jnp.stack([gfoq[:, hidden:].T.astype(f32), gkv[:, :PAIR].T, gkv[:, PAIR:].T])

    return (
        mixed_out,
        input_grad,
        gqkv,
        gino[:, hidden:].T.astype(f32),
        gino[:, :hidden].T.astype(f32),
        gfoq[:, :hidden].T.astype(f32),
        mine[0],
        mine[1],
        mine[2],
        mine[3],
    )


def solution(mesh):
    in_specs = (
        P("rows", "heads"),
        P("heads"),
        P("heads"),
        P(None, "heads", "rows"),
        P("heads", "rows"),
        P("heads"),
        P("heads"),
        P("heads", "rows"),
        P("heads", "rows"),
        P(),
        P(),
        P(),
        P("rows", "heads"),
    )
    out_specs = (
        P("rows", "heads"),
        P("rows", "heads"),
        P(None, "heads", "rows"),
        P("heads", "rows"),
        P("heads", "rows"),
        P("heads", "rows"),
        P("heads"),
        P("heads"),
        P("heads"),
        P("heads"),
    )
    return jax.shard_map(body, mesh=mesh, in_specs=in_specs, out_specs=out_specs, check_vma=False)
```

```python
import functools
import math

import jax
import jax.numpy as jnp
from jax import lax
from jax.experimental import pallas as pl
from jax.experimental.pallas import tpu as pltpu
from jax.sharding import PartitionSpec as P

D = 512
HEAD_DIM = 64
FEATS = 256
PAIR = 2 * HEAD_DIM
SPAN = 2
PACK = 80
SCALE = HEAD_DIM ** (-0.25)
HALF_SQ = 0.5 * SCALE * SCALE
LOG2E = math.log2(math.e)
LOG2_ROOT = 0.5 * math.log2(FEATS)
epsilon = 1e-05
f32 = jnp.float32
b16 = jnp.bfloat16
MIB = 1024 * 1024
TILE = 1024
FORWARD_TILE = 512
SMALL_TILE = 256
MASK_TILE = 304
US = 1.15e9


def mm(left, right):
    return lax.dot_general(left, right, (((1,), (0,)), ((), ())), preferred_element_type=f32)


def mm_nt(left, right):
    return lax.dot_general(left, right, (((1,), (1,)), ((), ())), preferred_element_type=f32)


def mm_tn(left, right):
    return lax.dot_general(left, right, (((0,), (0,)), ((), ())), preferred_element_type=f32)


def layer_stats(values):
    mean = jnp.sum(values, axis=1, keepdims=True) * (1.0 / D)
    centred = values - mean
    var = jnp.sum(centred * centred, axis=1, keepdims=True) * (1.0 / D)
    scale = lax.rsqrt(var + epsilon)
    return centred * scale, scale


def layer_back(grad, normed, scale, gain):
    scaled = grad * gain
    first = jnp.sum(scaled, axis=1, keepdims=True) * (1.0 / D)
    second = jnp.sum(scaled * normed, axis=1, keepdims=True) * (1.0 / D)
    return scale * (scaled - first - normed * second)


def features(rows, directions):
    projected = mm(rows, directions)
    wide = rows.astype(f32)
    square = wide * wide
    first = lax.broadcasted_iota(jnp.int32, square.shape, 1) < HEAD_DIM
    left = jnp.sum(jnp.where(first, square, 0.0), axis=1, keepdims=True)
    right = jnp.sum(jnp.where(first, 0.0, square), axis=1, keepdims=True)
    return jnp.concatenate(
        [
            jnp.exp2((SCALE * LOG2E) * projected[:, :FEATS] - (HALF_SQ * LOG2E * left + LOG2_ROOT)),
            jnp.exp2((SCALE * LOG2E) * projected[:, FEATS:] - (HALF_SQ * LOG2E * right + LOG2_ROOT)),
        ],
        axis=1,
    )


def normal_cdf(u):
    return 0.5 + 0.5 * lax.erf(u * math.sqrt(0.5))


def summary_matrix(packed, blk):
    half = packed[blk]
    zero = jnp.zeros((HEAD_DIM, FEATS), b16)
    top = jnp.concatenate([half[:HEAD_DIM, :FEATS], zero], axis=1)
    low = jnp.concatenate([zero, half[:HEAD_DIM, FEATS:]], axis=1)
    sums = half[HEAD_DIM : HEAD_DIM + 1].astype(f32)
    rows = jnp.broadcast_to(sums, (HEAD_DIM, 2 * FEATS))
    left = lax.broadcasted_iota(jnp.int32, rows.shape, 1) < FEATS
    return jnp.concatenate(
        [
            top,
            low,
            jnp.where(left, rows, 0.0).astype(b16),
            jnp.where(left, 0.0, rows).astype(b16),
        ],
        axis=0,
    )


def pack_summary(matrix, sums):
    kept = jnp.concatenate([matrix[:HEAD_DIM, :FEATS], matrix[HEAD_DIM:PAIR, FEATS:]], axis=1)
    return jnp.concatenate(
        [kept.astype(b16), jnp.broadcast_to(sums, (PACK - HEAD_DIM, 2 * FEATS)).astype(b16)], axis=0
    )


def block_of(own, sib, blk):
    return own[blk] if blk < 2 else sib[blk - 2]


def gather_columns(block, side, near, target, me):
    n = target.shape[0]
    parts = (
        block[pl.ds(pl.multiple_of(me * n, n), n), :],
        near[0, :n, :],
        side[pl.ds(pl.multiple_of((me & 1) * n, n), n), :],
        near[1, :n, :],
    )
    for j in range(4):
        target[:, pl.ds(pl.multiple_of((me ^ j) * PAIR, PAIR), PAIR)] = parts[j]


def spread_columns(source, own, near, far, me):
    def columns(j):
        return source[:, pl.ds(pl.multiple_of((me ^ j) * PAIR, PAIR), PAIR)]

    own[...] = columns(0)
    near[0] = columns(1)
    near[1] = columns(3)
    far[...] = columns(2)


def norm_kernel(me_ref, block, side, near, gains, gains_side, gains_near, x_ref, a_ref, norm_ref):
    gather_columns(block, side, near, x_ref, me_ref[0])
    for j, part in enumerate((gains[...], gains_near[0], gains_side[...], gains_near[1])):
        norm_ref[:, pl.ds(pl.multiple_of((me_ref[0] ^ j) * PAIR, PAIR), PAIR)] = part

    def step(i, carry):
        rows = pl.ds(pl.multiple_of(i * SMALL_TILE, SMALL_TILE), SMALL_TILE)
        normed, _ = layer_stats(x_ref[rows, :].astype(f32))
        a_ref[rows, :] = (normed * norm_ref[0:1, :] + norm_ref[1:2, :]).astype(b16)
        return carry

    lax.fori_loop(0, x_ref.shape[0] // SMALL_TILE, step, 0)


def keys_kernel(a_ref, own, sib, dirs, k_ref, v_ref, phi_ref, pack_own, pack_sib, w_ref, acc, sums):
    for blk in range(4):
        w_ref[blk] = block_of(own, sib, blk)
    acc[...] = jnp.zeros_like(acc)
    sums[...] = jnp.zeros_like(sums)

    def step(i, carry):
        rows = pl.ds(pl.multiple_of(i * TILE, TILE), TILE)
        a = a_ref[rows, :]
        def block(blk, carry):
            kv = mm(a, w_ref[blk, :, PAIR : 3 * PAIR]).astype(b16)
            k, v = kv[:, :PAIR], kv[:, PAIR:]
            cols = pl.ds(pl.multiple_of(blk * PAIR, PAIR), PAIR)
            k_ref[rows, cols] = k
            v_ref[rows, cols] = v
            phi = features(k, dirs[...]).astype(b16)
            phi_ref[rows, pl.ds(pl.multiple_of(blk * 2 * FEATS, 2 * FEATS), 2 * FEATS)] = phi
            acc[blk] += mm_tn(v, phi)
            sums[blk] += jnp.sum(phi.astype(f32).reshape(TILE // 8, 8, 2 * FEATS), axis=0)
            return carry

        lax.fori_loop(0, 4, block, 0, unroll=1)
        return carry

    lax.fori_loop(0, a_ref.shape[0] // TILE, step, 0)
    for blk in range(4):
        packed = pack_summary(acc[blk], jnp.sum(sums[blk], axis=0, keepdims=True))
        (pack_own if blk < 2 else pack_sib)[blk % 2] = packed


def queries_kernel(a_ref, w_ref, dirs, phi_ref):
    def step(blk, carry):
        q = mm(a_ref[...], w_ref[blk, :, :PAIR]).astype(b16)
        cols = pl.ds(pl.multiple_of(blk * 2 * FEATS, 2 * FEATS), 2 * FEATS)
        phi_ref[:, cols] = features(q, dirs[...]).astype(b16)
        return carry

    lax.fori_loop(0, 4, step, 0)


def attention_kernel(x_ref, phi_ref, pack_own, pack_sib, w_ref, hi_ref, lo_ref, summ, wout):
    for blk in range(4):
        summ[blk] = summary_matrix(pack_own if blk < 2 else pack_sib, blk % 2)
        wout[:, blk * PAIR : (blk + 1) * PAIR] = w_ref[blk, :, 3 * PAIR :]

    def step(i, carry):
        rows = pl.ds(pl.multiple_of(i * SMALL_TILE, SMALL_TILE), SMALL_TILE)
        heads = []
        for blk in range(4):
            both = mm_nt(phi_ref[rows, blk * 2 * FEATS : (blk + 1) * 2 * FEATS], summ[blk])
            heads.append((both[:, :PAIR] / both[:, PAIR:]).astype(b16))
        hidden = x_ref[rows, :].astype(f32) + mm_nt(jnp.concatenate(heads, axis=1), wout[...])
        high = hidden.astype(b16)
        hi_ref[rows, :] = high
        lo_ref[rows, :] = (hidden - high.astype(f32)).astype(b16)
        return carry

    lax.fori_loop(0, x_ref.shape[0] // SMALL_TILE, step, 0)


def forward_kernel(me_ref, hi_ref, lo_ref, norm_ref, in_own, in_sib, out_own, out_sib, m_own, m_near, m_far, mixed,
                   low_ref, sum_ref):
    def step(i, carry):
        rows = pl.ds(pl.multiple_of(i * FORWARD_TILE, FORWARD_TILE), FORWARD_TILE)
        hidden = hi_ref[rows, :].astype(f32) + lo_ref[rows, :].astype(f32)
        normed, _ = layer_stats(hidden)
        low_ref[...] = (normed * norm_ref[2:3, :] + norm_ref[3:4, :]).astype(b16)
        sum_ref[...] = hidden
        for w_in, w_out in ((in_own, out_own), (in_sib, out_sib)):

            def block(blk, carry, w_in=w_in, w_out=w_out):
                u = mm(low_ref[...], w_in[blk])
                g = (u * normal_cdf(u)).astype(b16)
                sum_ref[...] += mm_nt(g, w_out[blk])
                return carry

            lax.fori_loop(0, 2, block, 0)
        mixed[rows, :] = sum_ref[...].astype(b16)
        return carry

    lax.fori_loop(0, hi_ref.shape[0] // FORWARD_TILE, step, 0)
    spread_columns(mixed, m_own, m_near, m_far, me_ref[0])


def masked_kernel(me_ref, count_ref, rank_row, hi_ref, lo_ref, x_ref, dy_block, dy_side, dy_near, norm_ref,
                  in_own, in_sib, fo_own, fo_sib, w_ref, pack_own, pack_sib, dirs,
                  ino_keep, ino_send, foq_keep, foq_send, dpack_own, dpack_sib, grad_ref, norm_grad,
                  dy_ref, summ, wout, w_in, w_fo, acc_kv, dc_ref, dmix_ref):
    hidden = fo_own.shape[2]
    total = rank_row.shape[1]
    gather_columns(dy_block, dy_side, dy_near, dy_ref, me_ref[0])
    for blk in range(4):
        summ[blk] = summary_matrix(pack_own if blk < 2 else pack_sib, blk % 2)
        wout[:, blk * PAIR : (blk + 1) * PAIR] = w_ref[blk, :, 3 * PAIR :]
        w_in[blk] = block_of(in_own, in_sib, blk)
        w_fo[blk] = block_of(fo_own, fo_sib, blk)
    gain = norm_ref[2:3, :]

    def step(tile, carry):
        def put(ref, at, value):
            before = jnp.where(tile > 0, ref[at].astype(f32), 0.0)
            ref[at] = (before + value).astype(ref.dtype)

        base = tile * MASK_TILE
        slots = base + lax.broadcasted_iota(jnp.int32, (MASK_TILE, total), 0)
        pick = jnp.where(rank_row[...] == slots, 1.0, 0.0).astype(b16)
        h_m = mm(pick, hi_ref[...]) + mm(pick, lo_ref[...])
        first_normed, first_scale = layer_stats(mm(pick, x_ref[...]))
        a_m = (first_normed * norm_ref[0:1, :] + norm_ref[1:2, :]).astype(b16)
        dy = mm(pick, dy_ref[...])
        dy_low = dy.astype(b16)
        normed, scale = layer_stats(h_m)
        c = (normed * gain + norm_ref[3:4, :]).astype(b16)
        dc_ref[...] = jnp.zeros_like(dc_ref)

        def hidden_block(ino, foq, half, i, carry):
            blk = 2 * half + i
            u = mm(c, w_in[blk])
            phi = normal_cdf(u)
            g = (u * phi).astype(b16)
            slope = phi + u * (jnp.exp(-0.5 * u * u) * (1.0 / math.sqrt(2.0 * math.pi)))
            du = (mm(dy_low, w_fo[blk]) * slope).astype(b16)
            dc_ref[...] += mm_nt(du, w_in[blk])
            put(foq, (i, slice(None), slice(0, hidden)), mm_tn(dy_low, g))
            put(ino, (i, slice(None), slice(0, hidden)), mm_tn(c, du))
            return carry

        lax.fori_loop(0, 2, functools.partial(hidden_block, ino_keep, foq_keep, 0), 0, unroll=True)
        lax.fori_loop(0, 2, functools.partial(hidden_block, ino_send, foq_send, 1), 0, unroll=True)
        dc = dc_ref[...]
        put(norm_grad, slice(2, 3), jnp.sum(dc * normed, axis=0, keepdims=True))
        put(norm_grad, slice(3, 4), jnp.sum(dc, axis=0, keepdims=True))
        dh = dy + layer_back(dc, normed, scale, gain)
        dattn = dh.astype(b16)
        dmix = mm(dattn, wout[...])
        for blk in range(4):
            dmix_ref[blk] = dmix[:, blk * PAIR : (blk + 1) * PAIR]
        dc_ref[...] = jnp.zeros_like(dc_ref)

        def head_block(ino, foq, half, i, carry):
            blk = 2 * half + i
            q = mm(a_m, w_ref[blk, :, :PAIR]).astype(b16)
            eq = features(q, dirs[...])
            phi_q = eq.astype(b16)
            both = mm_nt(phi_q, summ[blk])
            num, den = both[:, :PAIR], both[:, PAIR:]
            inverse = 1.0 / den
            o = (num * inverse).astype(b16)
            put(ino, (i, slice(None), slice(hidden, hidden + PAIR)), mm_tn(dattn, o))
            do = dmix_ref[blk]
            dnum = (do * inverse).astype(b16)
            prod = do * num
            first = lax.broadcasted_iota(jnp.int32, prod.shape, 1) < HEAD_DIM
            left = jnp.sum(jnp.where(first, prod, 0.0), axis=1, keepdims=True)
            right = jnp.sum(jnp.where(first, 0.0, prod), axis=1, keepdims=True)
            dden = (-jnp.where(first, left, right) * inverse * inverse).astype(b16)
            ext = jnp.concatenate([dnum, (dden.astype(f32) * (1.0 / HEAD_DIM)).astype(b16)], axis=1)
            put(acc_kv, blk, mm_tn(ext, phi_q))
            d_exp = mm(ext, summ[blk]) * eq
            dp = (SCALE * d_exp).astype(b16)
            lin = mm_nt(dp, dirs[...])
            left = jnp.sum(d_exp[:, :FEATS], axis=1, keepdims=True)
            right = jnp.sum(d_exp[:, FEATS:], axis=1, keepdims=True)
            dq = (lin - (SCALE * SCALE) * q.astype(f32) * jnp.where(first, left, right)).astype(b16)
            put(foq, (i, slice(None), slice(hidden, hidden + PAIR)), mm_tn(a_m, dq))
            dc_ref[...] += mm_nt(dq, w_ref[blk, :, :PAIR])
            return carry

        lax.fori_loop(0, 2, functools.partial(head_block, ino_keep, foq_keep, 0), 0, unroll=True)
        lax.fori_loop(0, 2, functools.partial(head_block, ino_send, foq_send, 1), 0, unroll=True)
        da = dc_ref[...]
        put(norm_grad, slice(0, 1), jnp.sum(da * first_normed, axis=0, keepdims=True))
        put(norm_grad, slice(1, 2), jnp.sum(da, axis=0, keepdims=True))
        grad = dh + layer_back(da, first_normed, first_scale, norm_ref[0:1, :])
        put(grad_ref, slice(None), mm_tn(pick, grad.astype(b16)))
        return carry

    lax.fori_loop(0, jnp.maximum((count_ref[0] + MASK_TILE - 1) // MASK_TILE, 1), step, 0)
    for blk in range(4):
        sums = jnp.concatenate(
            [acc_kv[blk, PAIR : PAIR + 1, :FEATS], acc_kv[blk, PAIR + HEAD_DIM : PAIR + HEAD_DIM + 1, FEATS:]],
            axis=1,
        ) * float(HEAD_DIM)
        (dpack_own if blk < 2 else dpack_sib)[blk % 2] = pack_summary(acc_kv[blk, :PAIR], sums)


def inputs_kernel(me_ref, x_ref, k_ref, v_ref, phi_ref, grad_ref, pack_own, pack_sib,
                  norm_ref, w_ref, dirs, norm_masked,
                  i_own, i_near, i_far, rows_grad, norm_sums, summ, mixed, norm_grad):
    for blk in range(4):
        summ[blk] = summary_matrix(pack_own if blk < 2 else pack_sib, blk % 2)
    norm_grad[...] = jnp.zeros_like(norm_grad)
    wide = 2 * PAIR
    gain = norm_ref[0:1, :]

    def step(i, carry):
        rows = pl.ds(pl.multiple_of(i * TILE, TILE), TILE)
        da = jnp.zeros((TILE, D), f32)
        for blk in range(4):
            cols = slice(blk * PAIR, (blk + 1) * PAIR)
            v = v_ref[rows, cols]
            ext = jnp.concatenate([v, jnp.full(v.shape, 1.0 / HEAD_DIM, b16)], axis=1)
            phi = phi_ref[rows, blk * 2 * FEATS : (blk + 1) * 2 * FEATS]
            d_exp = mm(ext, summ[blk]) * phi.astype(f32)
            dp = (SCALE * d_exp).astype(b16)
            lin = mm_nt(dp, dirs[...])
            left = jnp.sum(d_exp[:, :FEATS], axis=1, keepdims=True)
            right = jnp.sum(d_exp[:, FEATS:], axis=1, keepdims=True)
            first = lax.broadcasted_iota(jnp.int32, lin.shape, 1) < HEAD_DIM
            k = k_ref[rows, cols].astype(f32)
            dk = (lin - (SCALE * SCALE) * k * jnp.where(first, left, right)).astype(b16)
            dv = mm_nt(phi, summ[blk, :PAIR, :]).astype(b16)
            grads = jnp.concatenate([dk, dv], axis=1)
            rows_grad[rows, blk * wide : (blk + 1) * wide] = grads
            da = da + mm_nt(grads, w_ref[blk, :, PAIR : 3 * PAIR])
        normed, scale = layer_stats(x_ref[rows, :].astype(f32))
        norm_grad[0:8, :] += jnp.sum((da * normed).reshape(TILE // 8, 8, D), axis=0)
        norm_grad[8:16, :] += jnp.sum(da.reshape(TILE // 8, 8, D), axis=0)
        grad = grad_ref[rows, :].astype(f32) + layer_back(da, normed, scale, gain)
        mixed[rows, :] = grad.astype(b16)
        return carry

    lax.fori_loop(0, x_ref.shape[0] // TILE, step, 0)
    spread_columns(mixed, i_own, i_near, i_far, me_ref[0])
    for i in range(4):
        row = norm_masked[i : i + 1, :]
        if i < 2:
            row = row + jnp.sum(norm_grad[i * 8 : i * 8 + 8, :], axis=0, keepdims=True)
        norm_sums[i : i + 1, :] = row[:, : D // 2]
        norm_sums[4 + i : 5 + i, :] = row[:, D // 2 :]


def weights_kernel(a_ref, rows_grad, norm_sums, keep, send):
    wide = 2 * PAIR
    for blk in (2, 3, 0, 1):
        grad = mm_tn(a_ref[...], rows_grad[:, blk * wide : (blk + 1) * wide])
        if blk < 2:
            keep[blk * D : (blk + 1) * D] = grad
        else:
            send[(blk - 2) * D : (blk - 1) * D] = grad.astype(b16)
    send[2 * D :] = two_parts(norm_sums[...])


def coarse(values):
    return lax.reduce_precision(values, exponent_bits=8, mantissa_bits=7)


def two_parts(values):
    high = values.astype(b16)
    return jnp.concatenate([high, (values - high.astype(f32)).astype(b16)], axis=0)


def call(kernel, name, outs, scratch, micros, args, smem=(), vmem=20):
    specs = [
        pl.BlockSpec(memory_space=pltpu.SMEM if i in smem else pltpu.VMEM) for i in range(len(args))
    ]
    return pl.pallas_call(
        kernel,
        name=name,
        out_shape=outs,
        in_specs=specs,
        out_specs=[pl.BlockSpec(memory_space=pltpu.VMEM)] * len(outs),
        scratch_shapes=scratch,
        compiler_params=pltpu.CompilerParams(vmem_limit_bytes=vmem * MIB),
        cost_estimate=pl.CostEstimate(flops=int(micros * US), bytes_accessed=1_000, transcendentals=0),
    )(*args)


def shape(dims, dtype=b16):
    return jax.ShapeDtypeStruct(dims, dtype)


def swap(block, rows=0, heads=0):
    count = lax.axis_size("heads")
    if rows == 0:
        return lax.ppermute(block, "heads", [(i, i ^ heads) for i in range(count)])
    total = lax.axis_size("rows")
    if heads == 0:
        return lax.ppermute(block, "rows", [(i, i ^ rows) for i in range(total)])
    pairs = [
        (r * count + h, (r ^ rows) * count + (h ^ heads)) for r in range(total) for h in range(count)
    ]
    return lax.ppermute(block, ("rows", "heads"), pairs)


def bit_of(axis, bit):
    return (lax.axis_index(axis) >> bit) & 1


def sort_blocks(blocks, low_bits):
    blocks = list(blocks)
    for i, low in enumerate(low_bits):
        for d in range(len(blocks)):
            if d >> i & 1 == 0:
                one, two = blocks[d], blocks[d | 1 << i]
                blocks[d] = jnp.where(low, one, two)
                blocks[d | 1 << i] = jnp.where(low, two, one)
    return blocks


def tie(value, *others):
    return lax.optimization_barrier((value,) + others)[0]


def row_bits():
    return lax.axis_size("rows").bit_length() - 1


def chunks_of_bits():
    high = row_bits()
    groups = []
    while high > 1:
        width = min(2, high - 1)
        high -= width
        groups.append((high, width))
    return groups


def widen_bit(block, axis, bit, at, after=()):
    other = swap(block, rows=1 << bit) if axis == "rows" else swap(block, heads=1 << bit)
    other = tie(other, *after)
    return jnp.stack(sort_blocks([block, other], [bit_of(axis, bit) == 0]), axis=at)


def widen_high(block, at, after=()):
    for low, width in chunks_of_bits():
        got = [block] + [tie(swap(block, rows=d << low), *after) for d in range(1, 1 << width)]
        lows = [bit_of("rows", low + i) == 0 for i in range(width)]
        block = jnp.stack(sort_blocks(got, lows), axis=at)
        at += 1
    return block


def widen_square(block):
    got = [block, swap(block, rows=1), swap(block, heads=2), swap(block, rows=1, heads=2)]
    got = sort_blocks(got, [bit_of("rows", 0) == 0, bit_of("heads", 1) == 0])
    at = block.ndim - 2
    sides = [jnp.stack(got[:2], axis=at), jnp.stack(got[2:], axis=at)]
    return jnp.stack(sides).reshape(2, D, block.shape[-1])


def split_half(total, axis, bit, at):
    mine = bit_of(axis, bit)
    return (lax.dynamic_index_in_dim(total, mine, at, keepdims=False),
            lax.dynamic_index_in_dim(total, 1 - mine, at, keepdims=False))


def halve(total, axis, bit, at, after=()):
    here, away = split_half(total, axis, bit, at)
    other = swap(away, rows=1 << bit) if axis == "rows" else swap(away, heads=1 << bit)
    return add_low(here, tie(other, *after))


def add_low(one, two):
    return (one.astype(f32) + two.astype(f32)).astype(b16)


def spread_sum(total, beside):
    sent = total.astype(b16)
    got = [tie(swap(sent, rows=rows, heads=heads), *beside) for rows, heads in ((1, 0), (0, 2), (1, 2))]
    for block in got:
        total = total + block.astype(f32)
    total = total.astype(b16)
    return total, swap(total, heads=1)


def add_parts(sums, got):
    tail = sums.shape[0]
    return sums + (got[-2 * tail : -tail].astype(f32) + got[-tail:].astype(f32))


def add_sibling(keep, send, sums, beside):
    got = tie(swap(send, heads=1), beside)
    total = keep + got[: -2 * sums.shape[0]].astype(f32)
    return total.reshape((2,) * (1 + row_bits()) + (D >> row_bits(), keep.shape[1])), add_parts(sums, got)


def sum_stage(total, sums, axis, bit, at, after=()):
    wide = total.shape[-1]
    mine = bit_of(axis, bit)
    away = lax.dynamic_index_in_dim(total, 1 - mine, at, keepdims=False).astype(b16).reshape(-1, wide)
    total = lax.dynamic_index_in_dim(total, mine, at, keepdims=False)
    high = coarse(sums)
    away = jnp.concatenate([away, high.astype(b16), (sums - high).astype(b16)], axis=0)
    got = tie(swap(away, rows=1 << bit) if axis == "rows" else swap(away, heads=1 << bit), *after)
    total = total + got[: -2 * sums.shape[0]].reshape(total.shape).astype(f32)
    return total, add_parts(sums, got)


def side_rows(block):
    parts = block.reshape(2, block.shape[0] // 2, block.shape[1])
    return lax.dynamic_index_in_dim(parts, 1 - bit_of("heads", 1), 0, keepdims=False)


def near_rows(block, side):
    core = bit_of("heads", 0)
    n = block.shape[0] // 4
    own = lax.dynamic_slice_in_dim(block, (2 * bit_of("heads", 1) + 1 - core) * n, n, 0)
    return jnp.stack([own, lax.dynamic_slice_in_dim(side, (1 - core) * n, n, 0)])


def join_rows(own, near, side, dtype):
    got = sort_blocks([own, near[0], side[0], side[1]], [bit_of("heads", 0) == 0, bit_of("heads", 1) == 0])
    return jnp.concatenate(got, axis=0).astype(dtype)


def mask_ranks(masked_pos, masked_count, rows_dev, n):
    group = lax.axis_index("rows")
    offset = group % SPAN * rows_dev + lax.axis_index("heads") * n
    place = lax.dynamic_index_in_dim(masked_pos, group // SPAN, 0, keepdims=False) - offset
    limit = lax.dynamic_index_in_dim(masked_count, group // SPAN, 0, keepdims=False)
    inside = (jnp.arange(place.shape[0], dtype=jnp.int32) < limit) & (place >= 0) & (place < n)
    side = 32
    grid = jnp.arange(side, dtype=jnp.int32)[None, :]
    high = ((place // side)[:, None] == grid) & inside[:, None]
    low = (place % side)[:, None] == grid
    hits = mm_tn(high.astype(b16), low.astype(b16))
    marks = jnp.minimum(hits, 1.0)
    lower = grid < grid.T
    within = mm_nt(marks.astype(b16), lower.astype(b16))
    rows = jnp.sum(marks, axis=1)
    before = jnp.sum(jnp.where(lower, rows[None, :], 0.0), axis=1)
    rank = jnp.where(marks > 0, within + before[:, None], -1.0).astype(jnp.int32)
    count = jnp.sum(rows).astype(jnp.int32)
    return rank.reshape(1, n), count.reshape(1)


def body(
    tokens,
    ln1_gain,
    ln1_bias,
    qkv_weight,
    out_weight,
    ln2_gain,
    ln2_bias,
    ffn_in,
    ffn_out,
    feature_proj,
    masked_pos,
    masked_count,
    out_grad,
):
    rows_dev = tokens.shape[0]
    n = rows_dev // 4
    hidden = ffn_out.shape[0]
    narrow = ffn_out.shape[1]
    bits = row_bits()
    groups = len(chunks_of_bits())
    me = lax.axis_index("heads").astype(jnp.int32).reshape(1)

    x_cut = side_rows(tokens)
    x_side = swap(x_cut, heads=2)
    shard = jnp.concatenate([tie(qkv_weight, x_cut).transpose(2, 0, 1).reshape(narrow, -1), out_weight.T], axis=1)
    shard = widen_bit(widen_high(shard, 0), "rows", 0, groups)
    both = jnp.concatenate([tie(ffn_in, x_cut).T, ffn_out.T], axis=1)
    both = widen_bit(both, "heads", 1, 0)
    gains = tie(jnp.stack([ln1_gain, ln1_bias, ln2_gain, ln2_bias]), x_cut)
    gains_side = swap(gains, heads=2)
    x_side, shard, both, gains_side = lax.optimization_barrier((x_side, shard, both, gains_side))

    attn_own = widen_bit(shard, "heads", 1, 0).reshape(2, D, 4 * PAIR)
    fin = widen_high(both[:, :, :hidden], 1)
    fo = widen_bit(both[:, :, hidden:], "rows", 0, 1)
    dy_cut = side_rows(tie(out_grad, x_side))
    rank_row, count = mask_ranks(tie(masked_pos, x_side), masked_count, rows_dev, n)
    zero = jnp.zeros_like(feature_proj)
    dirs = tie(feature_proj, x_side)
    dirs = jnp.concatenate([jnp.concatenate([dirs, zero], 1), jnp.concatenate([zero, dirs], 1)], 0)
    near = near_rows(tokens, x_side)
    attn_own, fin, fo, dirs, dy_cut, rank_row, count, near = lax.optimization_barrier(
        (attn_own, fin, fo, dirs, dy_cut, rank_row, count, near)
    )

    attn_sib = swap(attn_own, heads=1)
    x_near = swap(near, heads=1)
    gains_near = swap(jnp.stack([gains, gains_side]), heads=1)
    x, a, norms = call(
        norm_kernel, "norm", [shape((n, D)), shape((n, D)), shape((4, D), f32)], [], 1,
        [me, tokens, x_side, x_near, gains, gains_side, gains_near], smem=(0,),
    )
    k, v, phi_k, kv_own, kv_sib, w_attn = call(
        keys_kernel, "keys",
        [shape((n, D)), shape((n, D)), shape((n, 4 * D)), shape((2, PACK, D)), shape((2, PACK, D)),
         shape((4, D, 4 * PAIR))],
        [pltpu.VMEM((4, PAIR, D), f32), pltpu.VMEM((4, 8, D), f32)],
        4, [a, attn_own, attn_sib, dirs],
    )
    fin_own = widen_bit(fin, "rows", 0, 1 + groups, (k,)).reshape(2, D, hidden)
    fo = widen_bit(fo, "rows", bits - 1, 1, (k,))
    dy_side = tie(swap(dy_cut, heads=2), k)
    kv_total = kv_own.astype(f32) + swap(kv_sib, heads=1).astype(f32)
    kv_total, fin_own, fo, dy_side = lax.optimization_barrier((kv_total, fin_own, fo, dy_side))

    (phi_q,) = call(
        queries_kernel, "queries", [shape((n, 4 * D))], [], 3, [tie(a, kv_total), w_attn, dirs],
    )
    fin_sib = swap(fin_own, heads=1)
    kv_own, kv_sib = spread_sum(kv_total, (phi_q,))
    high, low = call(
        attention_kernel, "attention", [shape((n, D)), shape((n, D))],
        [pltpu.VMEM((4, 256, D), b16), pltpu.VMEM((D, D), b16)],
        2, [x, phi_q, kv_own, kv_sib, w_attn],
    )
    for step in range(1, bits - 1):
        fo = widen_bit(fo, "rows", bits - 1 - step, 1 + step, (high,))
    fo_own = fo.reshape(2, D, hidden)
    fo_sib = swap(fo_own, heads=1)
    dy_near = swap(near_rows(out_grad, tie(dy_side, kv_own)), heads=1)
    ino_keep, ino_send, foq_keep, foq_send, dkv_own, dkv_sib, masked_grad, norm_grad = call(
        masked_kernel, "masked",
        [shape((2, D, hidden + PAIR))] * 4 + [
         shape((2, PACK, D)), shape((2, PACK, D)), shape((n, D)), shape((4, D), f32)],
        [pltpu.VMEM((n, D), b16), pltpu.VMEM((4, 256, D), b16), pltpu.VMEM((D, D), b16),
         pltpu.VMEM((4, D, hidden), b16), pltpu.VMEM((4, D, hidden), b16),
         pltpu.VMEM((4, 256, D), f32), pltpu.VMEM((MASK_TILE, D), f32), pltpu.VMEM((4, MASK_TILE, PAIR), f32)],
        18,
        [me, count, rank_row, high, low, x, out_grad, dy_side, dy_near, norms, fin_own, fin_sib, fo_own, fo_sib,
         w_attn, kv_own, kv_sib, dirs],
        smem=(0, 1), vmem=26,
    )

    dkv_total = dkv_own.astype(f32) + swap(dkv_sib, heads=1).astype(f32)
    blocks = (2,) * (1 + bits) + (narrow, hidden + PAIR)
    gino = add_low(ino_keep, swap(tie(ino_send, dkv_total), heads=1)).reshape(blocks)
    gfoq = add_low(foq_keep, swap(tie(foq_send, dkv_total), heads=1)).reshape(blocks)
    dkv_own, dkv_sib = spread_sum(dkv_total, (gino, gfoq))
    gino, ino_away = split_half(gino, "rows", 0, bits)
    gfoq, foq_away = split_half(gfoq, "heads", 1, 0)
    i_own, i_near, i_far, rows_grad, norm_sums = call(
        inputs_kernel, "inputs",
        [shape((n, PAIR)), shape((2, n, PAIR)), shape((n, PAIR)), shape((n, 2 * D)), shape((8, D // 2), f32)],
        [pltpu.VMEM((4, 256, D), b16), pltpu.VMEM((n, D), b16), pltpu.VMEM((16, D), f32)],
        6,
        [me, tie(x, gino, gfoq, ino_away, foq_away), k, v, phi_k, masked_grad, dkv_own, dkv_sib, norms, w_attn, dirs, norm_grad],
        smem=(0,),
    )
    keep, send = call(
        weights_kernel, "weights",
        [shape((2 * D, 2 * PAIR), f32), shape((2 * D + 16, 2 * PAIR))], [],
        1.3, [a, rows_grad, norm_sums],
    )
    i_near = swap(i_near, heads=1)
    m_own, m_near, m_far = call(
        forward_kernel, "forward", [shape((n, PAIR)), shape((2, n, PAIR)), shape((n, PAIR))],
        [pltpu.VMEM((n, D), b16), pltpu.VMEM((FORWARD_TILE, D), b16), pltpu.VMEM((FORWARD_TILE, D), f32)], 6,
        [me, tie(high, send), low, norms, fin_own, fin_sib, fo_own, fo_sib], smem=(0,),
    )
    total, norm_sums = add_sibling(keep, send, norm_sums, m_own)
    gino = add_low(gino, tie(swap(ino_away, rows=1), m_own))
    gfoq = add_low(gfoq, tie(swap(foq_away, heads=2), m_own))
    total, norm_sums, gino, gfoq, i_near, m_near = lax.optimization_barrier(
        (total, norm_sums, gino, gfoq, i_near, m_near)
    )
    i_side = swap(jnp.stack([i_far, i_near[1]]), heads=2)

    m_near = swap(m_near, heads=1)
    total, norm_sums = sum_stage(total, norm_sums, "heads", 1, 0)
    gino = halve(gino, "rows", 1, bits - 1)
    gfoq = halve(gfoq, "rows", 0, bits - 1)
    total, norm_sums, gino, gfoq, m_near = lax.optimization_barrier((total, norm_sums, gino, gfoq, m_near))
    m_side = swap(jnp.stack([m_far, m_near[1]]), heads=2)
    total, norm_sums = sum_stage(total, norm_sums, "rows", 0, bits - 1)
    for step in range(2, bits):
        gino = halve(gino, "rows", step, bits - step)
    gfoq = halve(gfoq, "rows", 1, bits - 2)
    total, norm_sums, gino, gfoq, i_side = lax.optimization_barrier((total, norm_sums, gino, gfoq, i_side))
    gino = halve(gino, "heads", 1, 0)
    for step in range(2, bits):
        gfoq = halve(gfoq, "rows", step, bits - 1 - step)
    for step in range(1, bits):
        total, norm_sums = sum_stage(total, norm_sums, "rows", step, bits - 1 - step)
    gkv = total
    mixed_out = join_rows(m_own, m_near, m_side, b16)
    input_grad = join_rows(i_own, i_near, i_side, f32)
    head = lax.axis_index("heads")
    mine = lax.dynamic_slice(norm_sums, (4 * (head // 2), PAIR * (head % 2)), (4, PAIR))
    gqkv = jnp.stack([gfoq[:, hidden:].T.astype(f32), gkv[:, :PAIR].T, gkv[:, PAIR:].T])

    return (
        mixed_out,
        input_grad,
        gqkv,
        gino[:, hidden:].T.astype(f32),
        gino[:, :hidden].T.astype(f32),
        gfoq[:, :hidden].T.astype(f32),
        mine[0],
        mine[1],
        mine[2],
        mine[3],
    )


def solution(mesh):
    in_specs = (
        P("rows", "heads"),
        P("heads"),
        P("heads"),
        P(None, "heads", "rows"),
        P("heads", "rows"),
        P("heads"),
        P("heads"),
        P("heads", "rows"),
        P("heads", "rows"),
        P(),
        P(),
        P(),
        P("rows", "heads"),
    )
    out_specs = (
        P("rows", "heads"),
        P("rows", "heads"),
        P(None, "heads", "rows"),
        P("heads", "rows"),
        P("heads", "rows"),
        P("heads", "rows"),
        P("heads"),
        P("heads"),
        P("heads"),
        P("heads"),
    )
    return jax.shard_map(body, mesh=mesh, in_specs=in_specs, out_specs=out_specs, check_vma=False)
```

```python
import functools
import math

import jax
import jax.numpy as jnp
from jax import lax
from jax.experimental import pallas as pl
from jax.experimental.pallas import tpu as pltpu
from jax.sharding import PartitionSpec as P

D = 512
HEAD_DIM = 64
FEATS = 256
PAIR = 2 * HEAD_DIM
SPAN = 2
PACK = 72
SCALE = HEAD_DIM ** (-0.25)
HALF_SQ = 0.5 * SCALE * SCALE
LOG2E = math.log2(math.e)
LOG2_ROOT = 0.5 * math.log2(FEATS)
epsilon = 1e-05
f32 = jnp.float32
b16 = jnp.bfloat16
MIB = 1024 * 1024
TILE = 1024
FORWARD_TILE = 512
SMALL_TILE = 256
MASK_TILE = 304
US = 1.15e9


def mm(left, right):
    return lax.dot_general(left, right, (((1,), (0,)), ((), ())), preferred_element_type=f32)


def mm_nt(left, right):
    return lax.dot_general(left, right, (((1,), (1,)), ((), ())), preferred_element_type=f32)


def mm_tn(left, right):
    return lax.dot_general(left, right, (((0,), (0,)), ((), ())), preferred_element_type=f32)


def layer_stats(values):
    mean = jnp.sum(values, axis=1, keepdims=True) * (1.0 / D)
    centred = values - mean
    var = jnp.sum(centred * centred, axis=1, keepdims=True) * (1.0 / D)
    scale = lax.rsqrt(var + epsilon)
    return centred * scale, scale


def layer_back(grad, normed, scale, gain):
    scaled = grad * gain
    first = jnp.sum(scaled, axis=1, keepdims=True) * (1.0 / D)
    second = jnp.sum(scaled * normed, axis=1, keepdims=True) * (1.0 / D)
    return scale * (scaled - first - normed * second)


def features(rows, directions):
    projected = mm(rows, directions)
    wide = rows.astype(f32)
    square = wide * wide
    first = lax.broadcasted_iota(jnp.int32, square.shape, 1) < HEAD_DIM
    left = jnp.sum(jnp.where(first, square, 0.0), axis=1, keepdims=True)
    right = jnp.sum(jnp.where(first, 0.0, square), axis=1, keepdims=True)
    return jnp.concatenate(
        [
            jnp.exp2((SCALE * LOG2E) * projected[:, :FEATS] - (HALF_SQ * LOG2E * left + LOG2_ROOT)),
            jnp.exp2((SCALE * LOG2E) * projected[:, FEATS:] - (HALF_SQ * LOG2E * right + LOG2_ROOT)),
        ],
        axis=1,
    )


def normal_cdf(u):
    return 0.5 + 0.5 * lax.erf(u * math.sqrt(0.5))


def summary_matrix(packed, blk):
    half = packed[blk]
    zero = jnp.zeros((HEAD_DIM, FEATS), b16)
    top = jnp.concatenate([half[:HEAD_DIM, :FEATS], zero], axis=1)
    low = jnp.concatenate([zero, half[:HEAD_DIM, FEATS:]], axis=1)
    sums = half[HEAD_DIM : HEAD_DIM + 1].astype(f32)
    rows = jnp.broadcast_to(sums, (HEAD_DIM, 2 * FEATS))
    left = lax.broadcasted_iota(jnp.int32, rows.shape, 1) < FEATS
    return jnp.concatenate(
        [
            top,
            low,
            jnp.where(left, rows, 0.0).astype(b16),
            jnp.where(left, 0.0, rows).astype(b16),
        ],
        axis=0,
    )


def pack_summary(matrix, sums):
    kept = jnp.concatenate([matrix[:HEAD_DIM, :FEATS], matrix[HEAD_DIM:PAIR, FEATS:]], axis=1)
    return jnp.concatenate(
        [kept.astype(b16), jnp.broadcast_to(sums, (PACK - HEAD_DIM, 2 * FEATS)).astype(b16)], axis=0
    )


def block_of(own, sib, blk):
    return own[blk] if blk < 2 else sib[blk - 2]


def gather_columns(block, side, near, target, me):
    n = target.shape[0]
    parts = (
        block[pl.ds(pl.multiple_of(me * n, n), n), :],
        near[0, :n, :],
        side[pl.ds(pl.multiple_of((me & 1) * n, n), n), :],
        near[1, :n, :],
    )
    for j in range(4):
        target[:, pl.ds(pl.multiple_of((me ^ j) * PAIR, PAIR), PAIR)] = parts[j]


def spread_columns(source, own, near, far, me):
    def columns(j):
        return source[:, pl.ds(pl.multiple_of((me ^ j) * PAIR, PAIR), PAIR)]

    own[...] = columns(0)
    near[0] = columns(1)
    near[1] = columns(3)
    far[...] = columns(2)


def norm_kernel(me_ref, block, side, near, gains, gains_side, gains_near, x_ref, a_ref, norm_ref):
    gather_columns(block, side, near, x_ref, me_ref[0])
    for j, part in enumerate((gains[...], gains_near[0], gains_side[...], gains_near[1])):
        norm_ref[:, pl.ds(pl.multiple_of((me_ref[0] ^ j) * PAIR, PAIR), PAIR)] = part

    def step(i, carry):
        rows = pl.ds(pl.multiple_of(i * SMALL_TILE, SMALL_TILE), SMALL_TILE)
        normed, _ = layer_stats(x_ref[rows, :].astype(f32))
        a_ref[rows, :] = (normed * norm_ref[0:1, :] + norm_ref[1:2, :]).astype(b16)
        return carry

    lax.fori_loop(0, x_ref.shape[0] // SMALL_TILE, step, 0)


def keys_kernel(a_ref, own, sib, dirs, k_ref, v_ref, phi_ref, pack_own, pack_sib, w_ref, acc, sums):
    for blk in range(4):
        w_ref[blk] = block_of(own, sib, blk)
    acc[...] = jnp.zeros_like(acc)
    sums[...] = jnp.zeros_like(sums)

    def step(i, carry):
        rows = pl.ds(pl.multiple_of(i * TILE, TILE), TILE)
        a = a_ref[rows, :]
        def block(blk, carry):
            kv = mm(a, w_ref[blk, :, PAIR : 3 * PAIR]).astype(b16)
            k, v = kv[:, :PAIR], kv[:, PAIR:]
            cols = pl.ds(pl.multiple_of(blk * PAIR, PAIR), PAIR)
            k_ref[rows, cols] = k
            v_ref[rows, cols] = v
            phi = features(k, dirs[...]).astype(b16)
            phi_ref[rows, pl.ds(pl.multiple_of(blk * 2 * FEATS, 2 * FEATS), 2 * FEATS)] = phi
            acc[blk] += mm_tn(v, phi)
            sums[blk] += jnp.sum(phi.astype(f32).reshape(TILE // 8, 8, 2 * FEATS), axis=0)
            return carry

        lax.fori_loop(0, 4, block, 0, unroll=1)
        return carry

    lax.fori_loop(0, a_ref.shape[0] // TILE, step, 0)
    for blk in range(4):
        packed = pack_summary(acc[blk], jnp.sum(sums[blk], axis=0, keepdims=True))
        (pack_own if blk < 2 else pack_sib)[blk % 2] = packed


def queries_kernel(a_ref, w_ref, dirs, phi_ref):
    def step(blk, carry):
        q = mm(a_ref[...], w_ref[blk, :, :PAIR]).astype(b16)
        cols = pl.ds(pl.multiple_of(blk * 2 * FEATS, 2 * FEATS), 2 * FEATS)
        phi_ref[:, cols] = features(q, dirs[...]).astype(b16)
        return carry

    lax.fori_loop(0, 4, step, 0)


def attention_kernel(x_ref, phi_ref, pack_own, pack_sib, w_ref, hi_ref, lo_ref, summ, wout):
    for blk in range(4):
        summ[blk] = summary_matrix(pack_own if blk < 2 else pack_sib, blk % 2)
        wout[:, blk * PAIR : (blk + 1) * PAIR] = w_ref[blk, :, 3 * PAIR :]

    def step(i, carry):
        rows = pl.ds(pl.multiple_of(i * SMALL_TILE, SMALL_TILE), SMALL_TILE)
        heads = []
        for blk in range(4):
            both = mm_nt(phi_ref[rows, blk * 2 * FEATS : (blk + 1) * 2 * FEATS], summ[blk])
            heads.append((both[:, :PAIR] / both[:, PAIR:]).astype(b16))
        hidden = x_ref[rows, :].astype(f32) + mm_nt(jnp.concatenate(heads, axis=1), wout[...])
        high = hidden.astype(b16)
        hi_ref[rows, :] = high
        lo_ref[rows, :] = (hidden - high.astype(f32)).astype(b16)
        return carry

    lax.fori_loop(0, x_ref.shape[0] // SMALL_TILE, step, 0)


def forward_kernel(me_ref, hi_ref, lo_ref, norm_ref, in_own, in_sib, out_own, out_sib, m_own, m_near, m_far, mixed,
                   low_ref, sum_ref):
    def step(i, carry):
        rows = pl.ds(pl.multiple_of(i * FORWARD_TILE, FORWARD_TILE), FORWARD_TILE)
        hidden = hi_ref[rows, :].astype(f32) + lo_ref[rows, :].astype(f32)
        normed, _ = layer_stats(hidden)
        low_ref[...] = (normed * norm_ref[2:3, :] + norm_ref[3:4, :]).astype(b16)
        sum_ref[...] = hidden
        for w_in, w_out in ((in_own, out_own), (in_sib, out_sib)):

            def block(blk, carry, w_in=w_in, w_out=w_out):
                u = mm(low_ref[...], w_in[blk])
                g = (u * normal_cdf(u)).astype(b16)
                sum_ref[...] += mm_nt(g, w_out[blk])
                return carry

            lax.fori_loop(0, 2, block, 0, unroll=True)
        mixed[rows, :] = sum_ref[...].astype(b16)
        return carry

    lax.fori_loop(0, hi_ref.shape[0] // FORWARD_TILE, step, 0)
    spread_columns(mixed, m_own, m_near, m_far, me_ref[0])


def masked_kernel(me_ref, count_ref, rank_row, hi_ref, lo_ref, x_ref, dy_block, dy_side, dy_near, norm_ref,
                  in_own, in_sib, fo_own, fo_sib, w_ref, pack_own, pack_sib, dirs,
                  ino_keep, ino_send, foq_keep, foq_send, dpack_own, dpack_sib, grad_ref, norm_grad,
                  dy_ref, summ, wout, w_in, w_fo, acc_kv, dc_ref, dmix_ref):
    hidden = fo_own.shape[2]
    total = rank_row.shape[1]
    gather_columns(dy_block, dy_side, dy_near, dy_ref, me_ref[0])
    for blk in range(4):
        summ[blk] = summary_matrix(pack_own if blk < 2 else pack_sib, blk % 2)
        wout[:, blk * PAIR : (blk + 1) * PAIR] = w_ref[blk, :, 3 * PAIR :]
        w_in[blk] = block_of(in_own, in_sib, blk)
        w_fo[blk] = block_of(fo_own, fo_sib, blk)
    gain = norm_ref[2:3, :]

    def step(tile, carry):
        def put(ref, at, value):
            before = jnp.where(tile > 0, ref[at].astype(f32), 0.0)
            ref[at] = (before + value).astype(ref.dtype)

        base = tile * MASK_TILE
        slots = base + lax.broadcasted_iota(jnp.int32, (MASK_TILE, total), 0)
        pick = jnp.where(rank_row[...] == slots, 1.0, 0.0).astype(b16)
        h_m = mm(pick, hi_ref[...]) + mm(pick, lo_ref[...])
        first_normed, first_scale = layer_stats(mm(pick, x_ref[...]))
        a_m = (first_normed * norm_ref[0:1, :] + norm_ref[1:2, :]).astype(b16)
        dy = mm(pick, dy_ref[...])
        dy_low = dy.astype(b16)
        normed, scale = layer_stats(h_m)
        c = (normed * gain + norm_ref[3:4, :]).astype(b16)
        dc_ref[...] = jnp.zeros_like(dc_ref)

        def hidden_block(ino, foq, half, i, carry):
            blk = 2 * half + i
            u = mm(c, w_in[blk])
            phi = normal_cdf(u)
            g = (u * phi).astype(b16)
            slope = phi + u * (jnp.exp(-0.5 * u * u) * (1.0 / math.sqrt(2.0 * math.pi)))
            du = (mm(dy_low, w_fo[blk]) * slope).astype(b16)
            dc_ref[...] += mm_nt(du, w_in[blk])
            put(foq, (i, slice(None), slice(0, hidden)), mm_tn(dy_low, g))
            put(ino, (i, slice(None), slice(0, hidden)), mm_tn(c, du))
            return carry

        lax.fori_loop(0, 2, functools.partial(hidden_block, ino_keep, foq_keep, 0), 0, unroll=True)
        lax.fori_loop(0, 2, functools.partial(hidden_block, ino_send, foq_send, 1), 0, unroll=True)
        dc = dc_ref[...]
        put(norm_grad, slice(2, 3), jnp.sum(dc * normed, axis=0, keepdims=True))
        put(norm_grad, slice(3, 4), jnp.sum(dc, axis=0, keepdims=True))
        dh = dy + layer_back(dc, normed, scale, gain)
        dattn = dh.astype(b16)
        dmix = mm(dattn, wout[...])
        for blk in range(4):
            dmix_ref[blk] = dmix[:, blk * PAIR : (blk + 1) * PAIR]
        dc_ref[...] = jnp.zeros_like(dc_ref)

        def head_block(ino, foq, half, i, carry):
            blk = 2 * half + i
            q = mm(a_m, w_ref[blk, :, :PAIR]).astype(b16)
            eq = features(q, dirs[...])
            phi_q = eq.astype(b16)
            both = mm_nt(phi_q, summ[blk])
            num, den = both[:, :PAIR], both[:, PAIR:]
            inverse = 1.0 / den
            o = (num * inverse).astype(b16)
            put(ino, (i, slice(None), slice(hidden, hidden + PAIR)), mm_tn(dattn, o))
            do = dmix_ref[blk]
            dnum = (do * inverse).astype(b16)
            prod = do * num
            first = lax.broadcasted_iota(jnp.int32, prod.shape, 1) < HEAD_DIM
            left = jnp.sum(jnp.where(first, prod, 0.0), axis=1, keepdims=True)
            right = jnp.sum(jnp.where(first, 0.0, prod), axis=1, keepdims=True)
            dden = (-jnp.where(first, left, right) * inverse * inverse).astype(b16)
            ext = jnp.concatenate([dnum, (dden.astype(f32) * (1.0 / HEAD_DIM)).astype(b16)], axis=1)
            put(acc_kv, blk, mm_tn(ext, phi_q))
            d_exp = mm(ext, summ[blk]) * eq
            dp = (SCALE * d_exp).astype(b16)
            lin = mm_nt(dp, dirs[...])
            left = jnp.sum(d_exp[:, :FEATS], axis=1, keepdims=True)
            right = jnp.sum(d_exp[:, FEATS:], axis=1, keepdims=True)
            dq = (lin - (SCALE * SCALE) * q.astype(f32) * jnp.where(first, left, right)).astype(b16)
            put(foq, (i, slice(None), slice(hidden, hidden + PAIR)), mm_tn(a_m, dq))
            dc_ref[...] += mm_nt(dq, w_ref[blk, :, :PAIR])
            return carry

        lax.fori_loop(0, 2, functools.partial(head_block, ino_keep, foq_keep, 0), 0, unroll=True)
        lax.fori_loop(0, 2, functools.partial(head_block, ino_send, foq_send, 1), 0, unroll=True)
        da = dc_ref[...]
        put(norm_grad, slice(0, 1), jnp.sum(da * first_normed, axis=0, keepdims=True))
        put(norm_grad, slice(1, 2), jnp.sum(da, axis=0, keepdims=True))
        grad = dh + layer_back(da, first_normed, first_scale, norm_ref[0:1, :])
        put(grad_ref, slice(None), mm_tn(pick, grad.astype(b16)))
        return carry

    lax.fori_loop(0, jnp.maximum((count_ref[0] + MASK_TILE - 1) // MASK_TILE, 1), step, 0)
    for blk in range(4):
        sums = jnp.concatenate(
            [acc_kv[blk, PAIR : PAIR + 1, :FEATS], acc_kv[blk, PAIR + HEAD_DIM : PAIR + HEAD_DIM + 1, FEATS:]],
            axis=1,
        ) * float(HEAD_DIM)
        (dpack_own if blk < 2 else dpack_sib)[blk % 2] = pack_summary(acc_kv[blk, :PAIR], sums)


def inputs_kernel(me_ref, x_ref, k_ref, v_ref, phi_ref, grad_ref, pack_own, pack_sib,
                  norm_ref, w_ref, dirs, norm_masked,
                  i_own, i_near, i_far, rows_grad, norm_sums, summ, mixed, norm_grad):
    for blk in range(4):
        summ[blk] = summary_matrix(pack_own if blk < 2 else pack_sib, blk % 2)
    norm_grad[...] = jnp.zeros_like(norm_grad)
    wide = 2 * PAIR
    gain = norm_ref[0:1, :]

    def step(i, carry):
        rows = pl.ds(pl.multiple_of(i * TILE, TILE), TILE)
        da = jnp.zeros((TILE, D), f32)
        for blk in range(4):
            cols = slice(blk * PAIR, (blk + 1) * PAIR)
            v = v_ref[rows, cols]
            ext = jnp.concatenate([v, jnp.full(v.shape, 1.0 / HEAD_DIM, b16)], axis=1)
            phi = phi_ref[rows, blk * 2 * FEATS : (blk + 1) * 2 * FEATS]
            d_exp = mm(ext, summ[blk]) * phi.astype(f32)
            dp = (SCALE * d_exp).astype(b16)
            lin = mm_nt(dp, dirs[...])
            left = jnp.sum(d_exp[:, :FEATS], axis=1, keepdims=True)
            right = jnp.sum(d_exp[:, FEATS:], axis=1, keepdims=True)
            first = lax.broadcasted_iota(jnp.int32, lin.shape, 1) < HEAD_DIM
            k = k_ref[rows, cols].astype(f32)
            dk = (lin - (SCALE * SCALE) * k * jnp.where(first, left, right)).astype(b16)
            dv = mm_nt(phi, summ[blk, :PAIR, :]).astype(b16)
            grads = jnp.concatenate([dk, dv], axis=1)
            rows_grad[rows, blk * wide : (blk + 1) * wide] = grads
            da = da + mm_nt(grads, w_ref[blk, :, PAIR : 3 * PAIR])
        normed, scale = layer_stats(x_ref[rows, :].astype(f32))
        norm_grad[0:8, :] += jnp.sum((da * normed).reshape(TILE // 8, 8, D), axis=0)
        norm_grad[8:16, :] += jnp.sum(da.reshape(TILE // 8, 8, D), axis=0)
        grad = grad_ref[rows, :].astype(f32) + layer_back(da, normed, scale, gain)
        mixed[rows, :] = grad.astype(b16)
        return carry

    lax.fori_loop(0, x_ref.shape[0] // TILE, step, 0)
    spread_columns(mixed, i_own, i_near, i_far, me_ref[0])
    for i in range(4):
        row = norm_masked[i : i + 1, :]
        if i < 2:
            row = row + jnp.sum(norm_grad[i * 8 : i * 8 + 8, :], axis=0, keepdims=True)
        norm_sums[i : i + 1, :] = row[:, : D // 2]
        norm_sums[4 + i : 5 + i, :] = row[:, D // 2 :]


def weights_kernel(a_ref, rows_grad, norm_sums, keep, send):
    wide = 2 * PAIR
    for blk in (2, 3, 0, 1):
        grad = mm_tn(a_ref[...], rows_grad[:, blk * wide : (blk + 1) * wide])
        if blk < 2:
            keep[blk * D : (blk + 1) * D] = grad
        else:
            send[(blk - 2) * D : (blk - 1) * D] = grad.astype(b16)
    send[2 * D :] = two_parts(norm_sums[...])


def coarse(values):
    return lax.reduce_precision(values, exponent_bits=8, mantissa_bits=7)


def two_parts(values):
    high = values.astype(b16)
    return jnp.concatenate([high, (values - high.astype(f32)).astype(b16)], axis=0)


def call(kernel, name, outs, scratch, micros, args, smem=(), vmem=20):
    specs = [
        pl.BlockSpec(memory_space=pltpu.SMEM if i in smem else pltpu.VMEM) for i in range(len(args))
    ]
    return pl.pallas_call(
        kernel,
        name=name,
        out_shape=outs,
        in_specs=specs,
        out_specs=[pl.BlockSpec(memory_space=pltpu.VMEM)] * len(outs),
        scratch_shapes=scratch,
        compiler_params=pltpu.CompilerParams(vmem_limit_bytes=vmem * MIB),
        cost_estimate=pl.CostEstimate(flops=int(micros * US), bytes_accessed=1_000, transcendentals=0),
    )(*args)


def shape(dims, dtype=b16):
    return jax.ShapeDtypeStruct(dims, dtype)


def swap(block, rows=0, heads=0):
    count = lax.axis_size("heads")
    if rows == 0:
        return lax.ppermute(block, "heads", [(i, i ^ heads) for i in range(count)])
    total = lax.axis_size("rows")
    if heads == 0:
        return lax.ppermute(block, "rows", [(i, i ^ rows) for i in range(total)])
    pairs = [
        (r * count + h, (r ^ rows) * count + (h ^ heads)) for r in range(total) for h in range(count)
    ]
    return lax.ppermute(block, ("rows", "heads"), pairs)


def bit_of(axis, bit):
    return (lax.axis_index(axis) >> bit) & 1


def sort_blocks(blocks, low_bits):
    blocks = list(blocks)
    for i, low in enumerate(low_bits):
        for d in range(len(blocks)):
            if d >> i & 1 == 0:
                one, two = blocks[d], blocks[d | 1 << i]
                blocks[d] = jnp.where(low, one, two)
                blocks[d | 1 << i] = jnp.where(low, two, one)
    return blocks


def tie(value, *others):
    return lax.optimization_barrier((value,) + others)[0]


def row_bits():
    return lax.axis_size("rows").bit_length() - 1


def chunks_of_bits():
    high = row_bits()
    groups = []
    while high > 1:
        width = min(2, high - 1)
        high -= width
        groups.append((high, width))
    return groups


def widen_bit(block, axis, bit, at, after=()):
    other = swap(block, rows=1 << bit) if axis == "rows" else swap(block, heads=1 << bit)
    other = tie(other, *after)
    return jnp.stack(sort_blocks([block, other], [bit_of(axis, bit) == 0]), axis=at)


def widen_high(block, at, after=()):
    for low, width in chunks_of_bits():
        got = [block] + [tie(swap(block, rows=d << low), *after) for d in range(1, 1 << width)]
        lows = [bit_of("rows", low + i) == 0 for i in range(width)]
        block = jnp.stack(sort_blocks(got, lows), axis=at)
        at += 1
    return block


def widen_square(block):
    got = [block, swap(block, rows=1), swap(block, heads=2), swap(block, rows=1, heads=2)]
    got = sort_blocks(got, [bit_of("rows", 0) == 0, bit_of("heads", 1) == 0])
    at = block.ndim - 2
    sides = [jnp.stack(got[:2], axis=at), jnp.stack(got[2:], axis=at)]
    return jnp.stack(sides).reshape(2, D, block.shape[-1])


def split_half(total, axis, bit, at):
    mine = bit_of(axis, bit)
    return (lax.dynamic_index_in_dim(total, mine, at, keepdims=False),
            lax.dynamic_index_in_dim(total, 1 - mine, at, keepdims=False))


def halve(total, axis, bit, at, after=()):
    here, away = split_half(total, axis, bit, at)
    other = swap(away, rows=1 << bit) if axis == "rows" else swap(away, heads=1 << bit)
    return add_low(here, tie(other, *after))


def add_low(one, two):
    return (one.astype(f32) + two.astype(f32)).astype(b16)


def spread_sum(total, beside):
    sent = total.astype(b16)
    got = [tie(swap(sent, rows=rows, heads=heads), *beside) for rows, heads in ((1, 0), (0, 2), (1, 2))]
    for block in got:
        total = total + block.astype(f32)
    total = total.astype(b16)
    return total, swap(total, heads=1)


def add_parts(sums, got):
    tail = sums.shape[0]
    return sums + (got[-2 * tail : -tail].astype(f32) + got[-tail:].astype(f32))


def add_sibling(keep, send, sums, beside):
    got = tie(swap(send, heads=1), beside)
    total = keep + got[: -2 * sums.shape[0]].astype(f32)
    return total.reshape((2,) * (1 + row_bits()) + (D >> row_bits(), keep.shape[1])), add_parts(sums, got)


def sum_stage(total, sums, axis, bit, at, after=()):
    wide = total.shape[-1]
    mine = bit_of(axis, bit)
    away = lax.dynamic_index_in_dim(total, 1 - mine, at, keepdims=False).astype(b16).reshape(-1, wide)
    total = lax.dynamic_index_in_dim(total, mine, at, keepdims=False)
    high = coarse(sums)
    away = jnp.concatenate([away, high.astype(b16), (sums - high).astype(b16)], axis=0)
    got = tie(swap(away, rows=1 << bit) if axis == "rows" else swap(away, heads=1 << bit), *after)
    total = total + got[: -2 * sums.shape[0]].reshape(total.shape).astype(f32)
    return total, add_parts(sums, got)


def side_rows(block):
    parts = block.reshape(2, block.shape[0] // 2, block.shape[1])
    return lax.dynamic_index_in_dim(parts, 1 - bit_of("heads", 1), 0, keepdims=False)


def near_rows(block, side):
    core = bit_of("heads", 0)
    n = block.shape[0] // 4
    own = lax.dynamic_slice_in_dim(block, (2 * bit_of("heads", 1) + 1 - core) * n, n, 0)
    return jnp.stack([own, lax.dynamic_slice_in_dim(side, (1 - core) * n, n, 0)])


def join_rows(own, near, side, dtype):
    got = sort_blocks([own, near[0], side[0], side[1]], [bit_of("heads", 0) == 0, bit_of("heads", 1) == 0])
    return jnp.concatenate(got, axis=0).astype(dtype)


def mask_ranks(masked_pos, masked_count, rows_dev, n):
    group = lax.axis_index("rows")
    offset = group % SPAN * rows_dev + lax.axis_index("heads") * n
    place = lax.dynamic_index_in_dim(masked_pos, group // SPAN, 0, keepdims=False) - offset
    limit = lax.dynamic_index_in_dim(masked_count, group // SPAN, 0, keepdims=False)
    inside = (jnp.arange(place.shape[0], dtype=jnp.int32) < limit) & (place >= 0) & (place < n)
    side = 32
    grid = jnp.arange(side, dtype=jnp.int32)[None, :]
    high = ((place // side)[:, None] == grid) & inside[:, None]
    low = (place % side)[:, None] == grid
    hits = mm_tn(high.astype(b16), low.astype(b16))
    marks = jnp.minimum(hits, 1.0)
    lower = grid < grid.T
    within = mm_nt(marks.astype(b16), lower.astype(b16))
    rows = jnp.sum(marks, axis=1)
    before = jnp.sum(jnp.where(lower, rows[None, :], 0.0), axis=1)
    rank = jnp.where(marks > 0, within + before[:, None], -1.0).astype(jnp.int32)
    count = jnp.sum(rows).astype(jnp.int32)
    return rank.reshape(1, n), count.reshape(1)


def body(
    tokens,
    ln1_gain,
    ln1_bias,
    qkv_weight,
    out_weight,
    ln2_gain,
    ln2_bias,
    ffn_in,
    ffn_out,
    feature_proj,
    masked_pos,
    masked_count,
    out_grad,
):
    rows_dev = tokens.shape[0]
    n = rows_dev // 4
    hidden = ffn_out.shape[0]
    narrow = ffn_out.shape[1]
    bits = row_bits()
    groups = len(chunks_of_bits())
    me = lax.axis_index("heads").astype(jnp.int32).reshape(1)

    x_cut = side_rows(tokens)
    x_side = swap(x_cut, heads=2)
    shard = jnp.concatenate([tie(qkv_weight, x_cut).transpose(2, 0, 1).reshape(narrow, -1), out_weight.T], axis=1)
    shard = widen_bit(widen_high(shard, 0), "rows", 0, groups)
    both = jnp.concatenate([tie(ffn_in, x_cut).T, ffn_out.T], axis=1)
    both = widen_bit(both, "heads", 1, 0)
    gains = tie(jnp.stack([ln1_gain, ln1_bias, ln2_gain, ln2_bias]), x_cut)
    gains_side = swap(gains, heads=2)
    x_side, shard, both, gains_side = lax.optimization_barrier((x_side, shard, both, gains_side))

    attn_own = widen_bit(shard, "heads", 1, 0).reshape(2, D, 4 * PAIR)
    fin = widen_high(both[:, :, :hidden], 1)
    fo = widen_bit(both[:, :, hidden:], "rows", 0, 1)
    dy_cut = side_rows(tie(out_grad, x_side))
    rank_row, count = mask_ranks(tie(masked_pos, x_side), masked_count, rows_dev, n)
    zero = jnp.zeros_like(feature_proj)
    dirs = tie(feature_proj, x_side)
    dirs = jnp.concatenate([jnp.concatenate([dirs, zero], 1), jnp.concatenate([zero, dirs], 1)], 0)
    near = near_rows(tokens, x_side)
    attn_own, fin, fo, dirs, dy_cut, rank_row, count, near = lax.optimization_barrier(
        (attn_own, fin, fo, dirs, dy_cut, rank_row, count, near)
    )

    attn_sib = swap(attn_own, heads=1)
    x_near = swap(near, heads=1)
    gains_near = swap(jnp.stack([gains, gains_side]), heads=1)
    x, a, norms = call(
        norm_kernel, "norm", [shape((n, D)), shape((n, D)), shape((4, D), f32)], [], 1,
        [me, tokens, x_side, x_near, gains, gains_side, gains_near], smem=(0,),
    )
    k, v, phi_k, kv_own, kv_sib, w_attn = call(
        keys_kernel, "keys",
        [shape((n, D)), shape((n, D)), shape((n, 4 * D)), shape((2, PACK, D)), shape((2, PACK, D)),
         shape((4, D, 4 * PAIR))],
        [pltpu.VMEM((4, PAIR, D), f32), pltpu.VMEM((4, 8, D), f32)],
        4, [a, attn_own, attn_sib, dirs],
    )
    fin_own = widen_bit(fin, "rows", 0, 1 + groups, (k,)).reshape(2, D, hidden)
    fo = widen_bit(fo, "rows", bits - 1, 1, (k,))
    dy_side = tie(swap(dy_cut, heads=2), k)
    kv_total = kv_own.astype(f32) + swap(kv_sib, heads=1).astype(f32)
    kv_total, fin_own, fo, dy_side = lax.optimization_barrier((kv_total, fin_own, fo, dy_side))

    (phi_q,) = call(
        queries_kernel, "queries", [shape((n, 4 * D))], [], 3, [tie(a, kv_total), w_attn, dirs],
    )
    fin_sib = swap(fin_own, heads=1)
    kv_own, kv_sib = spread_sum(kv_total, (phi_q,))
    high, low = call(
        attention_kernel, "attention", [shape((n, D)), shape((n, D))],
        [pltpu.VMEM((4, 256, D), b16), pltpu.VMEM((D, D), b16)],
        2, [x, phi_q, kv_own, kv_sib, w_attn],
    )
    for step in range(1, bits - 1):
        fo = widen_bit(fo, "rows", bits - 1 - step, 1 + step, (high,))
    fo_own = fo.reshape(2, D, hidden)
    fo_sib = swap(fo_own, heads=1)
    dy_near = swap(near_rows(out_grad, tie(dy_side, kv_own)), heads=1)
    ino_keep, ino_send, foq_keep, foq_send, dkv_own, dkv_sib, masked_grad, norm_grad = call(
        masked_kernel, "masked",
        [shape((2, D, hidden + PAIR))] * 4 + [
         shape((2, PACK, D)), shape((2, PACK, D)), shape((n, D)), shape((4, D), f32)],
        [pltpu.VMEM((n, D), b16), pltpu.VMEM((4, 256, D), b16), pltpu.VMEM((D, D), b16),
         pltpu.VMEM((4, D, hidden), b16), pltpu.VMEM((4, D, hidden), b16),
         pltpu.VMEM((4, 256, D), f32), pltpu.VMEM((MASK_TILE, D), f32), pltpu.VMEM((4, MASK_TILE, PAIR), f32)],
        18,
        [me, count, rank_row, high, low, x, out_grad, dy_side, dy_near, norms, fin_own, fin_sib, fo_own, fo_sib,
         w_attn, kv_own, kv_sib, dirs],
        smem=(0, 1), vmem=26,
    )

    dkv_total = dkv_own.astype(f32) + swap(dkv_sib, heads=1).astype(f32)
    blocks = (2,) * (1 + bits) + (narrow, hidden + PAIR)
    gino = add_low(ino_keep, swap(tie(ino_send, dkv_total), heads=1)).reshape(blocks)
    gfoq = add_low(foq_keep, swap(tie(foq_send, dkv_total), heads=1)).reshape(blocks)
    dkv_own, dkv_sib = spread_sum(dkv_total, (gino, gfoq))
    gino, ino_away = split_half(gino, "rows", 0, bits)
    gfoq, foq_away = split_half(gfoq, "heads", 1, 0)
    i_own, i_near, i_far, rows_grad, norm_sums = call(
        inputs_kernel, "inputs",
        [shape((n, PAIR)), shape((2, n, PAIR)), shape((n, PAIR)), shape((n, 2 * D)), shape((8, D // 2), f32)],
        [pltpu.VMEM((4, 256, D), b16), pltpu.VMEM((n, D), b16), pltpu.VMEM((16, D), f32)],
        6,
        [me, tie(x, gino, gfoq, ino_away, foq_away), k, v, phi_k, masked_grad, dkv_own, dkv_sib, norms, w_attn, dirs, norm_grad],
        smem=(0,),
    )
    keep, send = call(
        weights_kernel, "weights",
        [shape((2 * D, 2 * PAIR), f32), shape((2 * D + 16, 2 * PAIR))], [],
        1.3, [a, rows_grad, norm_sums],
    )
    i_near = swap(i_near, heads=1)
    m_own, m_near, m_far = call(
        forward_kernel, "forward", [shape((n, PAIR)), shape((2, n, PAIR)), shape((n, PAIR))],
        [pltpu.VMEM((n, D), b16), pltpu.VMEM((FORWARD_TILE, D), b16), pltpu.VMEM((FORWARD_TILE, D), f32)], 6,
        [me, tie(high, send), low, norms, fin_own, fin_sib, fo_own, fo_sib], smem=(0,),
    )
    total, norm_sums = add_sibling(keep, send, norm_sums, m_own)
    gino = add_low(gino, tie(swap(ino_away, rows=1), m_own))
    gfoq = add_low(gfoq, tie(swap(foq_away, heads=2), m_own))
    total, norm_sums, gino, gfoq, i_near, m_near = lax.optimization_barrier(
        (total, norm_sums, gino, gfoq, i_near, m_near)
    )
    i_side = swap(jnp.stack([i_far, i_near[1]]), heads=2)

    m_near = swap(m_near, heads=1)
    total, norm_sums = sum_stage(total, norm_sums, "heads", 1, 0)
    gino = halve(gino, "rows", 1, bits - 1)
    gfoq = halve(gfoq, "rows", 0, bits - 1)
    total, norm_sums, gino, gfoq, m_near = lax.optimization_barrier((total, norm_sums, gino, gfoq, m_near))
    m_side = swap(jnp.stack([m_far, m_near[1]]), heads=2)
    total, norm_sums = sum_stage(total, norm_sums, "rows", 0, bits - 1)
    for step in range(2, bits):
        gino = halve(gino, "rows", step, bits - step)
    gfoq = halve(gfoq, "rows", 1, bits - 2)
    total, norm_sums, gino, gfoq, i_side = lax.optimization_barrier((total, norm_sums, gino, gfoq, i_side))
    gino = halve(gino, "heads", 1, 0)
    for step in range(2, bits):
        gfoq = halve(gfoq, "rows", step, bits - 1 - step)
    for step in range(1, bits):
        total, norm_sums = sum_stage(total, norm_sums, "rows", step, bits - 1 - step)
    gkv = total
    mixed_out = join_rows(m_own, m_near, m_side, b16)
    input_grad = join_rows(i_own, i_near, i_side, f32)
    head = lax.axis_index("heads")
    mine = lax.dynamic_slice(norm_sums, (4 * (head // 2), PAIR * (head % 2)), (4, PAIR))
    gqkv = jnp.stack([gfoq[:, hidden:].T.astype(f32), gkv[:, :PAIR].T, gkv[:, PAIR:].T])

    return (
        mixed_out,
        input_grad,
        gqkv,
        gino[:, hidden:].T.astype(f32),
        gino[:, :hidden].T.astype(f32),
        gfoq[:, :hidden].T.astype(f32),
        mine[0],
        mine[1],
        mine[2],
        mine[3],
    )


def solution(mesh):
    in_specs = (
        P("rows", "heads"),
        P("heads"),
        P("heads"),
        P(None, "heads", "rows"),
        P("heads", "rows"),
        P("heads"),
        P("heads"),
        P("heads", "rows"),
        P("heads", "rows"),
        P(),
        P(),
        P(),
        P("rows", "heads"),
    )
    out_specs = (
        P("rows", "heads"),
        P("rows", "heads"),
        P(None, "heads", "rows"),
        P("heads", "rows"),
        P("heads", "rows"),
        P("heads", "rows"),
        P("heads"),
        P("heads"),
        P("heads"),
        P("heads"),
    )
    return jax.shard_map(body, mesh=mesh, in_specs=in_specs, out_specs=out_specs, check_vma=False)
```

```python
import functools
import math

import jax
import jax.numpy as jnp
from jax import lax
from jax.experimental import pallas as pl
from jax.experimental.pallas import tpu as pltpu
from jax.sharding import PartitionSpec as P

D = 512
HEAD_DIM = 64
FEATS = 256
PAIR = 2 * HEAD_DIM
SPAN = 2
PACK = 72
SCALE = HEAD_DIM ** (-0.25)
HALF_SQ = 0.5 * SCALE * SCALE
LOG2E = math.log2(math.e)
LOG2_ROOT = 0.5 * math.log2(FEATS)
epsilon = 1e-05
f32 = jnp.float32
b16 = jnp.bfloat16
MIB = 1024 * 1024
TILE = 1024
FORWARD_TILE = 512
SMALL_TILE = 256
MASK_TILE = 304
US = 1.15e9


def mm(left, right):
    return lax.dot_general(left, right, (((1,), (0,)), ((), ())), preferred_element_type=f32)


def mm_nt(left, right):
    return lax.dot_general(left, right, (((1,), (1,)), ((), ())), preferred_element_type=f32)


def mm_tn(left, right):
    return lax.dot_general(left, right, (((0,), (0,)), ((), ())), preferred_element_type=f32)


def layer_stats(values):
    mean = jnp.sum(values, axis=1, keepdims=True) * (1.0 / D)
    centred = values - mean
    var = jnp.sum(centred * centred, axis=1, keepdims=True) * (1.0 / D)
    scale = lax.rsqrt(var + epsilon)
    return centred * scale, scale


def layer_back(grad, normed, scale, gain):
    scaled = grad * gain
    first = jnp.sum(scaled, axis=1, keepdims=True) * (1.0 / D)
    second = jnp.sum(scaled * normed, axis=1, keepdims=True) * (1.0 / D)
    return scale * (scaled - first - normed * second)


def features(rows, directions):
    projected = mm(rows, directions)
    wide = rows.astype(f32)
    square = wide * wide
    first = lax.broadcasted_iota(jnp.int32, square.shape, 1) < HEAD_DIM
    left = jnp.sum(jnp.where(first, square, 0.0), axis=1, keepdims=True)
    right = jnp.sum(jnp.where(first, 0.0, square), axis=1, keepdims=True)
    return jnp.concatenate(
        [
            jnp.exp2((SCALE * LOG2E) * projected[:, :FEATS] - (HALF_SQ * LOG2E * left + LOG2_ROOT)),
            jnp.exp2((SCALE * LOG2E) * projected[:, FEATS:] - (HALF_SQ * LOG2E * right + LOG2_ROOT)),
        ],
        axis=1,
    )


def normal_cdf(u):
    return 0.5 + 0.5 * lax.erf(u * math.sqrt(0.5))


def summary_matrix(packed, blk):
    half = packed[blk]
    zero = jnp.zeros((HEAD_DIM, FEATS), b16)
    top = jnp.concatenate([half[:HEAD_DIM, :FEATS], zero], axis=1)
    low = jnp.concatenate([zero, half[:HEAD_DIM, FEATS:]], axis=1)
    sums = half[HEAD_DIM : HEAD_DIM + 1].astype(f32)
    rows = jnp.broadcast_to(sums, (HEAD_DIM, 2 * FEATS))
    left = lax.broadcasted_iota(jnp.int32, rows.shape, 1) < FEATS
    return jnp.concatenate(
        [
            top,
            low,
            jnp.where(left, rows, 0.0).astype(b16),
            jnp.where(left, 0.0, rows).astype(b16),
        ],
        axis=0,
    )


def pack_summary(matrix, sums):
    kept = jnp.concatenate([matrix[:HEAD_DIM, :FEATS], matrix[HEAD_DIM:PAIR, FEATS:]], axis=1)
    return jnp.concatenate(
        [kept.astype(b16), jnp.broadcast_to(sums, (PACK - HEAD_DIM, 2 * FEATS)).astype(b16)], axis=0
    )


def block_of(own, sib, blk):
    return own[blk] if blk < 2 else sib[blk - 2]


def gather_columns(block, side, near, target, me):
    n = target.shape[0]
    parts = (
        block[pl.ds(pl.multiple_of(me * n, n), n), :],
        near[0, :n, :],
        side[pl.ds(pl.multiple_of((me & 1) * n, n), n), :],
        near[1, :n, :],
    )
    for j in range(4):
        target[:, pl.ds(pl.multiple_of((me ^ j) * PAIR, PAIR), PAIR)] = parts[j]


def spread_columns(source, own, near, far, me):
    def columns(j):
        return source[:, pl.ds(pl.multiple_of((me ^ j) * PAIR, PAIR), PAIR)]

    own[...] = columns(0)
    near[0] = columns(1)
    near[1] = columns(3)
    far[...] = columns(2)


def norm_kernel(me_ref, block, side, near, gains, gains_side, gains_near, x_ref, a_ref, norm_ref):
    gather_columns(block, side, near, x_ref, me_ref[0])
    for j, part in enumerate((gains[...], gains_near[0], gains_side[...], gains_near[1])):
        norm_ref[:, pl.ds(pl.multiple_of((me_ref[0] ^ j) * PAIR, PAIR), PAIR)] = part

    def step(i, carry):
        rows = pl.ds(pl.multiple_of(i * SMALL_TILE, SMALL_TILE), SMALL_TILE)
        normed, _ = layer_stats(x_ref[rows, :].astype(f32))
        a_ref[rows, :] = (normed * norm_ref[0:1, :] + norm_ref[1:2, :]).astype(b16)
        return carry

    lax.fori_loop(0, x_ref.shape[0] // SMALL_TILE, step, 0)


def keys_kernel(a_ref, own, sib, dirs, k_ref, v_ref, phi_ref, pack_own, pack_sib, w_ref, acc, sums):
    for blk in range(4):
        w_ref[blk] = block_of(own, sib, blk)
    acc[...] = jnp.zeros_like(acc)
    sums[...] = jnp.zeros_like(sums)

    def step(i, carry):
        rows = pl.ds(pl.multiple_of(i * TILE, TILE), TILE)
        a = a_ref[rows, :]
        def block(blk, carry):
            kv = mm(a, w_ref[blk, :, PAIR : 3 * PAIR]).astype(b16)
            k, v = kv[:, :PAIR], kv[:, PAIR:]
            cols = pl.ds(pl.multiple_of(blk * PAIR, PAIR), PAIR)
            k_ref[rows, cols] = k
            v_ref[rows, cols] = v
            phi = features(k, dirs[...]).astype(b16)
            phi_ref[rows, pl.ds(pl.multiple_of(blk * 2 * FEATS, 2 * FEATS), 2 * FEATS)] = phi
            acc[blk] += mm_tn(v, phi)
            sums[blk] += jnp.sum(phi.astype(f32).reshape(TILE // 8, 8, 2 * FEATS), axis=0)
            return carry

        lax.fori_loop(0, 4, block, 0, unroll=1)
        return carry

    lax.fori_loop(0, a_ref.shape[0] // TILE, step, 0)
    for blk in range(4):
        packed = pack_summary(acc[blk], jnp.sum(sums[blk], axis=0, keepdims=True))
        (pack_own if blk < 2 else pack_sib)[blk % 2] = packed


def queries_kernel(a_ref, w_ref, dirs, phi_ref):
    def step(blk, carry):
        q = mm(a_ref[...], w_ref[blk, :, :PAIR]).astype(b16)
        cols = pl.ds(pl.multiple_of(blk * 2 * FEATS, 2 * FEATS), 2 * FEATS)
        phi_ref[:, cols] = features(q, dirs[...]).astype(b16)
        return carry

    lax.fori_loop(0, 4, step, 0)


def attention_kernel(x_ref, phi_ref, pack_own, pack_sib, w_ref, hi_ref, lo_ref, summ, wout):
    for blk in range(4):
        summ[blk] = summary_matrix(pack_own if blk < 2 else pack_sib, blk % 2)
        wout[:, blk * PAIR : (blk + 1) * PAIR] = w_ref[blk, :, 3 * PAIR :]

    def step(i, carry):
        rows = pl.ds(pl.multiple_of(i * SMALL_TILE, SMALL_TILE), SMALL_TILE)
        heads = []
        for blk in range(4):
            both = mm_nt(phi_ref[rows, blk * 2 * FEATS : (blk + 1) * 2 * FEATS], summ[blk])
            heads.append((both[:, :PAIR] / both[:, PAIR:]).astype(b16))
        hidden = x_ref[rows, :].astype(f32) + mm_nt(jnp.concatenate(heads, axis=1), wout[...])
        high = hidden.astype(b16)
        hi_ref[rows, :] = high
        lo_ref[rows, :] = (hidden - high.astype(f32)).astype(b16)
        return carry

    lax.fori_loop(0, x_ref.shape[0] // SMALL_TILE, step, 0)


def forward_kernel(me_ref, hi_ref, lo_ref, norm_ref, in_own, in_sib, out_own, out_sib, m_own, m_near, m_far, mixed,
                   low_ref, sum_ref):
    def step(i, carry):
        rows = pl.ds(pl.multiple_of(i * FORWARD_TILE, FORWARD_TILE), FORWARD_TILE)
        hidden = hi_ref[rows, :].astype(f32) + lo_ref[rows, :].astype(f32)
        normed, _ = layer_stats(hidden)
        low_ref[...] = (normed * norm_ref[2:3, :] + norm_ref[3:4, :]).astype(b16)
        sum_ref[...] = hidden
        for w_in, w_out in ((in_own, out_own), (in_sib, out_sib)):

            def block(blk, carry, w_in=w_in, w_out=w_out):
                u = mm(low_ref[...], w_in[blk])
                g = (u * normal_cdf(u)).astype(b16)
                sum_ref[...] += mm_nt(g, w_out[blk])
                return carry

            lax.fori_loop(0, 2, block, 0, unroll=True)
        mixed[rows, :] = sum_ref[...].astype(b16)
        return carry

    lax.fori_loop(0, hi_ref.shape[0] // FORWARD_TILE, step, 0)
    spread_columns(mixed, m_own, m_near, m_far, me_ref[0])


def masked_kernel(me_ref, count_ref, rank_row, hi_ref, lo_ref, x_ref, dy_block, dy_side, dy_near, norm_ref,
                  in_own, in_sib, fo_own, fo_sib, w_ref, pack_own, pack_sib, dirs,
                  ino_keep, ino_send, foq_keep, foq_send, dpack_own, dpack_sib, grad_ref, norm_grad,
                  dy_ref, summ, wout, w_in, w_fo, acc_kv, dc_ref, dmix_ref):
    hidden = fo_own.shape[2]
    total = rank_row.shape[1]
    gather_columns(dy_block, dy_side, dy_near, dy_ref, me_ref[0])
    for blk in range(4):
        summ[blk] = summary_matrix(pack_own if blk < 2 else pack_sib, blk % 2)
        wout[:, blk * PAIR : (blk + 1) * PAIR] = w_ref[blk, :, 3 * PAIR :]
        w_in[blk] = block_of(in_own, in_sib, blk)
        w_fo[blk] = block_of(fo_own, fo_sib, blk)
    gain = norm_ref[2:3, :]

    def step(tile, carry):
        def put(ref, at, value):
            before = jnp.where(tile > 0, ref[at].astype(f32), 0.0)
            ref[at] = (before + value).astype(ref.dtype)

        base = tile * MASK_TILE
        slots = base + lax.broadcasted_iota(jnp.int32, (MASK_TILE, total), 0)
        pick = jnp.where(rank_row[...] == slots, 1.0, 0.0).astype(b16)
        h_m = mm(pick, hi_ref[...]) + mm(pick, lo_ref[...])
        first_normed, first_scale = layer_stats(mm(pick, x_ref[...]))
        a_m = (first_normed * norm_ref[0:1, :] + norm_ref[1:2, :]).astype(b16)
        dy = mm(pick, dy_ref[...])
        dy_low = dy.astype(b16)
        normed, scale = layer_stats(h_m)
        c = (normed * gain + norm_ref[3:4, :]).astype(b16)
        dc_ref[...] = jnp.zeros_like(dc_ref)

        def hidden_block(ino, foq, half, i, carry):
            blk = 2 * half + i
            u = mm(c, w_in[blk])
            phi = normal_cdf(u)
            g = (u * phi).astype(b16)
            slope = phi + u * (jnp.exp(-0.5 * u * u) * (1.0 / math.sqrt(2.0 * math.pi)))
            du = (mm(dy_low, w_fo[blk]) * slope).astype(b16)
            dc_ref[...] += mm_nt(du, w_in[blk])
            put(foq, (i, slice(None), slice(0, hidden)), mm_tn(dy_low, g))
            put(ino, (i, slice(None), slice(0, hidden)), mm_tn(c, du))
            return carry

        lax.fori_loop(0, 2, functools.partial(hidden_block, ino_keep, foq_keep, 0), 0, unroll=True)
        lax.fori_loop(0, 2, functools.partial(hidden_block, ino_send, foq_send, 1), 0, unroll=True)
        dc = dc_ref[...]
        put(norm_grad, slice(2, 3), jnp.sum(dc * normed, axis=0, keepdims=True))
        put(norm_grad, slice(3, 4), jnp.sum(dc, axis=0, keepdims=True))
        dh = dy + layer_back(dc, normed, scale, gain)
        dattn = dh.astype(b16)
        dmix = mm(dattn, wout[...])
        for blk in range(4):
            dmix_ref[blk] = dmix[:, blk * PAIR : (blk + 1) * PAIR]
        dc_ref[...] = jnp.zeros_like(dc_ref)

        def head_block(ino, foq, half, i, carry):
            blk = 2 * half + i
            q = mm(a_m, w_ref[blk, :, :PAIR]).astype(b16)
            eq = features(q, dirs[...])
            phi_q = eq.astype(b16)
            both = mm_nt(phi_q, summ[blk])
            num, den = both[:, :PAIR], both[:, PAIR:]
            inverse = 1.0 / den
            o = (num * inverse).astype(b16)
            put(ino, (i, slice(None), slice(hidden, hidden + PAIR)), mm_tn(dattn, o))
            do = dmix_ref[blk]
            dnum = (do * inverse).astype(b16)
            prod = do * num
            first = lax.broadcasted_iota(jnp.int32, prod.shape, 1) < HEAD_DIM
            left = jnp.sum(jnp.where(first, prod, 0.0), axis=1, keepdims=True)
            right = jnp.sum(jnp.where(first, 0.0, prod), axis=1, keepdims=True)
            dden = (-jnp.where(first, left, right) * inverse * inverse).astype(b16)
            ext = jnp.concatenate([dnum, (dden.astype(f32) * (1.0 / HEAD_DIM)).astype(b16)], axis=1)
            put(acc_kv, blk, mm_tn(ext, phi_q))
            d_exp = mm(ext, summ[blk]) * eq
            dp = (SCALE * d_exp).astype(b16)
            lin = mm_nt(dp, dirs[...])
            left = jnp.sum(d_exp[:, :FEATS], axis=1, keepdims=True)
            right = jnp.sum(d_exp[:, FEATS:], axis=1, keepdims=True)
            dq = (lin - (SCALE * SCALE) * q.astype(f32) * jnp.where(first, left, right)).astype(b16)
            put(foq, (i, slice(None), slice(hidden, hidden + PAIR)), mm_tn(a_m, dq))
            dc_ref[...] += mm_nt(dq, w_ref[blk, :, :PAIR])
            return carry

        lax.fori_loop(0, 2, functools.partial(head_block, ino_keep, foq_keep, 0), 0, unroll=True)
        lax.fori_loop(0, 2, functools.partial(head_block, ino_send, foq_send, 1), 0, unroll=True)
        da = dc_ref[...]
        put(norm_grad, slice(0, 1), jnp.sum(da * first_normed, axis=0, keepdims=True))
        put(norm_grad, slice(1, 2), jnp.sum(da, axis=0, keepdims=True))
        grad = dh + layer_back(da, first_normed, first_scale, norm_ref[0:1, :])
        put(grad_ref, slice(None), mm_tn(pick, grad.astype(b16)))
        return carry

    lax.fori_loop(0, jnp.maximum((count_ref[0] + MASK_TILE - 1) // MASK_TILE, 1), step, 0)
    for blk in range(4):
        sums = jnp.concatenate(
            [acc_kv[blk, PAIR : PAIR + 1, :FEATS], acc_kv[blk, PAIR + HEAD_DIM : PAIR + HEAD_DIM + 1, FEATS:]],
            axis=1,
        ) * float(HEAD_DIM)
        (dpack_own if blk < 2 else dpack_sib)[blk % 2] = pack_summary(acc_kv[blk, :PAIR], sums)


def inputs_kernel(me_ref, x_ref, k_ref, v_ref, phi_ref, grad_ref, pack_own, pack_sib,
                  norm_ref, w_ref, dirs, norm_masked,
                  i_own, i_near, i_far, rows_grad, norm_sums, summ, mixed, norm_grad):
    for blk in range(4):
        summ[blk] = summary_matrix(pack_own if blk < 2 else pack_sib, blk % 2)
    norm_grad[...] = jnp.zeros_like(norm_grad)
    wide = 2 * PAIR
    gain = norm_ref[0:1, :]

    def step(i, carry):
        rows = pl.ds(pl.multiple_of(i * TILE, TILE), TILE)
        da = jnp.zeros((TILE, D), f32)
        for blk in range(4):
            cols = slice(blk * PAIR, (blk + 1) * PAIR)
            v = v_ref[rows, cols]
            ext = jnp.concatenate([v, jnp.full(v.shape, 1.0 / HEAD_DIM, b16)], axis=1)
            phi = phi_ref[rows, blk * 2 * FEATS : (blk + 1) * 2 * FEATS]
            d_exp = mm(ext, summ[blk]) * phi.astype(f32)
            dp = (SCALE * d_exp).astype(b16)
            lin = mm_nt(dp, dirs[...])
            left = jnp.sum(d_exp[:, :FEATS], axis=1, keepdims=True)
            right = jnp.sum(d_exp[:, FEATS:], axis=1, keepdims=True)
            first = lax.broadcasted_iota(jnp.int32, lin.shape, 1) < HEAD_DIM
            k = k_ref[rows, cols].astype(f32)
            dk = (lin - (SCALE * SCALE) * k * jnp.where(first, left, right)).astype(b16)
            dv = mm_nt(phi, summ[blk, :PAIR, :]).astype(b16)
            grads = jnp.concatenate([dk, dv], axis=1)
            rows_grad[rows, blk * wide : (blk + 1) * wide] = grads
            da = da + mm_nt(grads, w_ref[blk, :, PAIR : 3 * PAIR])
        normed, scale = layer_stats(x_ref[rows, :].astype(f32))
        norm_grad[0:8, :] += jnp.sum((da * normed).reshape(TILE // 8, 8, D), axis=0)
        norm_grad[8:16, :] += jnp.sum(da.reshape(TILE // 8, 8, D), axis=0)
        grad = grad_ref[rows, :].astype(f32) + layer_back(da, normed, scale, gain)
        mixed[rows, :] = grad.astype(b16)
        return carry

    lax.fori_loop(0, x_ref.shape[0] // TILE, step, 0)
    spread_columns(mixed, i_own, i_near, i_far, me_ref[0])
    for i in range(4):
        row = norm_masked[i : i + 1, :]
        if i < 2:
            row = row + jnp.sum(norm_grad[i * 8 : i * 8 + 8, :], axis=0, keepdims=True)
        norm_sums[i : i + 1, :] = row[:, : D // 2]
        norm_sums[4 + i : 5 + i, :] = row[:, D // 2 :]


def weights_kernel(a_ref, rows_grad, norm_sums, keep, send):
    wide = 2 * PAIR
    for blk in (2, 3, 0, 1):
        grad = mm_tn(a_ref[...], rows_grad[:, blk * wide : (blk + 1) * wide])
        if blk < 2:
            keep[blk * D : (blk + 1) * D] = grad
        else:
            send[(blk - 2) * D : (blk - 1) * D] = grad.astype(b16)
    send[2 * D :] = two_parts(norm_sums[...])


def coarse(values):
    return lax.reduce_precision(values, exponent_bits=8, mantissa_bits=7)


def two_parts(values):
    high = values.astype(b16)
    return jnp.concatenate([high, (values - high.astype(f32)).astype(b16)], axis=0)


def call(kernel, name, outs, scratch, micros, args, smem=(), vmem=20):
    specs = [
        pl.BlockSpec(memory_space=pltpu.SMEM if i in smem else pltpu.VMEM) for i in range(len(args))
    ]
    return pl.pallas_call(
        kernel,
        name=name,
        out_shape=outs,
        in_specs=specs,
        out_specs=[pl.BlockSpec(memory_space=pltpu.VMEM)] * len(outs),
        scratch_shapes=scratch,
        compiler_params=pltpu.CompilerParams(vmem_limit_bytes=vmem * MIB),
        cost_estimate=pl.CostEstimate(flops=int(micros * US), bytes_accessed=1_000, transcendentals=0),
    )(*args)


def shape(dims, dtype=b16):
    return jax.ShapeDtypeStruct(dims, dtype)


def swap(block, rows=0, heads=0):
    count = lax.axis_size("heads")
    if rows == 0:
        return lax.ppermute(block, "heads", [(i, i ^ heads) for i in range(count)])
    total = lax.axis_size("rows")
    if heads == 0:
        return lax.ppermute(block, "rows", [(i, i ^ rows) for i in range(total)])
    pairs = [
        (r * count + h, (r ^ rows) * count + (h ^ heads)) for r in range(total) for h in range(count)
    ]
    return lax.ppermute(block, ("rows", "heads"), pairs)


def bit_of(axis, bit):
    return (lax.axis_index(axis) >> bit) & 1


def sort_blocks(blocks, low_bits):
    blocks = list(blocks)
    for i, low in enumerate(low_bits):
        for d in range(len(blocks)):
            if d >> i & 1 == 0:
                one, two = blocks[d], blocks[d | 1 << i]
                blocks[d] = jnp.where(low, one, two)
                blocks[d | 1 << i] = jnp.where(low, two, one)
    return blocks


def tie(value, *others):
    return lax.optimization_barrier((value,) + others)[0]


def row_bits():
    return lax.axis_size("rows").bit_length() - 1


def chunks_of_bits():
    high = row_bits()
    groups = []
    while high > 1:
        width = min(2, high - 1)
        high -= width
        groups.append((high, width))
    return groups


def widen_bit(block, axis, bit, at, after=()):
    other = swap(block, rows=1 << bit) if axis == "rows" else swap(block, heads=1 << bit)
    other = tie(other, *after)
    return jnp.stack(sort_blocks([block, other], [bit_of(axis, bit) == 0]), axis=at)


def widen_high(block, at, after=()):
    for low, width in chunks_of_bits():
        got = [block] + [tie(swap(block, rows=d << low), *after) for d in range(1, 1 << width)]
        lows = [bit_of("rows", low + i) == 0 for i in range(width)]
        block = jnp.stack(sort_blocks(got, lows), axis=at)
        at += 1
    return block


def widen_square(block):
    got = [block, swap(block, rows=1), swap(block, heads=2), swap(block, rows=1, heads=2)]
    got = sort_blocks(got, [bit_of("rows", 0) == 0, bit_of("heads", 1) == 0])
    at = block.ndim - 2
    sides = [jnp.stack(got[:2], axis=at), jnp.stack(got[2:], axis=at)]
    return jnp.stack(sides).reshape(2, D, block.shape[-1])


def split_half(total, axis, bit, at):
    mine = bit_of(axis, bit)
    return (lax.dynamic_index_in_dim(total, mine, at, keepdims=False),
            lax.dynamic_index_in_dim(total, 1 - mine, at, keepdims=False))


def halve(total, axis, bit, at, after=()):
    here, away = split_half(total, axis, bit, at)
    other = swap(away, rows=1 << bit) if axis == "rows" else swap(away, heads=1 << bit)
    return add_low(here, tie(other, *after))


def add_low(one, two):
    return (one.astype(f32) + two.astype(f32)).astype(b16)


def spread_sum(total, beside):
    sent = total.astype(b16)
    got = [tie(swap(sent, rows=rows, heads=heads), *beside) for rows, heads in ((1, 0), (0, 2), (1, 2))]
    for block in got:
        total = total + block.astype(f32)
    total = total.astype(b16)
    return total, swap(total, heads=1)


def add_parts(sums, got):
    tail = sums.shape[0]
    return sums + (got[-2 * tail : -tail].astype(f32) + got[-tail:].astype(f32))


def add_sibling(keep, send, sums, beside):
    got = tie(swap(send, heads=1), beside)
    total = keep + got[: -2 * sums.shape[0]].astype(f32)
    return total.reshape((2,) * (1 + row_bits()) + (D >> row_bits(), keep.shape[1])), add_parts(sums, got)


def sum_stage(total, sums, axis, bit, at, after=()):
    wide = total.shape[-1]
    mine = bit_of(axis, bit)
    away = lax.dynamic_index_in_dim(total, 1 - mine, at, keepdims=False).astype(b16).reshape(-1, wide)
    total = lax.dynamic_index_in_dim(total, mine, at, keepdims=False)
    high = coarse(sums)
    away = jnp.concatenate([away, high.astype(b16), (sums - high).astype(b16)], axis=0)
    got = tie(swap(away, rows=1 << bit) if axis == "rows" else swap(away, heads=1 << bit), *after)
    total = total + got[: -2 * sums.shape[0]].reshape(total.shape).astype(f32)
    return total, add_parts(sums, got)


def side_rows(block):
    parts = block.reshape(2, block.shape[0] // 2, block.shape[1])
    return lax.dynamic_index_in_dim(parts, 1 - bit_of("heads", 1), 0, keepdims=False)


def near_rows(block, side):
    core = bit_of("heads", 0)
    n = block.shape[0] // 4
    own = lax.dynamic_slice_in_dim(block, (2 * bit_of("heads", 1) + 1 - core) * n, n, 0)
    return jnp.stack([own, lax.dynamic_slice_in_dim(side, (1 - core) * n, n, 0)])


def join_rows(own, near, side, dtype):
    got = sort_blocks([own, near[0], side[0], side[1]], [bit_of("heads", 0) == 0, bit_of("heads", 1) == 0])
    return jnp.concatenate(got, axis=0).astype(dtype)


def mask_ranks(masked_pos, masked_count, rows_dev, n):
    group = lax.axis_index("rows")
    offset = group % SPAN * rows_dev + lax.axis_index("heads") * n
    place = lax.dynamic_index_in_dim(masked_pos, group // SPAN, 0, keepdims=False) - offset
    limit = lax.dynamic_index_in_dim(masked_count, group // SPAN, 0, keepdims=False)
    inside = (jnp.arange(place.shape[0], dtype=jnp.int32) < limit) & (place >= 0) & (place < n)
    side = 32
    grid = jnp.arange(side, dtype=jnp.int32)[None, :]
    high = ((place // side)[:, None] == grid) & inside[:, None]
    low = (place % side)[:, None] == grid
    hits = mm_tn(high.astype(b16), low.astype(b16))
    marks = jnp.minimum(hits, 1.0)
    lower = grid < grid.T
    within = mm_nt(marks.astype(b16), lower.astype(b16))
    rows = jnp.sum(marks, axis=1)
    before = jnp.sum(jnp.where(lower, rows[None, :], 0.0), axis=1)
    rank = jnp.where(marks > 0, within + before[:, None], -1.0).astype(jnp.int32)
    count = jnp.sum(rows).astype(jnp.int32)
    return rank.reshape(1, n), count.reshape(1)


def body(
    tokens,
    ln1_gain,
    ln1_bias,
    qkv_weight,
    out_weight,
    ln2_gain,
    ln2_bias,
    ffn_in,
    ffn_out,
    feature_proj,
    masked_pos,
    masked_count,
    out_grad,
):
    rows_dev = tokens.shape[0]
    n = rows_dev // 4
    hidden = ffn_out.shape[0]
    narrow = ffn_out.shape[1]
    bits = row_bits()
    groups = len(chunks_of_bits())
    me = lax.axis_index("heads").astype(jnp.int32).reshape(1)

    x_cut = side_rows(tokens)
    x_side = swap(x_cut, heads=2)
    shard = jnp.concatenate([tie(qkv_weight, x_cut).transpose(2, 0, 1).reshape(narrow, -1), out_weight.T], axis=1)
    shard = widen_bit(widen_high(shard, 0), "rows", 0, groups)
    both = jnp.concatenate([tie(ffn_in, x_cut).T, ffn_out.T], axis=1)
    both = widen_bit(both, "heads", 1, 0)
    gains = tie(jnp.stack([ln1_gain, ln1_bias, ln2_gain, ln2_bias]), x_cut)
    gains_side = swap(gains, heads=2)
    x_side, shard, both, gains_side = lax.optimization_barrier((x_side, shard, both, gains_side))

    attn_own = widen_bit(shard, "heads", 1, 0).reshape(2, D, 4 * PAIR)
    fin = widen_high(both[:, :, :hidden], 1)
    fo = widen_bit(both[:, :, hidden:], "rows", 0, 1)
    dy_cut = side_rows(tie(out_grad, x_side))
    rank_row, count = mask_ranks(tie(masked_pos, x_side), masked_count, rows_dev, n)
    zero = jnp.zeros_like(feature_proj)
    dirs = tie(feature_proj, x_side)
    dirs = jnp.concatenate([jnp.concatenate([dirs, zero], 1), jnp.concatenate([zero, dirs], 1)], 0)
    near = near_rows(tokens, x_side)
    attn_own, fin, fo, dirs, dy_cut, rank_row, count, near = lax.optimization_barrier(
        (attn_own, fin, fo, dirs, dy_cut, rank_row, count, near)
    )

    attn_sib = swap(attn_own, heads=1)
    x_near = swap(near, heads=1)
    gains_near = swap(jnp.stack([gains, gains_side]), heads=1)
    x, a, norms = call(
        norm_kernel, "norm", [shape((n, D)), shape((n, D)), shape((4, D), f32)], [], 1,
        [me, tokens, x_side, x_near, gains, gains_side, gains_near], smem=(0,),
    )
    k, v, phi_k, kv_own, kv_sib, w_attn = call(
        keys_kernel, "keys",
        [shape((n, D)), shape((n, D)), shape((n, 4 * D)), shape((2, PACK, D)), shape((2, PACK, D)),
         shape((4, D, 4 * PAIR))],
        [pltpu.VMEM((4, PAIR, D), f32), pltpu.VMEM((4, 8, D), f32)],
        4, [a, attn_own, attn_sib, dirs],
    )
    fin_own = widen_bit(fin, "rows", 0, 1 + groups, (k,)).reshape(2, D, hidden)
    fo = widen_bit(fo, "rows", bits - 1, 1, (k,))
    dy_side = tie(swap(dy_cut, heads=2), k)
    kv_total = kv_own.astype(f32) + swap(kv_sib, heads=1).astype(f32)
    kv_total, fin_own, fo, dy_side = lax.optimization_barrier((kv_total, fin_own, fo, dy_side))

    (phi_q,) = call(
        queries_kernel, "queries", [shape((n, 4 * D))], [], 3, [tie(a, kv_total), w_attn, dirs],
    )
    fin_sib = swap(fin_own, heads=1)
    kv_own, kv_sib = spread_sum(kv_total, (phi_q,))
    high, low = call(
        attention_kernel, "attention", [shape((n, D)), shape((n, D))],
        [pltpu.VMEM((4, 256, D), b16), pltpu.VMEM((D, D), b16)],
        2, [x, phi_q, kv_own, kv_sib, w_attn],
    )
    for step in range(1, bits - 1):
        fo = widen_bit(fo, "rows", bits - 1 - step, 1 + step, (high,))
    fo_own = fo.reshape(2, D, hidden)
    fo_sib = swap(fo_own, heads=1)
    dy_near = swap(near_rows(out_grad, tie(dy_side, kv_own)), heads=1)
    ino_keep, ino_send, foq_keep, foq_send, dkv_own, dkv_sib, masked_grad, norm_grad = call(
        masked_kernel, "masked",
        [shape((2, D, hidden + PAIR))] * 4 + [
         shape((2, PACK, D)), shape((2, PACK, D)), shape((n, D)), shape((4, D), f32)],
        [pltpu.VMEM((n, D), b16), pltpu.VMEM((4, 256, D), b16), pltpu.VMEM((D, D), b16),
         pltpu.VMEM((4, D, hidden), b16), pltpu.VMEM((4, D, hidden), b16),
         pltpu.VMEM((4, 256, D), f32), pltpu.VMEM((MASK_TILE, D), f32), pltpu.VMEM((4, MASK_TILE, PAIR), f32)],
        18,
        [me, count, rank_row, high, low, x, out_grad, dy_side, dy_near, norms, fin_own, fin_sib, fo_own, fo_sib,
         w_attn, kv_own, kv_sib, dirs],
        smem=(0, 1), vmem=26,
    )

    dkv_total = dkv_own.astype(f32) + swap(dkv_sib, heads=1).astype(f32)
    blocks = (2,) * (1 + bits) + (narrow, hidden + PAIR)
    gino = add_low(ino_keep, swap(tie(ino_send, dkv_total), heads=1)).reshape(blocks)
    gfoq = add_low(foq_keep, swap(tie(foq_send, dkv_total), heads=1)).reshape(blocks)
    dkv_own, dkv_sib = spread_sum(dkv_total, (gino, gfoq))
    gino, ino_away = split_half(gino, "rows", 0, bits)
    gfoq, foq_away = split_half(gfoq, "heads", 1, 0)
    i_own, i_near, i_far, rows_grad, norm_sums = call(
        inputs_kernel, "inputs",
        [shape((n, PAIR)), shape((2, n, PAIR)), shape((n, PAIR)), shape((n, 2 * D)), shape((8, D // 2), f32)],
        [pltpu.VMEM((4, 256, D), b16), pltpu.VMEM((n, D), b16), pltpu.VMEM((16, D), f32)],
        6,
        [me, tie(x, gino, gfoq, ino_away, foq_away), k, v, phi_k, masked_grad, dkv_own, dkv_sib, norms, w_attn, dirs, norm_grad],
        smem=(0,),
    )
    keep, send = call(
        weights_kernel, "weights",
        [shape((2 * D, 2 * PAIR), f32), shape((2 * D + 16, 2 * PAIR))], [],
        1.3, [a, rows_grad, norm_sums],
    )
    i_near = swap(i_near, heads=1)
    m_own, m_near, m_far = call(
        forward_kernel, "forward", [shape((n, PAIR)), shape((2, n, PAIR)), shape((n, PAIR))],
        [pltpu.VMEM((n, D), b16), pltpu.VMEM((FORWARD_TILE, D), b16), pltpu.VMEM((FORWARD_TILE, D), f32)], 6,
        [me, tie(high, send), low, norms, fin_own, fin_sib, fo_own, fo_sib], smem=(0,),
    )
    total, norm_sums = add_sibling(keep, send, norm_sums, m_own)
    gino = add_low(gino, tie(swap(ino_away, rows=1), m_own))
    gfoq = add_low(gfoq, tie(swap(foq_away, heads=2), m_own))
    total, norm_sums, gino, gfoq, i_near, m_near = lax.optimization_barrier(
        (total, norm_sums, gino, gfoq, i_near, m_near)
    )
    i_side = swap(jnp.stack([i_far, i_near[1]]), heads=2)

    m_near = swap(m_near, heads=1)
    total, norm_sums = sum_stage(total, norm_sums, "heads", 1, 0)
    gino = halve(gino, "rows", 1, bits - 1)
    gfoq = halve(gfoq, "rows", 0, bits - 1)
    total, norm_sums, gino, gfoq, m_near = lax.optimization_barrier((total, norm_sums, gino, gfoq, m_near))
    m_side = swap(jnp.stack([m_far, m_near[1]]), heads=2)
    total, norm_sums = sum_stage(total, norm_sums, "rows", 0, bits - 1)
    for step in range(2, bits):
        gino = halve(gino, "rows", step, bits - step)
    gfoq = halve(gfoq, "rows", 1, bits - 2)
    total, norm_sums, gino, gfoq, i_side = lax.optimization_barrier((total, norm_sums, gino, gfoq, i_side))
    gino = halve(gino, "heads", 1, 0)
    for step in range(2, bits):
        gfoq = halve(gfoq, "rows", step, bits - 1 - step)
    for step in range(1, bits):
        total, norm_sums = sum_stage(total, norm_sums, "rows", step, bits - 1 - step)
        if step == bits - 2:
            m_own, i_own = tie(m_own, total), tie(i_own, total)
    gkv = total
    mixed_out = join_rows(m_own, m_near, m_side, b16)
    input_grad = join_rows(i_own, i_near, i_side, f32)
    head = lax.axis_index("heads")
    mine = lax.dynamic_slice(norm_sums, (4 * (head // 2), PAIR * (head % 2)), (4, PAIR))
    gqkv = jnp.stack([gfoq[:, hidden:].T.astype(f32), gkv[:, :PAIR].T, gkv[:, PAIR:].T])

    return (
        mixed_out,
        input_grad,
        gqkv,
        gino[:, hidden:].T.astype(f32),
        gino[:, :hidden].T.astype(f32),
        gfoq[:, :hidden].T.astype(f32),
        mine[0],
        mine[1],
        mine[2],
        mine[3],
    )


def solution(mesh):
    in_specs = (
        P("rows", "heads"),
        P("heads"),
        P("heads"),
        P(None, "heads", "rows"),
        P("heads", "rows"),
        P("heads"),
        P("heads"),
        P("heads", "rows"),
        P("heads", "rows"),
        P(),
        P(),
        P(),
        P("rows", "heads"),
    )
    out_specs = (
        P("rows", "heads"),
        P("rows", "heads"),
        P(None, "heads", "rows"),
        P("heads", "rows"),
        P("heads", "rows"),
        P("heads", "rows"),
        P("heads"),
        P("heads"),
        P("heads"),
        P("heads"),
    )
    return jax.shard_map(body, mesh=mesh, in_specs=in_specs, out_specs=out_specs, check_vma=False)
```
